256 devices in a mesh: guide: 64 (over z, x, y_hi), face: 4 (over y_lo, core).
Axes of the slice: x: 4, y: 4 (y_hi: 2, y_lo: 2; y = y_hi * 2 + y_lo), z: 8, core: 2. Of those that a mesh axis runs over, the one named last changes fastest.
Arguments:
- transfer: bfloat16 [64, 1024, 1024], P('guide'), may hold values from -0.2 to 1.2
- leaf_map: bfloat16 [64, 1024, 4096], P('guide'), may hold values from -0.09375 to 0.09375
- volume_source: bfloat16 [64, 1024, 4096], P('guide', 'face'), may hold values from -6 to 6
Outputs:
- traces: bfloat16 [64, 1024, 1024], P('guide', 'face')
The draws below stay inside these ranges and needn't reach their ends.
All inputs are finite; a program needn't handle non-finite values.
Results may differ from the reference program's by a relative error of at most 0.02.
Values may be sent and summed in bfloat16 or wider, within the bound.
No kernel may reach another device: no remote copies, remote signals or barrier semaphores. Data moves between devices by JAX's collectives and lax.ppermute only.
A program may use at most 128 MiB of HBM per device.

```python
import math
import jax
import jax.numpy as jnp

F = 1024
LEAF = 4096
SLABS = 64
GROUPS = 16
SOURCES = 1024


def draw_transfer(key, part):
    key = jax.random.fold_in(key, 7)
    rate_key, jitter_key, mix_key = jax.random.split(key, 3)
    rates = jnp.exp(jax.random.uniform(rate_key, (F,), jnp.float32, math.log(0.3), math.log(60.0)))
    jitter = jax.random.uniform(jitter_key, (SLABS, F), jnp.float32, 0.5, 1.5)
    diagonal = jnp.exp(-rates[None, :] * jitter / SLABS)
    mixing = jnp.clip(jax.random.normal(mix_key, (SLABS, F, F), jnp.float32), -6.0, 6.0)
    mixing = mixing * (0.2 / math.sqrt(F))
    identity = jnp.eye(F, dtype=jnp.float32)
    return (mixing + diagonal[:, :, None] * identity[None]).astype(jnp.bfloat16)


def levels(key, shape, cuts, least, top_value):
    loudness, own = 1.0, jax.random.fold_in(key, 6)
    for dim, parts in cuts:
        draws = jnp.exp(jax.random.uniform(jax.random.fold_in(own, dim), (parts,), jnp.float32, least / len(cuts), top_value / len(cuts)))
        loudness = loudness * jnp.repeat(draws, shape[dim] // parts).reshape([-1 if axis == dim else 1 for axis in range(len(shape))])
    return loudness


def bell_draw(stream_key, dims, scale, most, shards=(), kind=jnp.bfloat16):
    values = jax.random.normal(stream_key, dims, jnp.float32) * scale
    if len(shards) > 0:
        values = levels(stream_key, dims, shards, -0.22, 0.18) * values
    return jnp.clip(values, min=-most, max=most).astype(kind)


def setup_inputs(seed: int = 0) -> dict:
    arg_keys = jax.random.split(jax.random.key(seed), 4)
    return {
        "transfer": draw_transfer(jax.random.fold_in(arg_keys[3], 71), 0),
        "leaf_map": bell_draw(arg_keys[1], (SLABS, F, LEAF), LEAF ** -0.5, 0.09375, ((0, 64),)),
        "volume_source": bell_draw(arg_keys[2], (SLABS, SOURCES, LEAF), 1.0, 6.0, ((0, 64), (1, 4))),
    }


def apply_maps(maps, vectors):
    return jnp.einsum("srf,sgf->srg", vectors.astype(jnp.float32), maps.astype(jnp.float32))


def compose_maps(upper, lower):
    return jnp.einsum("sij,sjk->sik", upper.astype(jnp.float32), lower.astype(jnp.float32))


def reference(transfer, leaf_map, volume_source):
    source = jnp.einsum("srl,sfl->srf", volume_source.astype(jnp.float32), leaf_map.astype(jnp.float32)).astype(jnp.bfloat16)
    lower_maps, upper_maps = transfer[0::2], transfer[1::2]
    lower_src, upper_src = source[0::2], source[1::2]
    first_map = compose_maps(upper_maps, lower_maps).astype(jnp.bfloat16)
    first_trace = (apply_maps(upper_maps, lower_src) + upper_src.astype(jnp.float32)).astype(jnp.bfloat16)
    half_lower, half_upper = first_map[0::2], first_map[1::2]
    trace_lower, trace_upper = first_trace[0::2], first_trace[1::2]
    group_map = compose_maps(half_upper, half_lower).astype(jnp.bfloat16)
    group_trace = (apply_maps(half_upper, trace_lower) + trace_upper.astype(jnp.float32)).astype(jnp.bfloat16)
    moving = group_trace
    for turn_index in range(GROUPS - 1):
        moving = jnp.roll(moving, 1, axis=0)
        moving = (apply_maps(group_map, moving) + group_trace.astype(jnp.float32)).astype(jnp.bfloat16)
    entering = jnp.roll(moving, 1, axis=0)
    inner = (apply_maps(half_lower, entering) + trace_lower.astype(jnp.float32)).astype(jnp.bfloat16)
    lifted = (apply_maps(transfer[0::4], entering) + source[0::4].astype(jnp.float32)).astype(jnp.bfloat16)
    outer = (apply_maps(transfer[2::4], inner) + source[2::4].astype(jnp.float32)).astype(jnp.bfloat16)
    traces = jnp.stack([entering, lifted, inner, outer], axis=1)
    return traces.reshape(SLABS, SOURCES, F)
```

```python
import jax
import jax.numpy as jnp
from jax import lax
from jax.experimental import pallas as pl
from jax.experimental.pallas import tpu as pltpu
from jax.sharding import PartitionSpec as P

AXES = ("guide", "face")
BF16, F32 = jnp.bfloat16, jnp.float32


def coords(device):
    guide, face = divmod(device, 4)
    return guide // 2 % 4, guide % 2 * 2 + face // 2, guide // 8, face % 2


def device_at(x, y, z, core):
    x, y, z = x % 4, y % 4, z % 8
    return (z * 8 + x * 2 + y // 2) * 4 + y % 2 * 2 + core


def permute(block, target):
    route = [(i, device_at(*target(*coords(i)))) for i in range(256)]
    return lax.ppermute(block, AXES, route)


def to_core(x, y, z, c):
    return x, y, z, 1 - c


def to_y_mirror(x, y, z, c):
    return x, 3 - y, z, c


def to_y_pair(x, y, z, c):
    return x, y ^ 1, z, c


def to_y_next(x, y, z, c):
    return x, y + 1, z, c


def to_y_last(x, y, z, c):
    return x, y - 1, z, c


def to_y_far(x, y, z, c):
    return x, y + 2, z, c


def to_x_pair(x, y, z, c):
    return x ^ 1, y, z, c


def to_x_mirror(x, y, z, c):
    return 3 - x, y, z, c


def to_z_next(x, y, z, c):
    return x, y, z + 1, c


def rows_at(block, index, count):
    return lax.dynamic_slice_in_dim(block, index * count, count, 0)


def act(linear_map, vectors):
    return lax.dot_general(
        vectors, linear_map, (((1,), (1,)), ((), ())), preferred_element_type=F32
    )


def act_add(linear_map, vectors, added):
    return (act(linear_map, vectors) + added.astype(F32)).astype(BF16)


def merge_kernel(info, own, p0, p1, p2, p3, mine, theirs, product, other, trace):
    for slot, piece in enumerate((p0, p1, p2, p3)):
        start = pl.multiple_of(info[1 + slot] * 256, 256)
        other[pl.ds(start, 256), :] = piece[...]

    def merge(left, right, low, high):
        @pl.loop(0, 4)
        def _(tile):
            cols = pl.ds(pl.multiple_of(tile * 256, 256), 256)
            product[:, cols] = jnp.dot(
                left[...], right[:, cols], preferred_element_type=F32
            ).astype(BF16)

        trace[...] = act_add(left[...], low[...], high[...])

    @pl.when(info[0] == 1)
    def _():
        merge(own, other, theirs, mine)

    @pl.when(info[0] == 0)
    def _():
        merge(other, own, mine, theirs)


def merge(is_upper, order, own, pieces, mine, theirs):
    info = jnp.stack([is_upper] + order).astype(jnp.int32)
    full = pl.BlockSpec(memory_space=pltpu.VMEM)
    size = own.shape[0]
    return pl.pallas_call(
        merge_kernel,
        in_specs=[pl.BlockSpec(memory_space=pltpu.SMEM)] + [full] * 7,
        out_specs=[full] * 3,
        out_shape=[
            jax.ShapeDtypeStruct((size, size), BF16),
            jax.ShapeDtypeStruct((size, size), BF16),
            jax.ShapeDtypeStruct(mine.shape, BF16),
        ],
        compiler_params=pltpu.CompilerParams(vmem_limit_bytes=32 * 1024 * 1024),
        cost_estimate=pl.CostEstimate(
            flops=2 * size**3, bytes_accessed=8 * size**2, transcendentals=0
        ),
    )(info, own, *pieces, mine, theirs)


def local(transfer, leaf_map, volume_source):
    guide, face = lax.axis_index("guide"), lax.axis_index("face")
    x, y_hi, y_lo, core = guide // 2 % 4, guide % 2, face // 2, face % 2
    x_hi, x_lo = x // 2, x % 2
    strip = (x_lo + x_hi) % 2
    own_map = transfer[0]

    order = [face, face ^ 2, face ^ 1, face ^ 3]

    near = permute(rows_at(own_map, face ^ 2, 256), to_y_mirror)
    far = permute(near, to_y_pair)
    near_core, far_core = permute(near, to_core), permute(far, to_core)
    source = act(leaf_map[0], volume_source[0]).astype(BF16)
    theirs = permute(rows_at(source, 1 - y_hi, 128), to_y_far)
    source_rest = permute(rows_at(source, y_hi, 128), to_y_far)
    first_map, pair_map, first_trace = merge(
        y_hi, order, own_map, (near, far, near_core, far_core), rows_at(source, y_hi, 128), theirs
    )
    pair_trace = jnp.where(
        y_hi == 1,
        jnp.concatenate([source_rest, theirs], 0),
        jnp.concatenate([theirs, source_rest], 0),
    )

    def cross(block, partner):
        near = permute(rows_at(block, face, 256), partner)
        top = permute(near[:128], to_y_next)
        bottom = permute(near[128:], to_y_last)
        far = jnp.concatenate([top, bottom], 0)
        return near, far, permute(near, to_core), permute(far, to_core)

    pieces = cross(first_map, to_x_pair)
    theirs = permute(rows_at(first_trace, 1 - strip, 64), to_x_pair)
    rest = permute(rows_at(first_trace, strip, 64), to_x_pair)
    group_map, half_map, group_trace = merge(
        x_lo, order, first_map, pieces, rows_at(first_trace, strip, 64), theirs
    )
    half_trace = jnp.where(
        strip == 1, jnp.concatenate([rest, theirs], 0), jnp.concatenate([theirs, rest], 0)
    )
    half_trace_far = permute(half_trace, to_y_far)
    half_trace = jnp.where(
        y_hi == 1,
        jnp.concatenate([half_trace_far, half_trace], 0),
        jnp.concatenate([half_trace, half_trace_far], 0),
    )

    pieces = cross(group_map, to_x_mirror)
    theirs = permute(group_trace, to_x_mirror)
    plane_map, other_map, plane_trace = merge(
        x_hi, order, group_map, pieces, group_trace, theirs
    )

    moving = jnp.where(x_hi == 1, group_trace, plane_trace)
    for _ in range(7):
        moving = act_add(plane_map, permute(moving, to_z_next), plane_trace)
    arrived = permute(moving, to_z_next)
    entering = jnp.where(x_hi == 1, act_add(other_map, arrived, theirs), arrived)

    side = permute(entering, to_x_pair)
    half = jnp.where(
        strip == 1, jnp.concatenate([side, entering], 0), jnp.concatenate([entering, side], 0)
    )
    far = permute(half, to_y_far)
    entering = jnp.where(
        y_hi == 1, jnp.concatenate([far, half], 0), jnp.concatenate([half, far], 0)
    )
    lifted = jnp.where(x_lo == 1, act_add(half_map, entering, half_trace), entering)
    traces = jnp.where(y_hi == 1, act_add(pair_map, lifted, pair_trace), lifted)
    return traces[None]


def solution(mesh):
    in_specs = (P("guide", None, None), P("guide", None, None), P("guide", "face", None))
    out_specs = P("guide", "face", None)
    return jax.shard_map(local, mesh=mesh, in_specs=in_specs, out_specs=out_specs, check_vma=False)
```

```python
import jax
import jax.numpy as jnp
from jax import lax
from jax.experimental import pallas as pl
from jax.experimental.pallas import tpu as pltpu
from jax.sharding import PartitionSpec as P

AXES = ("guide", "face")
BF16, F32 = jnp.bfloat16, jnp.float32
SIDE = 256
ANY = pl.BlockSpec(memory_space=pl.ANY)
VMEM = pl.BlockSpec(memory_space=pltpu.VMEM)


def coords(device):
    guide, face = divmod(device, 4)
    return guide // 2 % 4, guide % 2 * 2 + face // 2, guide // 8, face % 2


def device_at(x, y, z, core):
    x, y, z = x % 4, y % 4, z % 8
    return (z * 8 + x * 2 + y // 2) * 4 + y % 2 * 2 + core


def permute(block, target, sends=lambda x, y: True):
    route = []
    for i in range(256):
        place = coords(i)
        if sends(place[0], place[1]):
            route.append((i, device_at(*target(*place))))
    return lax.ppermute(block, AXES, route)


def to_core(x, y, z, c):
    return x, y, z, 1 - c


def to_y_mirror(x, y, z, c):
    return x, 3 - y, z, c


def to_y_pair(x, y, z, c):
    return x, y ^ 1, z, c


def to_y_far(x, y, z, c):
    return x, y + 2, z, c


def to_x_pair(x, y, z, c):
    return x ^ 1, y, z, c


def to_x_mirror(x, y, z, c):
    return 3 - x, y, z, c


def to_x_far(x, y, z, c):
    return x + 2, y, z, c


def to_xy_far(x, y, z, c):
    return x ^ 1, y + 2, z, c


def to_z_next(x, y, z, c):
    return x, y, z + 1, c


def rows_at(block, index, count):
    return lax.dynamic_slice_in_dim(block, index * count, count, 0)


def act(linear_map, vectors):
    return lax.dot_general(
        vectors, linear_map, (((1,), (1,)), ((), ())), preferred_element_type=F32
    )


def act_add(linear_map, vectors, added):
    return (act(linear_map, vectors) + added.astype(F32)).astype(BF16)


class Place:
    def __init__(self):
        guide, self.face = lax.axis_index("guide"), lax.axis_index("face")
        self.x, self.y_hi, self.y_lo = guide // 2 % 4, guide % 2, self.face // 2
        self.core = self.face % 2
        self.x_hi, self.x_lo = self.x // 2, self.x % 2
        self.strip = (self.x_lo + self.x_hi) % 2


def span(index, size=SIDE):
    return pl.ds(pl.multiple_of(index * size, size), size)


def block_of(ref, row, col):
    return ref.at[span(row), span(col)]


def send_kernel(own, out, sems):
    place = Place()
    line = (place.face + 2) % 4
    copies = []
    for t in range(4):
        row = jnp.where(place.y_hi == 1, line, t)
        col = jnp.where(place.y_hi == 1, t, line)
        copies.append(pltpu.make_async_copy(block_of(own, row, col), out.at[t], sems.at[t]))
    for copy in copies:
        copy.start()
    for copy in copies:
        copy.wait()


def send_line(own):
    return pl.pallas_call(
        send_kernel,
        in_specs=[ANY],
        out_specs=ANY,
        out_shape=jax.ShapeDtypeStruct((4, SIDE, SIDE), BF16),
        scratch_shapes=[pltpu.SemaphoreType.DMA((4,))],
    )(own)


def line_kernel(own, got, out):
    place = Place()

    @pl.when(place.y_hi == 0)
    def _():
        row = jnp.concatenate([got[t] for t in range(4)], axis=1)
        for t in range(4):
            cols = slice(t * SIDE, (t + 1) * SIDE)
            out[t] = jnp.dot(row, own[:, cols], preferred_element_type=F32).astype(BF16)

    @pl.when(place.y_hi == 1)
    def _():
        col = jnp.concatenate([got[t] for t in range(4)], axis=0)
        for t in range(4):
            rows = slice(t * SIDE, (t + 1) * SIDE)
            out[t] = jnp.dot(own[rows, :], col, preferred_element_type=F32).astype(BF16)


def pair_line(own, got):
    return pl.pallas_call(
        line_kernel,
        in_specs=[VMEM] * 2,
        out_specs=VMEM,
        out_shape=jax.ShapeDtypeStruct((4, SIDE, SIDE), BF16),
        compiler_params=pltpu.CompilerParams(vmem_limit_bytes=16 * 1024 * 1024),
        cost_estimate=pl.CostEstimate(
            flops=2 * SIDE * 1024**2, bytes_accessed=3 * 1024**2, transcendentals=0
        ),
    )(own, got)


def gather_copies(place, target, line, line_core, sides, sides_core, sems):
    copies = []

    def add(source, across, index, along):
        row = jnp.where(across, along, index)
        col = jnp.where(across, index, along)
        copies.append(
            pltpu.make_async_copy(source, block_of(target, row, col), sems.at[len(copies)])
        )

    upper, lower = place.y_hi == 1, place.y_hi == 0
    for other, (lines, both) in enumerate(((line, sides), (line_core, sides_core))):
        core = (place.core + other) % 2
        mine, far = 2 * place.y_lo + core, 2 * (1 - place.y_lo) + core
        for t in range(4):
            add(lines[t], upper, mine, t)
        for t in range(2):
            add(both[t], upper, far, 2 * place.y_lo + t)
        for t in range(2):
            add(both[2 + t], lower, far, 2 * (1 - place.y_lo) + t)
    return copies


def blocks(ref, count=4):
    return [ref.at[t] for t in range(count)]


def start_all(copies):
    for copy in copies:
        copy.start()


def wait_all(copies):
    for copy in copies:
        copy.wait()


def multiply(left, right, store):
    @pl.loop(0, 4)
    def _(tile):
        cols = span(tile)
        store(cols, jnp.dot(left[...], right[:, cols], preferred_element_type=F32).astype(BF16))


def group_kernel(*refs):
    (line, sides, line_c, sides_c, p_line, p_sides, p_line_c, p_sides_c) = refs[:8]
    mine, theirs, group, pair, trace, maps, sems, out_sem = refs[8:]
    place = Place()
    own_slot, pair_slot = 1 - place.x_lo, place.x_lo
    copies = gather_copies(
        place, maps.at[own_slot], blocks(line), blocks(line_c), blocks(sides), blocks(sides_c),
        sems.at[0],
    ) + gather_copies(
        place, maps.at[pair_slot], blocks(p_line), blocks(p_line_c), blocks(p_sides),
        blocks(p_sides_c), sems.at[1],
    )
    start_all(copies)
    wait_all(copies)
    out = pltpu.make_async_copy(maps.at[pair_slot], pair, out_sem)
    out.start()

    def store(cols, value):
        group[:, cols] = value

    multiply(maps.at[0], maps.at[1], store)
    upper = place.x_lo == 1
    high = jnp.where(upper, mine[...], theirs[...])
    low = jnp.where(upper, theirs[...], mine[...])
    trace[...] = act_add(maps[0], low, high)
    out.wait()


def map_shape():
    return jax.ShapeDtypeStruct((1024, 1024), BF16)


def to_group(pieces, pair_pieces, mine, theirs):
    return pl.pallas_call(
        group_kernel,
        in_specs=[ANY] * 8 + [VMEM] * 2,
        out_specs=[VMEM, ANY, VMEM],
        out_shape=[map_shape(), map_shape(), jax.ShapeDtypeStruct(mine.shape, BF16)],
        scratch_shapes=[
            pltpu.VMEM((2, 1024, 1024), BF16),
            pltpu.SemaphoreType.DMA((2, 16)),
            pltpu.SemaphoreType.DMA,
        ],
        compiler_params=pltpu.CompilerParams(vmem_limit_bytes=24 * 1024 * 1024),
        cost_estimate=pl.CostEstimate(
            flops=2 * 1024**3, bytes_accessed=8 * 1024**2, transcendentals=0
        ),
    )(*pieces, *pair_pieces, mine, theirs)


def plane_kernel(*refs):
    (line, sides, line_c, sides_c, f_line, f_sides, f_line_c, f_sides_c) = refs[:8]
    group, mine, mirror, far, plane, other, other_trace, plane_trace, first = refs[8:17]
    maps, groups, sems, out_sem = refs[17:]
    place = Place()
    mirror_slot, far_slot = place.x_lo, 1 - place.x_lo
    own_slot, other_slot = 1 - place.x_hi, place.x_hi
    copies = gather_copies(
        place, maps.at[mirror_slot], blocks(line), blocks(line_c), blocks(sides),
        blocks(sides_c), sems.at[0],
    ) + gather_copies(
        place, maps.at[far_slot], blocks(f_line), blocks(f_line_c), blocks(f_sides),
        blocks(f_sides_c), sems.at[1],
    )
    load = pltpu.make_async_copy(group, groups.at[own_slot], out_sem)
    load.start()
    start_all(copies)
    wait_all(copies)
    load.wait()

    def store_other(cols, value):
        groups[other_slot, :, cols] = value

    multiply(maps.at[0], maps.at[1], store_other)
    out = pltpu.make_async_copy(groups.at[other_slot], other, out_sem)
    out.start()

    def store(cols, value):
        plane[:, cols] = value

    multiply(groups.at[0], groups.at[1], store)
    mirror_up = place.x_lo == 0
    high = jnp.where(mirror_up, mirror[...], far[...])
    low = jnp.where(mirror_up, far[...], mirror[...])
    side = act_add(maps[0], low, high)
    other_trace[...] = side
    upper = place.x_hi == 1
    high = jnp.where(upper, mine[...], side)
    low = jnp.where(upper, side, mine[...])
    total = act_add(groups[0], low, high)
    plane_trace[...] = total
    first[...] = jnp.where(upper, mine[...], total)
    out.wait()


def to_plane(pieces, far_pieces, group, mine, mirror, far):
    strip = jax.ShapeDtypeStruct(mine.shape, BF16)
    return pl.pallas_call(
        plane_kernel,
        in_specs=[ANY] * 9 + [VMEM] * 3,
        out_specs=[VMEM, ANY, VMEM, VMEM, VMEM],
        out_shape=[map_shape(), map_shape(), strip, strip, strip],
        scratch_shapes=[
            pltpu.VMEM((2, 1024, 1024), BF16),
            pltpu.VMEM((2, 1024, 1024), BF16),
            pltpu.SemaphoreType.DMA((2, 16)),
            pltpu.SemaphoreType.DMA,
        ],
        compiler_params=pltpu.CompilerParams(vmem_limit_bytes=32 * 1024 * 1024),
        cost_estimate=pl.CostEstimate(
            flops=4 * 1024**3, bytes_accessed=12 * 1024**2, transcendentals=0
        ),
    )(*pieces, *far_pieces, group, mine, mirror, far)


def last_kernel(e00, e01, e10, e11, half_map, half_trace, c0, c1, c2, c3, pair_trace, out, held):
    place = Place()
    for part, (flip_y, flip_x) in ((e00, (0, 0)), (e01, (0, 1)), (e10, (1, 0)), (e11, (1, 1))):
        index = 2 * ((place.y_hi + flip_y) % 2) + (place.strip + flip_x) % 2
        held[span(index, 64), :] = part[...]

    @pl.when(place.x_lo == 1)
    def _():
        held[...] = act_add(half_map[...], held[...], half_trace[...])

    @pl.when(place.y_hi == 0)
    def _():
        out[...] = held[...]

    @pl.when(place.y_hi == 1)
    def _():
        total = pair_trace[...].astype(F32)
        for column, strip in ((0, c0), (2, c1), (1, c2), (3, c3)):
            index = (place.face // 2 + column // 2) % 2 * 2 + (place.face + column) % 2
            for_strip = jnp.concatenate([strip[t] for t in range(4)], axis=0)
            total = total + act(for_strip, held[:, span(index)])
        out[...] = total.astype(BF16)


def last(entering, half_map, half_trace, columns, pair_trace):
    return pl.pallas_call(
        last_kernel,
        in_specs=[VMEM] * 11,
        out_specs=VMEM,
        out_shape=jax.ShapeDtypeStruct((256, 1024), BF16),
        scratch_shapes=[pltpu.VMEM((256, 1024), BF16)],
        compiler_params=pltpu.CompilerParams(vmem_limit_bytes=24 * 1024 * 1024),
        cost_estimate=pl.CostEstimate(
            flops=4 * 256 * 1024**2, bytes_accessed=6 * 1024**2, transcendentals=0
        ),
    )(*entering, half_map, half_trace, *columns, pair_trace)


def after(value, *others):
    return lax.optimization_barrier((value, *others))[0]


def local(transfer, leaf_map, volume_source):
    place = Place()
    y_hi, y_lo, strip = place.y_hi, place.y_lo, place.strip
    own_map = transfer[0]

    got = permute(send_line(own_map), to_y_mirror)
    source = act(leaf_map[0], volume_source[0]).astype(BF16)
    got, source = lax.optimization_barrier((got, source))
    line = pair_line(own_map, got)

    line_pair = permute(line, to_x_pair)
    line_mirror = permute(line, to_x_mirror)

    def halves(lines):
        return rows_at(lines, y_lo, 2), rows_at(lines, 1 - y_lo, 2)

    to_mirror, to_pair = halves(line)
    sides = jnp.concatenate([permute(to_pair, to_y_pair), permute(to_mirror, to_y_mirror)], 0)
    line_core = permute(line, to_core)
    sides_core = permute(sides, to_core)

    lower_source = permute(source, to_y_far, lambda x, y: y < 2)
    first = act_add(own_map, lower_source, source)
    first_far = permute(first, to_y_far, lambda x, y: y >= 2)
    first = jnp.where(y_hi == 1, first, first_far)
    mine = rows_at(first, 2 * y_hi + strip, 64)
    theirs = rows_at(first, 2 * y_hi + 1 - strip, 64)
    from_pair = permute(theirs, to_x_pair)
    from_mirror = permute(mine, to_x_mirror)
    from_far = permute(theirs, to_x_far)

    far_a = permute(line_pair[:2], to_x_mirror)
    far_b = permute(line_mirror[2:], to_x_pair)
    pair_to_mirror, pair_to_pair = halves(line_pair)
    mirror_to_mirror, mirror_to_pair = halves(line_mirror)
    by_pair = permute(jnp.concatenate([pair_to_pair, mirror_to_pair], 0), to_y_pair)
    by_mirror = permute(jnp.concatenate([pair_to_mirror, mirror_to_mirror], 0), to_y_mirror)
    line_pair_core = permute(line_pair, to_core)
    line_mirror_core = permute(line_mirror, to_core)
    sides_pair = jnp.concatenate([by_pair[:2], by_mirror[:2]], 0)
    sides_mirror = jnp.concatenate([by_pair[2:], by_mirror[2:]], 0)
    sides_pair_core = permute(sides_pair, to_core)
    sides_mirror_core = permute(sides_mirror, to_core)

    line_far = jnp.concatenate([far_a, far_b], 0)
    to_mirror, to_pair = halves(line_far)
    sides_far = jnp.concatenate([permute(to_pair, to_y_pair), permute(to_mirror, to_y_mirror)], 0)
    line_far_core = permute(line_far, to_core)
    sides_far_core = permute(sides_far, to_core)

    group_map, half_map, group_trace = to_group(
        (line, sides, line_core, sides_core),
        (line_pair, sides_pair, line_pair_core, sides_pair_core),
        mine, from_pair,
    )
    plane_map, other_map, other_trace, plane_trace, moving = to_plane(
        (line_mirror, sides_mirror, line_mirror_core, sides_mirror_core),
        (line_far, sides_far, line_far_core, sides_far_core),
        group_map, group_trace, from_mirror, from_far,
    )

    column, first_late = after(got, plane_trace), after(first, plane_trace)
    half_trace = permute(first_late, to_x_pair, lambda x, y: x % 2 == 0)
    column_pair = permute(column, to_y_pair, lambda x, y: y >= 2)
    column_core = permute(column, to_core, lambda x, y: y >= 2)
    column_both = permute(column_pair, to_core, lambda x, y: y >= 2)

    parts = [moving[:32], moving[32:]]
    added = [plane_trace[:32], plane_trace[32:]]
    for _ in range(7):
        parts = [
            act_add(plane_map, permute(part, to_z_next), extra)
            for part, extra in zip(parts, added)
        ]
    arrived = jnp.concatenate([permute(part, to_z_next) for part in parts], 0)
    entering = jnp.where(place.x_hi == 1, act_add(other_map, arrived, other_trace), arrived)

    pieces = (
        entering,
        permute(entering, to_x_pair),
        permute(entering, to_y_far),
        permute(entering, to_xy_far),
    )
    traces = last(
        pieces, half_map, half_trace, (column, column_pair, column_core, column_both), lower_source
    )
    return traces[None]


def solution(mesh):
    in_specs = (P("guide", None, None), P("guide", None, None), P("guide", "face", None))
    out_specs = P("guide", "face", None)
    return jax.shard_map(local, mesh=mesh, in_specs=in_specs, out_specs=out_specs, check_vma=False)
```

```python
import functools

import jax
import jax.numpy as jnp
from jax import lax
from jax.experimental import pallas as pl
from jax.experimental.pallas import tpu as pltpu
from jax.sharding import PartitionSpec as P

AXES = ("guide", "face")
BF16, F32 = jnp.bfloat16, jnp.float32
SIDE = 256
ANY = pl.BlockSpec(memory_space=pl.ANY)
VMEM = pl.BlockSpec(memory_space=pltpu.VMEM)


def coords(device):
    guide, face = divmod(device, 4)
    return guide // 2 % 4, guide % 2 * 2 + face // 2, guide // 8, face % 2


def device_at(x, y, z, core):
    x, y, z = x % 4, y % 4, z % 8
    return (z * 8 + x * 2 + y // 2) * 4 + y % 2 * 2 + core


def permute(block, target, sends=lambda x, y: True):
    route = []
    for i in range(256):
        place = coords(i)
        if sends(place[0], place[1]):
            route.append((i, device_at(*target(*place))))
    return lax.ppermute(block, AXES, route)


def to_core(x, y, z, c):
    return x, y, z, 1 - c


def to_y_mirror(x, y, z, c):
    return x, 3 - y, z, c


def to_y_pair(x, y, z, c):
    return x, y ^ 1, z, c


def to_y_far(x, y, z, c):
    return x, y + 2, z, c


def to_x_pair(x, y, z, c):
    return x ^ 1, y, z, c


def to_x_mirror(x, y, z, c):
    return 3 - x, y, z, c


def to_xy_far(x, y, z, c):
    return x ^ 1, y + 2, z, c


def to_z_next(x, y, z, c):
    return x, y, z + 1, c


def rows_at(block, index, count):
    return lax.dynamic_slice_in_dim(block, index * count, count, 0)


def act(linear_map, vectors):
    return lax.dot_general(
        vectors, linear_map, (((1,), (1,)), ((), ())), preferred_element_type=F32
    )


def act_add(linear_map, vectors, added):
    return (act(linear_map, vectors) + added.astype(F32)).astype(BF16)


class Place:
    def __init__(self):
        guide, self.face = lax.axis_index("guide"), lax.axis_index("face")
        self.x, self.y_hi, self.y_lo = guide // 2 % 4, guide % 2, self.face // 2
        self.core = self.face % 2
        self.x_hi, self.x_lo = self.x // 2, self.x % 2
        self.strip = (self.x_lo + self.x_hi) % 2


def span(index, size=SIDE):
    return pl.ds(pl.multiple_of(index * size, size), size)


def block_of(ref, row, col):
    return ref.at[span(row), span(col)]


def send_kernel(own, out):
    place = Place()
    line = span((place.face + 2) % 4)

    @pl.when(place.y_hi == 1)
    def _():
        for t in range(4):
            out[t] = own[line, t * SIDE : (t + 1) * SIDE]

    @pl.when(place.y_hi == 0)
    def _():
        for t in range(4):
            out[t] = own[t * SIDE : (t + 1) * SIDE, line]


def send_line(own):
    return pl.pallas_call(
        send_kernel,
        in_specs=[VMEM],
        out_specs=VMEM,
        out_shape=jax.ShapeDtypeStruct((4, SIDE, SIDE), BF16),
        compiler_params=pltpu.CompilerParams(vmem_limit_bytes=8 * 1024 * 1024),
    )(own)


def line_kernel(own, got, out):
    place = Place()

    @pl.when(place.y_hi == 0)
    def _():
        row = jnp.concatenate([got[t] for t in range(4)], axis=1)
        for t in range(4):
            cols = slice(t * SIDE, (t + 1) * SIDE)
            out[t] = jnp.dot(row, own[:, cols], preferred_element_type=F32).astype(BF16)

    @pl.when(place.y_hi == 1)
    def _():
        col = jnp.concatenate([got[t] for t in range(4)], axis=0)
        for t in range(4):
            rows = slice(t * SIDE, (t + 1) * SIDE)
            out[t] = jnp.dot(own[rows, :], col, preferred_element_type=F32).astype(BF16)


def pair_line(own, got):
    return pl.pallas_call(
        line_kernel,
        in_specs=[VMEM] * 2,
        out_specs=VMEM,
        out_shape=jax.ShapeDtypeStruct((4, SIDE, SIDE), BF16),
        compiler_params=pltpu.CompilerParams(vmem_limit_bytes=16 * 1024 * 1024),
        cost_estimate=pl.CostEstimate(
            flops=2 * SIDE * 1024**2, bytes_accessed=3 * 1024**2, transcendentals=0
        ),
    )(own, got)


def gather_copies(place, target, parts, sems):
    copies = []

    def add(source, across, index, along):
        row = jnp.where(across, along, index)
        col = jnp.where(across, index, along)
        copies.append(
            pltpu.make_async_copy(source, block_of(target, row, col), sems.at[len(copies)])
        )

    upper, lower = place.y_hi == 1, place.y_hi == 0
    for other, (line, pair, mirror) in enumerate(parts):
        core = (place.core + other) % 2
        mine, far = 2 * place.y_lo + core, 2 * (1 - place.y_lo) + core
        for t in range(4):
            add(line.at[t], upper, mine, t)
        for t in range(2):
            add(pair.at[t], upper, far, 2 * place.y_lo + t)
        for t in range(2):
            add(mirror.at[t], lower, far, 2 * (1 - place.y_lo) + t)
    return copies


def multiply(left, right, store):
    @pl.loop(0, 4)
    def _(tile):
        cols = span(tile)
        store(cols, jnp.dot(left[...], right[:, cols], preferred_element_type=F32).astype(BF16))


def merge_kernel(step, *refs):
    place = Place()
    first_parts = (refs[0:3], refs[3:6])
    second_parts = (refs[6:9], refs[9:12])
    refs = refs[12:]
    if step == 0:
        mine, theirs, group, lower_map, trace, maps, sems, out_sem = refs
        first_slot = 1 - place.x_lo
    else:
        own_map, mine, theirs, group, trace, moving, maps, sems, out_sem = refs
        first_slot = place.x_lo
    copies = gather_copies(place, maps.at[first_slot], first_parts, sems.at[0])
    copies += gather_copies(place, maps.at[1 - first_slot], second_parts, sems.at[1])
    for copy in copies:
        copy.start()
    for copy in copies:
        copy.wait()
    if step == 0:
        out = pltpu.make_async_copy(maps.at[1], lower_map, out_sem)
        out.start()

    def store(cols, value):
        group[:, cols] = value

    multiply(maps.at[0], maps.at[1], store)
    if step == 0:
        upper = place.x_lo == 1
        high = jnp.where(upper, mine[...], theirs[...])
        low = jnp.where(upper, theirs[...], mine[...])
        trace[...] = act_add(maps[0], low, high)
        out.wait()
    else:

        @pl.when(place.x_hi == 1)
        def _():
            trace[...] = act_add(own_map[...], theirs[...], mine[...])
            moving[...] = mine[...]

        @pl.when(place.x_hi == 0)
        def _():
            total = act_add(group[...], mine[...], theirs[...])
            trace[...] = total
            moving[...] = total


def map_shape():
    return jax.ShapeDtypeStruct((1024, 1024), BF16)


def merge(step, first, second, *rest):
    strip = jax.ShapeDtypeStruct(rest[-1].shape, BF16)
    if step == 0:
        out_specs, out_shape = [VMEM, ANY, VMEM], [map_shape(), map_shape(), strip]
    else:
        out_specs, out_shape = [VMEM] * 3, [map_shape(), strip, strip]
    return pl.pallas_call(
        functools.partial(merge_kernel, step),
        in_specs=[ANY] * 12 + [VMEM] * len(rest),
        out_specs=out_specs,
        out_shape=out_shape,
        scratch_shapes=[
            pltpu.VMEM((2, 1024, 1024), BF16),
            pltpu.SemaphoreType.DMA((2, 16)),
            pltpu.SemaphoreType.DMA,
        ],
        compiler_params=pltpu.CompilerParams(vmem_limit_bytes=16 * 1024 * 1024),
        cost_estimate=pl.CostEstimate(
            flops=2 * 1024**3, bytes_accessed=8 * 1024**2, transcendentals=0
        ),
    )(*first, *second, *rest)


def plane_kernel(own, other, plane):
    place = Place()

    def store(cols, value):
        plane[:, cols] = value

    @pl.when(place.x_hi == 1)
    def _():
        multiply(own, other, store)

    @pl.when(place.x_hi == 0)
    def _():
        multiply(other, own, store)


def to_plane(own, other):
    return pl.pallas_call(
        plane_kernel,
        in_specs=[VMEM] * 2,
        out_specs=VMEM,
        out_shape=map_shape(),
        compiler_params=pltpu.CompilerParams(vmem_limit_bytes=12 * 1024 * 1024),
        cost_estimate=pl.CostEstimate(
            flops=2 * 1024**3, bytes_accessed=6 * 1024**2, transcendentals=0
        ),
    )(own, other)


def lift_kernel(part_a, part_b, other_map, other_trace, lower_map, lower_trace, own, across):
    place = Place()
    own[0:32, :] = part_a[...]
    own[32:64, :] = part_b[...]

    @pl.when(place.x_hi == 1)
    def _():
        own[...] = act_add(other_map[...], own[...], other_trace[...])

    entering = own[...]
    inner = act_add(lower_map[...], entering, lower_trace[...])
    upper = place.x_lo == 1
    own[...] = jnp.where(upper, inner, entering)
    across[...] = jnp.where(upper, entering, inner)


def lift(*args):
    strip = jax.ShapeDtypeStruct((64, 1024), BF16)
    return pl.pallas_call(
        lift_kernel,
        in_specs=[VMEM] * 6,
        out_specs=[VMEM] * 2,
        out_shape=[strip, strip],
        compiler_params=pltpu.CompilerParams(vmem_limit_bytes=12 * 1024 * 1024),
        cost_estimate=pl.CostEstimate(
            flops=4 * 64 * 1024**2, bytes_accessed=5 * 1024**2, transcendentals=0
        ),
    )(*args)


def last_kernel(e00, e01, e10, e11, c0, c1, c2, c3, pair_trace, out, held):
    place = Place()
    for part, (flip_y, flip_x) in ((e00, (0, 0)), (e01, (0, 1)), (e10, (1, 0)), (e11, (1, 1))):
        index = 2 * ((place.y_hi + flip_y) % 2) + (place.strip + flip_x) % 2
        held[span(index, 64), :] = part[...]

    @pl.when(place.y_hi == 0)
    def _():
        out[...] = held[...]

    @pl.when(place.y_hi == 1)
    def _():
        total = pair_trace[...].astype(F32)
        for column, strip in ((0, c0), (2, c1), (1, c2), (3, c3)):
            index = (place.face // 2 + column // 2) % 2 * 2 + (place.face + column) % 2
            for_strip = jnp.concatenate([strip[t] for t in range(4)], axis=0)
            total = total + act(for_strip, held[:, span(index)])
        out[...] = total.astype(BF16)


def last(*args):
    return pl.pallas_call(
        last_kernel,
        in_specs=[VMEM] * 9,
        out_specs=VMEM,
        out_shape=jax.ShapeDtypeStruct((256, 1024), BF16),
        scratch_shapes=[pltpu.VMEM((256, 1024), BF16)],
        compiler_params=pltpu.CompilerParams(vmem_limit_bytes=12 * 1024 * 1024),
        cost_estimate=pl.CostEstimate(
            flops=2 * 256 * 1024**2, bytes_accessed=4 * 1024**2, transcendentals=0
        ),
    )(*args)


def after(value, *others):
    return lax.optimization_barrier((value, *others))[0]


def local(transfer, leaf_map, volume_source):
    place = Place()
    y_hi, y_lo, strip = place.y_hi, place.y_lo, place.strip
    own_map = transfer[0]

    got = permute(send_line(own_map), to_y_mirror)
    source = act(leaf_map[0], volume_source[0]).astype(BF16)
    got, source = lax.optimization_barrier((got, source))
    line = pair_line(own_map, got)

    line_pair = permute(line, to_x_pair)
    line_mirror = permute(line, to_x_mirror)

    def halves(*lines):
        stacked = lines[0] if len(lines) == 1 else jnp.stack(lines)
        axis = stacked.ndim - 3
        return [
            lax.dynamic_slice_in_dim(stacked, half * 2, 2, axis) for half in (y_lo, 1 - y_lo)
        ]

    def along_y(*lines):
        to_mirror, to_pair = halves(*lines)
        return permute(to_pair, to_y_pair), permute(to_mirror, to_y_mirror)

    own_sides = along_y(line)
    line_core = permute(line, to_core)
    lower_source = permute(after(source, line), to_y_far, lambda x, y: y < 2)

    far_a = permute(line_pair[:2], to_x_mirror)
    far_b = permute(line_mirror[2:], to_x_pair)
    both_sides = along_y(line_pair, line_mirror)
    own_sides_core = [permute(side, to_core) for side in own_sides]
    line_pair_core = permute(line_pair, to_core)
    line_mirror_core = permute(line_mirror, to_core)

    first = act_add(own_map, lower_source, source)
    first, _, _ = lax.optimization_barrier((first, far_a, far_b))
    first_far = permute(first[:128], to_y_far, lambda x, y: y >= 2)
    line_far = jnp.concatenate([far_a, far_b], 0)
    far_sides = along_y(line_far)
    line_far_core = permute(line_far, to_core)
    both_sides_core = [permute(side, to_core) for side in both_sides]

    half = jnp.where(y_hi == 1, first[128:], first_far)
    mine = rows_at(half, strip, 64)
    from_pair = permute(rows_at(half, 1 - strip, 64), to_x_pair)

    group_map, lower_map, group_trace = merge(
        0,
        (line, *own_sides, line_core, *own_sides_core),
        (
            line_pair, both_sides[0][0], both_sides[1][0],
            line_pair_core, both_sides_core[0][0], both_sides_core[1][0],
        ),
        mine, from_pair,
    )
    other_trace = permute(group_trace, to_x_mirror)
    far_sides = lax.optimization_barrier((*far_sides, group_map))[:2]
    far_sides_core = [permute(side, to_core) for side in far_sides]
    other_map, plane_trace, moving = merge(
        1,
        (
            line_mirror, both_sides[0][1], both_sides[1][1],
            line_mirror_core, both_sides_core[0][1], both_sides_core[1][1],
        ),
        (line_far, *far_sides, line_far_core, *far_sides_core),
        group_map, group_trace, other_trace,
    )

    parts = [moving[:32], moving[32:]]
    added = [plane_trace[:32], plane_trace[32:]]
    parts = [permute(part, to_z_next) for part in parts]
    plane_map = to_plane(group_map, after(other_map, moving))
    for turn in range(7):
        parts = [act_add(plane_map, part, extra) for part, extra in zip(parts, added)]
        if turn == 1:
            column = after(got, parts[1])
            column_pair = permute(column, to_y_pair, lambda x, y: y >= 2)
        if turn == 3:
            column_core = permute(after(got, parts[1]), to_core, lambda x, y: y >= 2)
        if turn == 4:
            column_both = permute(after(column_pair, parts[1]), to_core, lambda x, y: y >= 2)
        parts = [permute(part, to_z_next) for part in parts]

    lower_trace = jnp.where(place.x_lo == 1, from_pair, mine)
    own, across = lift(*parts, other_map, other_trace, lower_map, lower_trace)
    pieces = (
        own,
        permute(across, to_x_pair),
        permute(own, to_y_far),
        permute(across, to_xy_far),
    )
    traces = last(*pieces, got, column_pair, column_core, column_both, lower_source)
    return traces[None]


def solution(mesh):
    in_specs = (P("guide", None, None), P("guide", None, None), P("guide", "face", None))
    out_specs = P("guide", "face", None)
    return jax.shard_map(local, mesh=mesh, in_specs=in_specs, out_specs=out_specs, check_vma=False)
```

```python
import functools

import jax
import jax.numpy as jnp
from jax import lax
from jax.experimental import pallas as pl
from jax.experimental.pallas import tpu as pltpu
from jax.sharding import PartitionSpec as P

AXES = ("guide", "face")
BF16, F32 = jnp.bfloat16, jnp.float32
SIDE = 256
ANY = pl.BlockSpec(memory_space=pl.ANY)
VMEM = pl.BlockSpec(memory_space=pltpu.VMEM)


def coords(device):
    guide, face = divmod(device, 4)
    return guide // 2 % 4, guide % 2 * 2 + face // 2, guide // 8, face % 2


def device_at(x, y, z, core):
    x, y, z = x % 4, y % 4, z % 8
    return (z * 8 + x * 2 + y // 2) * 4 + y % 2 * 2 + core


def permute(block, target, sends=lambda x, y: True):
    route = []
    for i in range(256):
        place = coords(i)
        if sends(place[0], place[1]):
            route.append((i, device_at(*target(*place))))
    return lax.ppermute(block, AXES, route)


def to_core(x, y, z, c):
    return x, y, z, 1 - c


def to_y_mirror(x, y, z, c):
    return x, 3 - y, z, c


def to_y_pair(x, y, z, c):
    return x, y ^ 1, z, c


def to_y_far(x, y, z, c):
    return x, y + 2, z, c


def to_x_pair(x, y, z, c):
    return x ^ 1, y, z, c


def to_x_mirror(x, y, z, c):
    return 3 - x, y, z, c


def to_xy_far(x, y, z, c):
    return x ^ 1, y + 2, z, c


def to_z_next(x, y, z, c):
    return x, y, z + 1, c


def rows_at(block, index, count):
    return lax.dynamic_slice_in_dim(block, index * count, count, 0)


def act(linear_map, vectors):
    return lax.dot_general(
        vectors, linear_map, (((1,), (1,)), ((), ())), preferred_element_type=F32
    )


def act_add(linear_map, vectors, added):
    return (act(linear_map, vectors) + added.astype(F32)).astype(BF16)


class Place:
    def __init__(self):
        guide, self.face = lax.axis_index("guide"), lax.axis_index("face")
        self.x, self.y_hi, self.y_lo = guide // 2 % 4, guide % 2, self.face // 2
        self.core = self.face % 2
        self.x_hi, self.x_lo = self.x // 2, self.x % 2
        self.strip = (self.x_lo + self.x_hi) % 2


def span(index, size=SIDE):
    return pl.ds(pl.multiple_of(index * size, size), size)


def block_of(ref, row, col):
    return ref.at[span(row), span(col)]


def send_kernel(own, out):
    place = Place()
    line = span((place.face + 2) % 4)

    @pl.when(place.y_hi == 1)
    def _():
        for t in range(4):
            out[t] = own[line, t * SIDE : (t + 1) * SIDE]

    @pl.when(place.y_hi == 0)
    def _():
        for t in range(4):
            out[t] = own[t * SIDE : (t + 1) * SIDE, line]


def send_line(own):
    return pl.pallas_call(
        send_kernel,
        in_specs=[VMEM],
        out_specs=VMEM,
        out_shape=jax.ShapeDtypeStruct((4, SIDE, SIDE), BF16),
        compiler_params=pltpu.CompilerParams(vmem_limit_bytes=8 * 1024 * 1024),
    )(own)


def line_kernel(own, got, out):
    place = Place()

    @pl.when(place.y_hi == 0)
    def _():
        row = jnp.concatenate([got[t] for t in range(4)], axis=1)
        for t in range(4):
            cols = slice(t * SIDE, (t + 1) * SIDE)
            out[t] = jnp.dot(row, own[:, cols], preferred_element_type=F32).astype(BF16)

    @pl.when(place.y_hi == 1)
    def _():
        col = jnp.concatenate([got[t] for t in range(4)], axis=0)
        for t in range(4):
            rows = slice(t * SIDE, (t + 1) * SIDE)
            out[t] = jnp.dot(own[rows, :], col, preferred_element_type=F32).astype(BF16)


def pair_line(own, got):
    return pl.pallas_call(
        line_kernel,
        in_specs=[VMEM] * 2,
        out_specs=VMEM,
        out_shape=jax.ShapeDtypeStruct((4, SIDE, SIDE), BF16),
        compiler_params=pltpu.CompilerParams(vmem_limit_bytes=16 * 1024 * 1024),
        cost_estimate=pl.CostEstimate(
            flops=2 * SIDE * 1024**2, bytes_accessed=3 * 1024**2, transcendentals=0
        ),
    )(own, got)


def gather_copies(place, target, parts, sems):
    copies = []

    def add(source, across, index, along):
        row = jnp.where(across, along, index)
        col = jnp.where(across, index, along)
        copies.append(
            pltpu.make_async_copy(source, block_of(target, row, col), sems.at[len(copies)])
        )

    upper, lower = place.y_hi == 1, place.y_hi == 0
    for other, (line, pair, mirror) in enumerate(parts):
        core = (place.core + other) % 2
        mine, far = 2 * place.y_lo + core, 2 * (1 - place.y_lo) + core
        for t in range(4):
            add(line.at[t], upper, mine, t)
        for t in range(2):
            add(pair.at[t], upper, far, 2 * place.y_lo + t)
        for t in range(2):
            add(mirror.at[t], lower, far, 2 * (1 - place.y_lo) + t)
    return copies


def multiply(left, right, store):
    @pl.loop(0, 4)
    def _(tile):
        cols = span(tile)
        store(cols, jnp.dot(left[...], right[:, cols], preferred_element_type=F32).astype(BF16))


def join_kernel(step, *refs):
    place = Place()
    if step == 0:
        line, own_p, own_m, core_a, pair, both_p, both_m, core_b = refs[:8]
        mine, theirs, maps, trace, sems = refs[8:]
        first_slot = 1 - place.x_lo
        first_parts = ((line, own_p, own_m), (core_a, core_a.at[4:6], core_a.at[6:8]))
        second_parts = (
            (pair, both_p.at[0:2], both_m.at[0:2]),
            (core_b.at[0:4], core_b.at[8:10], core_b.at[12:14]),
        )
    else:
        mirror, both_p, both_m, core_b, far, far_p, far_m, core_c = refs[:8]
        own_map, mine, theirs, maps, trace, moving, sems = refs[8:]
        first_slot = place.x_lo
        first_parts = (
            (mirror, both_p.at[2:4], both_m.at[2:4]),
            (core_b.at[4:8], core_b.at[10:12], core_b.at[14:16]),
        )
        second_parts = ((far, far_p, far_m), (core_c, core_c.at[4:6], core_c.at[6:8]))
    copies = gather_copies(place, maps.at[first_slot], first_parts, sems.at[0])
    copies += gather_copies(place, maps.at[1 - first_slot], second_parts, sems.at[1])
    for copy in copies:
        copy.start()
    for copy in copies:
        copy.wait()
    if step == 0:
        upper = place.x_lo == 1
        high = jnp.where(upper, mine[...], theirs[...])
        low = jnp.where(upper, theirs[...], mine[...])
        trace[...] = act_add(maps[0], low, high)
    else:

        @pl.when(place.x_hi == 1)
        def _():
            trace[...] = act_add(own_map[...], theirs[...], mine[...])
            moving[...] = mine[...]

        @pl.when(place.x_hi == 0)
        def _():
            lifted = act(maps[1], mine[...]).astype(BF16)
            total = act_add(maps[0], lifted, theirs[...])
            trace[...] = total
            moving[...] = total


def map_shape(*lead):
    return jax.ShapeDtypeStruct((*lead, 1024, 1024), BF16)


def join(step, pieces, *rest):
    strip = jax.ShapeDtypeStruct(rest[-1].shape, BF16)
    out_shape = [map_shape(2)] + [strip] * (1 + step)
    return pl.pallas_call(
        functools.partial(join_kernel, step),
        in_specs=[ANY] * 8 + [VMEM] * len(rest),
        out_specs=[VMEM] * len(out_shape),
        out_shape=out_shape,
        scratch_shapes=[pltpu.SemaphoreType.DMA((2, 16))],
        compiler_params=pltpu.CompilerParams(vmem_limit_bytes=12 * 1024 * 1024),
        cost_estimate=pl.CostEstimate(
            flops=2 * 64 * 1024**2, bytes_accessed=8 * 1024**2, transcendentals=0
        ),
    )(*pieces, *rest)


def group_kernel(maps, group):
    def store(cols, value):
        group[:, cols] = value

    multiply(maps.at[0], maps.at[1], store)


def to_group(maps):
    return pl.pallas_call(
        group_kernel,
        in_specs=[VMEM],
        out_specs=VMEM,
        out_shape=map_shape(),
        compiler_params=pltpu.CompilerParams(vmem_limit_bytes=12 * 1024 * 1024),
        cost_estimate=pl.CostEstimate(
            flops=2 * 1024**3, bytes_accessed=6 * 1024**2, transcendentals=0
        ),
    )(maps)


def plane_kernel(own, maps, other, plane):
    place = Place()

    def store_other(cols, value):
        other[:, cols] = value

    def store(cols, value):
        plane[:, cols] = value

    multiply(maps.at[0], maps.at[1], store_other)

    @pl.when(place.x_hi == 1)
    def _():
        multiply(own, other, store)

    @pl.when(place.x_hi == 0)
    def _():
        multiply(other, own, store)


def to_plane(own, maps):
    return pl.pallas_call(
        plane_kernel,
        in_specs=[VMEM] * 2,
        out_specs=[VMEM] * 2,
        out_shape=[map_shape()] * 2,
        compiler_params=pltpu.CompilerParams(vmem_limit_bytes=16 * 1024 * 1024),
        cost_estimate=pl.CostEstimate(
            flops=4 * 1024**3, bytes_accessed=10 * 1024**2, transcendentals=0
        ),
    )(own, maps)


def lift_kernel(part_a, part_b, other_map, other_trace, maps, lower_trace, own, across):
    place = Place()
    own[0:32, :] = part_a[...]
    own[32:64, :] = part_b[...]

    @pl.when(place.x_hi == 1)
    def _():
        own[...] = act_add(other_map[...], own[...], other_trace[...])

    entering = own[...]
    inner = act_add(maps[1], entering, lower_trace[...])
    upper = place.x_lo == 1
    own[...] = jnp.where(upper, inner, entering)
    across[...] = jnp.where(upper, entering, inner)


def lift(*args):
    strip = jax.ShapeDtypeStruct((64, 1024), BF16)
    return pl.pallas_call(
        lift_kernel,
        in_specs=[VMEM] * 6,
        out_specs=[VMEM] * 2,
        out_shape=[strip, strip],
        compiler_params=pltpu.CompilerParams(vmem_limit_bytes=12 * 1024 * 1024),
        cost_estimate=pl.CostEstimate(
            flops=4 * 64 * 1024**2, bytes_accessed=5 * 1024**2, transcendentals=0
        ),
    )(*args)


def last_kernel(e00, e01, e10, e11, c0, c1, c2, c3, pair_trace, out, held):
    place = Place()
    for part, (flip_y, flip_x) in ((e00, (0, 0)), (e01, (0, 1)), (e10, (1, 0)), (e11, (1, 1))):
        index = 2 * ((place.y_hi + flip_y) % 2) + (place.strip + flip_x) % 2
        held[span(index, 64), :] = part[...]

    @pl.when(place.y_hi == 0)
    def _():
        out[...] = held[...]

    @pl.when(place.y_hi == 1)
    def _():
        total = pair_trace[...].astype(F32)
        for column, strip in ((0, c0), (2, c1), (1, c2), (3, c3)):
            index = (place.face // 2 + column // 2) % 2 * 2 + (place.face + column) % 2
            for_strip = jnp.concatenate([strip[t] for t in range(4)], axis=0)
            total = total + act(for_strip, held[:, span(index)])
        out[...] = total.astype(BF16)


def last(*args):
    return pl.pallas_call(
        last_kernel,
        in_specs=[VMEM] * 9,
        out_specs=VMEM,
        out_shape=jax.ShapeDtypeStruct((256, 1024), BF16),
        scratch_shapes=[pltpu.VMEM((256, 1024), BF16)],
        compiler_params=pltpu.CompilerParams(vmem_limit_bytes=12 * 1024 * 1024),
        cost_estimate=pl.CostEstimate(
            flops=2 * 256 * 1024**2, bytes_accessed=4 * 1024**2, transcendentals=0
        ),
    )(*args)


def together(*values):
    return lax.optimization_barrier(values)


def local(transfer, leaf_map, volume_source):
    place = Place()
    y_hi, y_lo, strip = place.y_hi, place.y_lo, place.strip
    own_map = transfer[0]

    got = permute(send_line(own_map), to_y_mirror)
    source = act(leaf_map[0], volume_source[0]).astype(BF16)
    got, source = together(got, source)
    line = pair_line(own_map, got)

    def along_y(*lines):
        to_mirror, to_pair = [
            jnp.concatenate([rows_at(one, half, 2) for one in lines], 0)
            for half in (y_lo, 1 - y_lo)
        ]
        return permute(to_pair, to_y_pair), permute(to_mirror, to_y_mirror)

    def across_core(*arrays):
        return permute(jnp.concatenate(arrays, 0), to_core)

    source = together(source, line)[0]
    pair = permute(line, to_x_pair)
    mirror = permute(line, to_x_mirror)
    own_p, own_m = along_y(line)
    lower_source = permute(source, to_y_far, lambda x, y: y < 2)
    pair, mirror, own_p, own_m, lower_source = together(
        pair, mirror, own_p, own_m, lower_source
    )

    far_a = permute(pair[:2], to_x_mirror)
    far_b = permute(mirror[2:], to_x_pair)
    both_p, both_m = along_y(pair, mirror)
    first = act_add(own_map, lower_source, source)
    first, far_a, far_b = together(first, far_a, far_b)
    from_upper = permute(rows_at(first, strip, 64), to_y_far)
    from_across = permute(rows_at(first, 1 - strip, 64), to_xy_far)
    from_beside = permute(rows_at(first, 3 - strip, 64), to_x_pair)
    mine = jnp.where(y_hi == 1, rows_at(first, 2 + strip, 64), from_upper)
    beside = jnp.where(y_hi == 1, from_beside, from_across)
    far_a, far_b, both_p, both_m, mine, beside = together(
        far_a, far_b, both_p, both_m, mine, beside
    )

    far = jnp.concatenate([far_a, far_b], 0)
    far_p, far_m = along_y(far)
    core_a = across_core(line, own_p, own_m, got)
    core_b = across_core(pair, mirror, both_p, both_m)
    maps, group_trace = join(
        0, (line, own_p, own_m, core_a, pair, both_p, both_m, core_b), mine, beside
    )
    far_p, far_m, group_trace = together(far_p, far_m, group_trace)

    core_c = across_core(far, far_p, far_m)
    other_trace = permute(group_trace, to_x_mirror)
    group_map = to_group(maps)
    other_maps, plane_trace, moving = join(
        1,
        (mirror, both_p, both_m, core_b, far, far_p, far_m, core_c),
        group_map, group_trace, other_trace,
    )

    added = [plane_trace[:32], plane_trace[32:]]
    parts = [permute(part, to_z_next) for part in (moving[:32], moving[32:])]
    other_map, plane_map = to_plane(group_map, other_maps)
    for turn in range(7):
        parts = [act_add(plane_map, part, extra) for part, extra in zip(parts, added)]
        if turn == 0:
            got_late, got_core, *parts = together(got, core_a[8:], *parts)
            got_pair = permute(got_late, to_y_pair)
            got_both = permute(got_core, to_y_pair)
        parts = [permute(part, to_z_next) for part in parts]

    lower_trace = jnp.where(place.x_lo == 1, beside, mine)
    own, across = lift(*parts, other_map, other_trace, maps, lower_trace)
    pieces = (
        own,
        permute(across, to_x_pair),
        permute(own, to_y_far),
        permute(across, to_xy_far),
    )
    traces = last(*pieces, got, got_pair, got_core, got_both, lower_source)
    return traces[None]


def solution(mesh):
    in_specs = (P("guide", None, None), P("guide", None, None), P("guide", "face", None))
    out_specs = P("guide", "face", None)
    return jax.shard_map(local, mesh=mesh, in_specs=in_specs, out_specs=out_specs, check_vma=False)
```

```python
import functools

import jax
import jax.numpy as jnp
from jax import lax
from jax.experimental import pallas as pl
from jax.experimental.pallas import tpu as pltpu
from jax.sharding import PartitionSpec as P

AXES = ("guide", "face")
BF16, F32 = jnp.bfloat16, jnp.float32
SIDE = 256
ANY = pl.BlockSpec(memory_space=pl.ANY)
VMEM = pl.BlockSpec(memory_space=pltpu.VMEM)


def coords(device):
    guide, face = divmod(device, 4)
    return guide // 2 % 4, guide % 2 * 2 + face // 2, guide // 8, face % 2


def device_at(x, y, z, core):
    x, y, z = x % 4, y % 4, z % 8
    return (z * 8 + x * 2 + y // 2) * 4 + y % 2 * 2 + core


def permute(block, target):
    route = [(i, device_at(*target(*coords(i)))) for i in range(256)]
    return lax.ppermute(block, AXES, route)


def to_core(x, y, z, c):
    return x, y, z, 1 - c


def to_y_mirror(x, y, z, c):
    return x, 3 - y, z, c


def to_y_pair(x, y, z, c):
    return x, y ^ 1, z, c


def to_y_far(x, y, z, c):
    return x, y + 2, z, c


def to_x_pair(x, y, z, c):
    return x ^ 1, y, z, c


def to_x_mirror(x, y, z, c):
    return 3 - x, y, z, c


def to_x_far(x, y, z, c):
    return x + 2, y, z, c


def to_xy_far(x, y, z, c):
    return x ^ 1, y + 2, z, c


def to_z_next(x, y, z, c):
    return x, y, z + 1, c


def act(linear_map, vectors):
    return lax.dot_general(
        vectors, linear_map, (((1,), (1,)), ((), ())), preferred_element_type=F32
    )


def act_add(linear_map, vectors, added):
    return (act(linear_map, vectors) + added.astype(F32)).astype(BF16)


class Place:
    def __init__(self):
        guide, self.face = lax.axis_index("guide"), lax.axis_index("face")
        self.x, self.y_hi, self.y_lo = guide // 2 % 4, guide % 2, self.face // 2
        self.core = self.face % 2
        self.x_hi, self.x_lo = self.x // 2, self.x % 2
        self.strip = (self.x_lo + self.x_hi) % 2


def span(index, size=SIDE):
    return pl.ds(pl.multiple_of(index * size, size), size)


def block_of(ref, row, col):
    return ref.at[span(row), span(col)]


def send_kernel(own, out):
    place = Place()
    line = span((place.face + 2) % 4)

    @pl.when(place.y_hi == 1)
    def _():
        for t in range(4):
            out[t] = own[line, t * SIDE : (t + 1) * SIDE]

    @pl.when(place.y_hi == 0)
    def _():
        for t in range(4):
            out[t] = own[t * SIDE : (t + 1) * SIDE, line]


def send_line(own):
    return pl.pallas_call(
        send_kernel,
        in_specs=[VMEM],
        out_specs=VMEM,
        out_shape=jax.ShapeDtypeStruct((4, SIDE, SIDE), BF16),
        compiler_params=pltpu.CompilerParams(vmem_limit_bytes=8 * 1024 * 1024),
    )(own)


def small(**sizes):
    return dict(
        compiler_params=pltpu.CompilerParams(vmem_limit_bytes=12 * 1024 * 1024),
        cost_estimate=pl.CostEstimate(
            flops=sizes.get("flops", 0), bytes_accessed=1024**2, transcendentals=0
        ),
    )


def blocks(count):
    return jax.ShapeDtypeStruct((count, SIDE, SIDE), BF16)


def line_kernel(own, got, source, line, to_pair, to_mirror, rest):
    place = Place()

    @pl.when(place.y_hi == 0)
    def _():
        row = jnp.concatenate([got[t] for t in range(4)], axis=1)
        for t in range(4):
            cols = slice(t * SIDE, (t + 1) * SIDE)
            line[t] = jnp.dot(row, own[:, cols], preferred_element_type=F32).astype(BF16)

    @pl.when(place.y_hi == 1)
    def _():
        col = jnp.concatenate([got[t] for t in range(4)], axis=0)
        for t in range(4):
            rows = slice(t * SIDE, (t + 1) * SIDE)
            line[t] = jnp.dot(own[rows, :], col, preferred_element_type=F32).astype(BF16)

    for out, half in ((to_pair, 1 - place.y_lo), (to_mirror, place.y_lo)):
        out[0:2] = line[pl.ds(2 * half, 2)]
        for t in range(2):
            out[2 + t] = source[:, t * SIDE : (t + 1) * SIDE]
    for t in range(2):
        rest[t] = source[:, (2 + t) * SIDE : (3 + t) * SIDE]


def pair_line(own, got, source):
    return pl.pallas_call(
        line_kernel,
        in_specs=[VMEM] * 3,
        out_specs=[VMEM] * 4,
        out_shape=[blocks(4), blocks(4), blocks(4), blocks(2)],
        **small(flops=2 * SIDE * 1024**2),
    )(own, got, source)


def first_kernel(own, by_pair, by_mirror, rest_pair, rest_mirror, low_rows, high_rows):
    place = Place()

    @pl.when(place.y_hi == 1)
    def _():
        low, high = [
            jnp.concatenate([ref[2], ref[3], rest[0], rest[1]], axis=1)
            for ref, rest in ((by_mirror, rest_mirror), (by_pair, rest_pair))
        ]
        total = act_add(own[...], low, high)
        for half, out in enumerate((low_rows, high_rows)):
            for index in range(2):
                rows = slice(128 * half + 64 * index, 128 * half + 64 * index + 64)
                out[span((place.strip + index) % 2, 64), :] = total[rows]

    @pl.when(place.y_hi == 0)
    def _():
        low_rows[...] = jnp.zeros_like(low_rows)
        high_rows[...] = jnp.zeros_like(high_rows)


def first_strips(*args):
    return pl.pallas_call(
        first_kernel,
        in_specs=[VMEM] * 5,
        out_specs=[VMEM] * 2,
        out_shape=[jax.ShapeDtypeStruct((128, 1024), BF16)] * 2,
        **small(flops=2 * 256 * 1024**2),
    )(*args)


def pack_kernel(plans, count, *refs):
    place = Place()
    for plan, out in zip(plans, refs[count:]):
        if plan in ("pair", "mirror"):
            for half in range(2):

                @pl.when((place.y_lo == half) == (plan == "mirror"))
                def _():
                    out[...] = refs[half][...]

            continue
        filled = 0
        for index, start, size in plan:
            out[filled : filled + size] = refs[index][start : start + size]
            filled += size


def pack(arrays, *plans):
    return pl.pallas_call(
        functools.partial(pack_kernel, plans, len(arrays)),
        in_specs=[VMEM] * len(arrays),
        out_specs=[VMEM] * len(plans),
        out_shape=[
            blocks(2 if isinstance(plan, str) else sum(entry[2] for entry in plan))
            for plan in plans
        ],
        **small(),
    )(*arrays)


def gather_copies(place, target, parts, sems):
    copies = []

    def add(source, across, index, along):
        row = jnp.where(across, along, index)
        col = jnp.where(across, index, along)
        copies.append(
            pltpu.make_async_copy(source, block_of(target, row, col), sems.at[len(copies)])
        )

    upper, lower = place.y_hi == 1, place.y_hi == 0
    for other, (line, pair, mirror) in enumerate(parts):
        core = (place.core + other) % 2
        mine, far = 2 * place.y_lo + core, 2 * (1 - place.y_lo) + core
        for t in range(4):
            add(line.at[t], upper, mine, t)
        for t in range(2):
            add(pair.at[t], upper, far, 2 * place.y_lo + t)
        for t in range(2):
            add(mirror.at[t], lower, far, 2 * (1 - place.y_lo) + t)
    return copies


def multiply(left, right, store):
    @pl.loop(0, 4)
    def _(tile):
        cols = span(tile)
        store(cols, jnp.dot(left[...], right[:, cols], preferred_element_type=F32).astype(BF16))


def join_kernel(step, *refs):
    place = Place()
    if step == 0:
        line, by_pair, by_mirror, x_line, x_sides, c_line, c_x, c_sides = refs[:8]
        mine, theirs, maps, trace, sems = refs[8:]
        own_parts = ((line, by_pair, by_mirror), (c_line, c_sides, c_sides.at[2:4]))
        x_core = (c_x, c_sides.at[4:6], c_sides.at[6:8])
    else:
        line, by_pair, by_mirror, x_line, x_sides, c_far, c_x, c_sides = refs[:8]
        mine, theirs, own_maps, own_trace, maps, trace, total, moving, sems = refs[8:]
        own_parts = ((line, by_pair, by_mirror), (c_far, c_far.at[4:6], c_far.at[6:8]))
        x_core = (c_x.at[4:8], c_sides.at[8:10], c_sides.at[10:12])
    x_parts = ((x_line, x_sides, x_sides.at[2:4]), x_core)
    own_slot = 1 - place.x_lo
    copies = gather_copies(place, maps.at[own_slot], own_parts, sems.at[0])
    copies += gather_copies(place, maps.at[1 - own_slot], x_parts, sems.at[1])
    for copy in copies:
        copy.start()
    for copy in copies:
        copy.wait()
    upper = place.x_lo == 1
    high = jnp.where(upper, mine[...], theirs[...])
    low = jnp.where(upper, theirs[...], mine[...])
    trace[...] = act_add(maps[0], low, high)
    if step == 1:

        def through(both, low, high):
            inner = act(both[1], low).astype(BF16)
            total[...] = act_add(both[0], inner, high)

        @pl.when(place.x_hi == 1)
        def _():
            through(own_maps, trace[...], own_trace[...])
            moving[...] = own_trace[...]

        @pl.when(place.x_hi == 0)
        def _():
            through(maps, own_trace[...], trace[...])
            moving[...] = total[...]


def map_shape(*lead):
    return jax.ShapeDtypeStruct((*lead, 1024, 1024), BF16)


def join(step, pieces, *rest):
    strip = jax.ShapeDtypeStruct(rest[-1].shape, BF16)
    out_shape = [map_shape(2)] + [strip] * (1 + 2 * step)
    return pl.pallas_call(
        functools.partial(join_kernel, step),
        in_specs=[ANY] * 8 + [VMEM] * len(rest),
        out_specs=[VMEM] * len(out_shape),
        out_shape=out_shape,
        scratch_shapes=[pltpu.SemaphoreType.DMA((2, 16))],
        compiler_params=pltpu.CompilerParams(vmem_limit_bytes=16 * 1024 * 1024),
        cost_estimate=pl.CostEstimate(
            flops=2 * 64 * 1024**2, bytes_accessed=8 * 1024**2, transcendentals=0
        ),
    )(*pieces, *rest)


def plane_kernel(own_maps, other_maps, other, plane, own):
    place = Place()

    def store_in(ref):
        def store(cols, value):
            ref[:, cols] = value

        return store

    multiply(own_maps.at[0], own_maps.at[1], store_in(own))
    multiply(other_maps.at[0], other_maps.at[1], store_in(other))

    @pl.when(place.x_hi == 1)
    def _():
        multiply(own, other, store_in(plane))

    @pl.when(place.x_hi == 0)
    def _():
        multiply(other, own, store_in(plane))


def to_plane(own_maps, other_maps):
    return pl.pallas_call(
        plane_kernel,
        in_specs=[VMEM] * 2,
        out_specs=[VMEM] * 2,
        out_shape=[map_shape()] * 2,
        scratch_shapes=[pltpu.VMEM((1024, 1024), BF16)],
        compiler_params=pltpu.CompilerParams(vmem_limit_bytes=20 * 1024 * 1024),
        cost_estimate=pl.CostEstimate(
            flops=6 * 1024**3, bytes_accessed=12 * 1024**2, transcendentals=0
        ),
    )(own_maps, other_maps)


def lift_kernel(part_a, part_b, other_map, other_trace, maps, lower_trace, own, across):
    place = Place()
    own[0:32, :] = part_a[...]
    own[32:64, :] = part_b[...]

    @pl.when(place.x_hi == 1)
    def _():
        own[...] = act_add(other_map[...], own[...], other_trace[...])

    entering = own[...]
    inner = act_add(maps[1], entering, lower_trace[...])
    upper = place.x_lo == 1
    own[...] = jnp.where(upper, inner, entering)
    across[...] = jnp.where(upper, entering, inner)


def lift(*args):
    strip = jax.ShapeDtypeStruct((64, 1024), BF16)
    return pl.pallas_call(
        lift_kernel,
        in_specs=[VMEM] * 6,
        out_specs=[VMEM] * 2,
        out_shape=[strip, strip],
        compiler_params=pltpu.CompilerParams(vmem_limit_bytes=12 * 1024 * 1024),
        cost_estimate=pl.CostEstimate(
            flops=4 * 64 * 1024**2, bytes_accessed=5 * 1024**2, transcendentals=0
        ),
    )(*args)


def last_kernel(e00, e01, e10, e11, got, core_line, late, out, held):
    place = Place()
    for part, (flip_y, flip_x) in ((e00, (0, 0)), (e01, (0, 1)), (e10, (1, 0)), (e11, (1, 1))):
        index = 2 * ((place.y_hi + flip_y) % 2) + (place.strip + flip_x) % 2
        held[span(index, 64), :] = part[...]

    @pl.when(place.y_hi == 0)
    def _():
        out[...] = held[...]

    @pl.when(place.y_hi == 1)
    def _():
        total = jnp.concatenate([late[8 + t] for t in range(4)], axis=1).astype(F32)
        for flip, ref, start in ((0, got, 0), (1, core_line, 4), (2, late, 0), (3, late, 4)):
            index = (place.y_lo + flip // 2) % 2 * 2 + (place.core + flip) % 2
            column = jnp.concatenate([ref[start + t] for t in range(4)], axis=0)
            total = total + act(column, held[:, span(index)])
        out[...] = total.astype(BF16)


def last(*args):
    return pl.pallas_call(
        last_kernel,
        in_specs=[VMEM] * 7,
        out_specs=VMEM,
        out_shape=jax.ShapeDtypeStruct((256, 1024), BF16),
        scratch_shapes=[pltpu.VMEM((256, 1024), BF16)],
        **small(flops=2 * 256 * 1024**2),
    )(*args)


def together(*values):
    return lax.optimization_barrier(values)


def local(transfer, leaf_map, volume_source):
    place = Place()
    own_map = transfer[0]

    got = permute(send_line(own_map), to_y_mirror)
    source = act(leaf_map[0], volume_source[0]).astype(BF16)
    line, to_pair, to_mirror, rest = pair_line(own_map, got, source)

    pair = permute(line, to_x_pair)
    mirror = permute(line, to_x_mirror)
    by_pair = permute(to_pair, to_y_pair)
    by_mirror = permute(to_mirror, to_y_mirror)
    (core_line,) = pack((line, got), ((0, 0, 4), (1, 0, 4)))
    core_line = permute(core_line, to_core)
    pair, mirror, by_pair, by_mirror, core_line, rest = together(
        pair, mirror, by_pair, by_mirror, core_line, rest
    )

    rest_pair = permute(rest, to_y_pair)
    rest_mirror = permute(rest, to_y_mirror)
    far_a = permute(pair[:2], to_x_mirror)
    far_b = permute(mirror[2:], to_x_pair)
    (core_x,) = pack((pair, mirror), ((0, 0, 4), (1, 0, 4)))
    core_x = permute(core_x, to_core)
    far_a, far_b, core_x, rest_pair, rest_mirror, by_pair, by_mirror = together(
        far_a, far_b, core_x, rest_pair, rest_mirror, by_pair, by_mirror
    )

    (sides,) = pack((by_pair, by_mirror), ((0, 0, 2), (1, 0, 2)))
    pair_sides = permute(sides, to_x_pair)
    mirror_sides = permute(sides, to_x_mirror)
    far, far_to_pair, far_to_mirror = pack(
        (far_a, far_b), ((0, 0, 2), (1, 0, 2)), "pair", "mirror"
    )
    far_pair = permute(far_to_pair, to_y_pair)
    far_mirror = permute(far_to_mirror, to_y_mirror)
    low_rows, high_rows = first_strips(own_map, by_pair, by_mirror, rest_pair, rest_mirror)
    low_rows, high_rows = permute(low_rows, to_y_mirror), permute(high_rows, to_y_pair)
    pair_sides, mirror_sides, far_pair, far_mirror, low_rows, high_rows = together(
        pair_sides, mirror_sides, far_pair, far_mirror, low_rows, high_rows
    )

    core_sides, core_far = pack(
        (sides, pair_sides, mirror_sides, far, far_pair, far_mirror),
        ((0, 0, 4), (1, 0, 4), (2, 0, 4)),
        ((3, 0, 4), (4, 0, 2), (5, 0, 2)),
    )
    core_sides, core_far = permute(core_sides, to_core), permute(core_far, to_core)
    strips = jnp.where(place.y_hi == 1, high_rows, low_rows)
    mine, others = strips[:64], strips[64:]
    beside = permute(others, to_x_pair)
    from_mirror = permute(mine, to_x_mirror)
    from_far = permute(others, to_x_far)
    maps, group_trace = join(
        0, (line, by_pair, by_mirror, pair, pair_sides, core_line, core_x, core_sides), mine, beside
    )
    other_maps, other_trace, plane_trace, moving = join(
        1,
        (far, far_pair, far_mirror, mirror, mirror_sides, core_far, core_x, core_sides),
        from_far, from_mirror, maps, group_trace,
    )

    (late,) = pack(
        (got, core_line, by_mirror, rest_mirror), ((0, 0, 4), (1, 4, 4), (2, 2, 2), (3, 0, 2))
    )
    added = [plane_trace[:32], plane_trace[32:]]
    parts = [permute(part, to_z_next) for part in (moving[:32], moving[32:])]
    other_map, plane_map = to_plane(maps, other_maps)
    for turn in range(7):
        parts = [act_add(plane_map, part, extra) for part, extra in zip(parts, added)]
        if turn == 0:
            late = together(late, *parts)[0]
            late = permute(late, to_y_pair)
        parts = [permute(part, to_z_next) for part in parts]

    lower_trace = jnp.where(place.x_lo == 1, beside, mine)
    own, across = lift(*parts, other_map, other_trace, maps, lower_trace)
    pieces = (
        own,
        permute(across, to_x_pair),
        permute(own, to_y_far),
        permute(across, to_xy_far),
    )
    traces = last(*pieces, got, core_line, late)
    return traces[None]


def solution(mesh):
    in_specs = (P("guide", None, None), P("guide", None, None), P("guide", "face", None))
    out_specs = P("guide", "face", None)
    return jax.shard_map(local, mesh=mesh, in_specs=in_specs, out_specs=out_specs, check_vma=False)
```

```python
import functools

import jax
import jax.numpy as jnp
from jax import lax
from jax.experimental import pallas as pl
from jax.experimental.pallas import tpu as pltpu
from jax.sharding import PartitionSpec as P

AXES = ("guide", "face")
BF16, F32 = jnp.bfloat16, jnp.float32
SIDE = 256
ANY = pl.BlockSpec(memory_space=pl.ANY)
VMEM = pl.BlockSpec(memory_space=pltpu.VMEM)


def coords(device):
    guide, face = divmod(device, 4)
    return guide // 2 % 4, guide % 2 * 2 + face // 2, guide // 8, face % 2


def device_at(x, y, z, core):
    x, y, z = x % 4, y % 4, z % 8
    return (z * 8 + x * 2 + y // 2) * 4 + y % 2 * 2 + core


def permute(block, target):
    route = [(i, device_at(*target(*coords(i)))) for i in range(256)]
    return lax.ppermute(block, AXES, route)


def to_core(x, y, z, c):
    return x, y, z, 1 - c


def to_y_mirror(x, y, z, c):
    return x, 3 - y, z, c


def to_y_pair(x, y, z, c):
    return x, y ^ 1, z, c


def to_y_far(x, y, z, c):
    return x, y + 2, z, c


def to_x_pair(x, y, z, c):
    return x ^ 1, y, z, c


def to_x_mirror(x, y, z, c):
    return 3 - x, y, z, c


def to_x_far(x, y, z, c):
    return x + 2, y, z, c


def to_xy_far(x, y, z, c):
    return x ^ 1, y + 2, z, c


def to_z_next(x, y, z, c):
    return x, y, z + 1, c


def act(linear_map, vectors):
    return lax.dot_general(
        vectors, linear_map, (((1,), (1,)), ((), ())), preferred_element_type=F32
    )


def act_add(linear_map, vectors, added):
    return (act(linear_map, vectors) + added.astype(F32)).astype(BF16)


class Place:
    def __init__(self):
        guide, self.face = lax.axis_index("guide"), lax.axis_index("face")
        self.x, self.y_hi, self.y_lo = guide // 2 % 4, guide % 2, self.face // 2
        self.core = self.face % 2
        self.x_hi, self.x_lo = self.x // 2, self.x % 2
        self.strip = (self.x_lo + self.x_hi) % 2


def span(index, size=SIDE):
    return pl.ds(pl.multiple_of(index * size, size), size)


def block_of(ref, row, col):
    return ref.at[span(row), span(col)]


def send_kernel(own, out):
    place = Place()
    line = span((place.face + 2) % 4)

    @pl.when(place.y_hi == 1)
    def _():
        for t in range(4):
            out[t] = own[line, t * SIDE : (t + 1) * SIDE]

    @pl.when(place.y_hi == 0)
    def _():
        for t in range(4):
            out[t] = own[t * SIDE : (t + 1) * SIDE, line]


def send_line(own):
    return pl.pallas_call(
        send_kernel,
        in_specs=[VMEM],
        out_specs=VMEM,
        out_shape=jax.ShapeDtypeStruct((4, SIDE, SIDE), BF16),
        compiler_params=pltpu.CompilerParams(vmem_limit_bytes=8 * 1024 * 1024),
    )(own)


def small(**sizes):
    return dict(
        compiler_params=pltpu.CompilerParams(vmem_limit_bytes=12 * 1024 * 1024),
        cost_estimate=pl.CostEstimate(
            flops=sizes.get("flops", 0), bytes_accessed=1024**2, transcendentals=0
        ),
    )


def blocks(count):
    return jax.ShapeDtypeStruct((count, SIDE, SIDE), BF16)


def line_kernel(own, got, line):
    place = Place()

    @pl.when(place.y_hi == 0)
    def _():
        row = jnp.concatenate([got[t] for t in range(4)], axis=1)
        for t in range(4):
            cols = slice(t * SIDE, (t + 1) * SIDE)
            line[t] = jnp.dot(row, own[:, cols], preferred_element_type=F32).astype(BF16)

    @pl.when(place.y_hi == 1)
    def _():
        col = jnp.concatenate([got[t] for t in range(4)], axis=0)
        for t in range(4):
            rows = slice(t * SIDE, (t + 1) * SIDE)
            line[t] = jnp.dot(own[rows, :], col, preferred_element_type=F32).astype(BF16)


def pair_line(own, got):
    return pl.pallas_call(
        line_kernel,
        in_specs=[VMEM] * 2,
        out_specs=VMEM,
        out_shape=blocks(4),
        **small(flops=2 * SIDE * 1024**2),
    )(own, got)


def multiply(left, right, out):
    @pl.loop(0, 4)
    def _(tile):
        cols = span(tile)
        out[:, cols] = jnp.dot(left[...], right[:, cols], preferred_element_type=F32).astype(BF16)


def strip_to_block(strip):
    return jnp.concatenate([strip[:, t * SIDE : (t + 1) * SIDE] for t in range(4)], axis=0)


def block_to_strip(block):
    return jnp.concatenate([block[64 * t : 64 * (t + 1)] for t in range(4)], axis=1)


def full_kernel(own, got, got_pair, core_a, core_b, source, theirs, *outs):
    partner, full, to_pair, to_mirror, mine, others = outs
    place = Place()
    quarters = ((0, got, 0), (2, got_pair, 0), (1, core_a, 4), (3, core_b, 0))

    def line_of(flip):
        return (place.y_lo + flip // 2) % 2 * 2 + (place.core + flip) % 2

    half = source[pl.ds(pl.multiple_of(128 * place.y_hi, 128), 128), :]

    @pl.when(place.y_hi == 1)
    def _():
        for flip, ref, start in quarters:
            for t in range(4):
                partner[t * SIDE : (t + 1) * SIDE, span(line_of(flip))] = ref[start + t]
        multiply(own, partner, full)
        for t in range(4):
            to_pair[t] = full[t * SIDE : (t + 1) * SIDE, span(line_of(2))]
        trace = act_add(own[...], theirs[...], half)
        mine[...] = trace[:64]
        others[...] = trace[64:]

    @pl.when(place.y_hi == 0)
    def _():
        for flip, ref, start in quarters:
            for t in range(4):
                partner[span(line_of(flip)), t * SIDE : (t + 1) * SIDE] = ref[start + t]
        multiply(partner, own, full)
        for t in range(4):
            to_pair[t] = full[span(line_of(2)), t * SIDE : (t + 1) * SIDE]
        trace = act_add(partner[...], half, theirs[...])
        mine[...] = trace[:64]
        others[...] = trace[64:]

    @pl.when(place.strip == 1)
    def _():
        first, second = mine[...], others[...]
        mine[...] = second
        others[...] = first

    to_mirror[0:4] = to_pair[0:4]
    to_pair[4] = strip_to_block(others[...])
    to_mirror[4] = strip_to_block(mine[...])


def pair_map(*args):
    strip = jax.ShapeDtypeStruct((64, 1024), BF16)
    return pl.pallas_call(
        full_kernel,
        in_specs=[VMEM] * 7,
        out_specs=[VMEM] * 6,
        out_shape=[map_shape(), map_shape(), blocks(5), blocks(5), strip, strip],
        compiler_params=pltpu.CompilerParams(vmem_limit_bytes=20 * 1024 * 1024),
        cost_estimate=pl.CostEstimate(
            flops=2 * 1024**3, bytes_accessed=8 * 1024**2, transcendentals=0
        ),
    )(*args)


def pack_kernel(*refs):
    out, filled = refs[-1], 0
    for ref in refs[:-1]:
        size = min(ref.shape[0], 4)
        out[filled : filled + size] = ref[:size]
        filled += size


def pack(*arrays):
    return pl.pallas_call(
        pack_kernel,
        in_specs=[VMEM] * len(arrays),
        out_specs=VMEM,
        out_shape=blocks(sum(min(array.shape[0], 4) for array in arrays)),
        **small(),
    )(*arrays)


def gather_copies(place, target, lines, sems):
    copies = []
    upper = place.y_hi == 1
    for flip, line in zip((0, 2, 1, 3), lines):
        index = (place.y_lo + flip // 2) % 2 * 2 + (place.core + flip) % 2
        for t in range(4):
            row = jnp.where(upper, t, index)
            col = jnp.where(upper, index, t)
            copies.append(
                pltpu.make_async_copy(line.at[t], block_of(target, row, col), sems.at[len(copies)])
            )
    return copies


def map_shape(*lead):
    return jax.ShapeDtypeStruct((*lead, 1024, 1024), BF16)


def join_kernel(*refs):
    pair, pair_2, mirror, mirror_2, far, far_2, core_b, core_c = refs[:8]
    full, mine, from_far, pair_strip, mirror_strip = refs[8:13]
    pair_full, others, group_trace, other_trace, plane_trace, moving, sems = refs[13:]
    place = Place()
    mirror_slot = place.x_lo
    pair_lines = (pair, pair_2, core_b.at[4:8], core_c.at[0:4])
    mirror_lines = (mirror, mirror_2, core_b.at[8:12], core_c.at[4:8])
    far_lines = (far, far_2, core_c.at[8:12], core_c.at[12:16])
    pair_copies = gather_copies(place, pair_full, pair_lines, sems.at[0])
    other_copies = gather_copies(place, others.at[mirror_slot], mirror_lines, sems.at[1])
    other_copies += gather_copies(place, others.at[1 - mirror_slot], far_lines, sems.at[2])
    for copy in pair_copies + other_copies:
        copy.start()
    for copy in pair_copies:
        copy.wait()
    beside, across = block_to_strip(pair_strip[4]), block_to_strip(mirror_strip[4])

    @pl.when(place.x_lo == 1)
    def _():
        group_trace[...] = act_add(full[...], beside, mine[...])

    @pl.when(place.x_lo == 0)
    def _():
        group_trace[...] = act_add(pair_full[...], mine[...], beside)

    for copy in other_copies:
        copy.wait()
    mirror_low = place.x_lo == 1
    low = jnp.where(mirror_low, across, from_far[...])
    high = jnp.where(mirror_low, from_far[...], across)
    other_trace[...] = act_add(others[0], low, high)

    def through(upper, lower, low, high):
        inner = act(lower[...], low[...]).astype(BF16)
        plane_trace[...] = act_add(upper[...], inner, high[...])

    @pl.when(jnp.logical_and(place.x_hi == 1, place.x_lo == 1))
    def _():
        through(full, pair_full, other_trace, group_trace)

    @pl.when(jnp.logical_and(place.x_hi == 1, place.x_lo == 0))
    def _():
        through(pair_full, full, other_trace, group_trace)

    @pl.when(place.x_hi == 0)
    def _():
        through(others.at[0], others.at[1], group_trace, other_trace)

    moving[...] = jnp.where(place.x_hi == 1, group_trace[...], plane_trace[...])


def join(*args):
    strip = jax.ShapeDtypeStruct((64, 1024), BF16)
    return pl.pallas_call(
        join_kernel,
        in_specs=[ANY] * 8 + [VMEM] * 5,
        out_specs=[VMEM] * 6,
        out_shape=[map_shape(), map_shape(2), strip, strip, strip, strip],
        scratch_shapes=[pltpu.SemaphoreType.DMA((3, 16))],
        compiler_params=pltpu.CompilerParams(vmem_limit_bytes=20 * 1024 * 1024),
        cost_estimate=pl.CostEstimate(
            flops=8 * 64 * 1024**2, bytes_accessed=14 * 1024**2, transcendentals=0
        ),
    )(*args)


def plane_kernel(full, pair_full, others, other, plane, own):
    place = Place()

    @pl.when(place.x_lo == 1)
    def _():
        multiply(full, pair_full, own)

    @pl.when(place.x_lo == 0)
    def _():
        multiply(pair_full, full, own)

    multiply(others.at[0], others.at[1], other)

    @pl.when(place.x_hi == 1)
    def _():
        multiply(own, other, plane)

    @pl.when(place.x_hi == 0)
    def _():
        multiply(other, own, plane)


def to_plane(*args):
    return pl.pallas_call(
        plane_kernel,
        in_specs=[VMEM] * 3,
        out_specs=[VMEM] * 2,
        out_shape=[map_shape()] * 2,
        scratch_shapes=[pltpu.VMEM((1024, 1024), BF16)],
        compiler_params=pltpu.CompilerParams(vmem_limit_bytes=20 * 1024 * 1024),
        cost_estimate=pl.CostEstimate(
            flops=6 * 1024**3, bytes_accessed=12 * 1024**2, transcendentals=0
        ),
    )(*args)


def lift_kernel(part_a, part_b, other_map, other_trace, full, pair_full, mine, beside, own, across):
    place = Place()
    own[0:32, :] = part_a[...]
    own[32:64, :] = part_b[...]

    @pl.when(place.x_hi == 1)
    def _():
        own[...] = act_add(other_map[...], own[...], other_trace[...])

    @pl.when(place.x_lo == 1)
    def _():
        across[...] = own[...]
        own[...] = act_add(pair_full[...], own[...], block_to_strip(beside[4]))

    @pl.when(place.x_lo == 0)
    def _():
        across[...] = act_add(full[...], own[...], mine[...])


def lift(*args):
    strip = jax.ShapeDtypeStruct((64, 1024), BF16)
    return pl.pallas_call(
        lift_kernel,
        in_specs=[VMEM] * 8,
        out_specs=[VMEM] * 2,
        out_shape=[strip, strip],
        **small(flops=4 * 64 * 1024**2),
    )(*args)


def last_kernel(e00, e01, e10, e11, partner, late, theirs, out, held):
    place = Place()
    for part, (flip_y, flip_x) in ((e00, (0, 0)), (e01, (0, 1)), (e10, (1, 0)), (e11, (1, 1))):
        index = 2 * ((place.y_hi + flip_y) % 2) + (place.strip + flip_x) % 2
        held[span(index, 64), :] = part[...]

    @pl.when(place.y_hi == 0)
    def _():
        out[...] = held[...]

    @pl.when(place.y_hi == 1)
    def _():
        added = jnp.concatenate([late[...], theirs[...]], axis=0)
        out[...] = act_add(partner[...], held[...], added)


def last(*args):
    return pl.pallas_call(
        last_kernel,
        in_specs=[VMEM] * 7,
        out_specs=VMEM,
        out_shape=jax.ShapeDtypeStruct((256, 1024), BF16),
        scratch_shapes=[pltpu.VMEM((256, 1024), BF16)],
        **small(flops=2 * 256 * 1024**2),
    )(*args)


def together(*values):
    return lax.optimization_barrier(values)


def local(transfer, leaf_map, volume_source):
    place = Place()
    own_map = transfer[0]

    got = permute(send_line(own_map), to_y_mirror)
    source = act(leaf_map[0], volume_source[0]).astype(BF16)
    got, source = together(got, source)
    line = pair_line(own_map, got)

    pair = permute(line, to_x_pair)
    mirror = permute(line, to_x_mirror)
    got_pair = permute(got, to_y_pair)
    halves = source.reshape(2, 128, 1024)
    theirs = permute(lax.dynamic_index_in_dim(halves, 1 - place.y_hi, 0, False), to_y_far)
    core_a = permute(pack(line, got), to_core)
    pair, mirror, got_pair, theirs, core_a = together(pair, mirror, got_pair, theirs, core_a)

    core_b = permute(pack(got_pair, pair, mirror), to_core)
    far_a = permute(pair[:2], to_x_mirror)
    far_b = permute(mirror[2:], to_x_pair)
    partner, full, to_pair, to_mirror, mine, others = pair_map(
        own_map, got, got_pair, core_a, core_b, source, theirs
    )

    pair_2 = permute(to_pair, to_x_pair)
    mirror_2 = permute(to_mirror, to_x_mirror)
    far = pack(far_a, far_b)
    far_2 = permute(far, to_y_pair)
    from_far = permute(others, to_x_far)
    pair_2, mirror_2, far_2, from_far = together(pair_2, mirror_2, far_2, from_far)

    core_c = permute(pack(pair_2, mirror_2, far, far_2), to_core)
    pair_full, other_maps, group_trace, other_trace, plane_trace, moving = join(
        pair, pair_2, mirror, mirror_2, far, far_2, core_b, core_c,
        full, mine, from_far, pair_2, mirror_2,
    )

    added = [plane_trace[:32], plane_trace[32:]]
    parts = [permute(part, to_z_next) for part in (moving[:32], moving[32:])]
    other_map, plane_map = to_plane(full, pair_full, other_maps)
    for turn in range(7):
        parts = [act_add(plane_map, part, extra) for part, extra in zip(parts, added)]
        if turn == 1:
            late = together(lax.dynamic_index_in_dim(halves, place.y_hi, 0, False), *parts)[0]
            late = permute(late, to_y_far)
        parts = [permute(part, to_z_next) for part in parts]

    own, across = lift(*parts, other_map, other_trace, full, pair_full, mine, pair_2)
    pieces = (
        own,
        permute(across, to_x_pair),
        permute(own, to_y_far),
        permute(across, to_xy_far),
    )
    traces = last(*pieces, partner, late, theirs)
    return traces[None]


def solution(mesh):
    in_specs = (P("guide", None, None), P("guide", None, None), P("guide", "face", None))
    out_specs = P("guide", "face", None)
    return jax.shard_map(local, mesh=mesh, in_specs=in_specs, out_specs=out_specs, check_vma=False)
```

```python
import functools

import jax
import jax.numpy as jnp
from jax import lax
from jax.experimental import pallas as pl
from jax.experimental.pallas import tpu as pltpu
from jax.sharding import PartitionSpec as P

AXES = ("guide", "face")
BF16, F32 = jnp.bfloat16, jnp.float32
SIDE = 256
ANY = pl.BlockSpec(memory_space=pl.ANY)
VMEM = pl.BlockSpec(memory_space=pltpu.VMEM)


def coords(device):
    guide, face = divmod(device, 4)
    return guide // 2 % 4, guide % 2 * 2 + face // 2, guide // 8, face % 2


def device_at(x, y, z, core):
    x, y, z = x % 4, y % 4, z % 8
    return (z * 8 + x * 2 + y // 2) * 4 + y % 2 * 2 + core


def permute(block, target):
    route = [(i, device_at(*target(*coords(i)))) for i in range(256)]
    return lax.ppermute(block, AXES, route)


def to_core(x, y, z, c):
    return x, y, z, 1 - c


def to_y_mirror(x, y, z, c):
    return x, 3 - y, z, c


def to_y_pair(x, y, z, c):
    return x, y ^ 1, z, c


def to_y_far(x, y, z, c):
    return x, y + 2, z, c


def to_x_pair(x, y, z, c):
    return x ^ 1, y, z, c


def to_x_mirror(x, y, z, c):
    return 3 - x, y, z, c


def to_xy_far(x, y, z, c):
    return x ^ 1, y + 2, z, c


def to_z_next(x, y, z, c):
    return x, y, z + 1, c


def act(linear_map, vectors):
    return lax.dot_general(
        vectors, linear_map, (((1,), (1,)), ((), ())), preferred_element_type=F32
    )


def act_add(linear_map, vectors, added):
    return (act(linear_map, vectors) + added.astype(F32)).astype(BF16)


class Place:
    def __init__(self):
        guide, self.face = lax.axis_index("guide"), lax.axis_index("face")
        self.x, self.y_hi, self.y_lo = guide // 2 % 4, guide % 2, self.face // 2
        self.core = self.face % 2
        self.x_hi, self.x_lo = self.x // 2, self.x % 2
        self.strip = (self.x_lo + self.x_hi) % 2


def span(index, size=SIDE):
    return pl.ds(pl.multiple_of(index * size, size), size)


def block_of(ref, row, col):
    return ref.at[span(row), span(col)]


def send_kernel(own, out):
    place = Place()
    line = span((place.face + 2) % 4)

    @pl.when(place.y_hi == 1)
    def _():
        for t in range(4):
            out[t] = own[line, t * SIDE : (t + 1) * SIDE]

    @pl.when(place.y_hi == 0)
    def _():
        for t in range(4):
            out[t] = own[t * SIDE : (t + 1) * SIDE, line]


def send_line(own):
    return pl.pallas_call(
        send_kernel,
        in_specs=[VMEM],
        out_specs=VMEM,
        out_shape=jax.ShapeDtypeStruct((4, SIDE, SIDE), BF16),
        compiler_params=pltpu.CompilerParams(vmem_limit_bytes=8 * 1024 * 1024),
    )(own)


def small(**sizes):
    return dict(
        compiler_params=pltpu.CompilerParams(vmem_limit_bytes=12 * 1024 * 1024),
        cost_estimate=pl.CostEstimate(
            flops=sizes.get("flops", 0), bytes_accessed=1024**2, transcendentals=0
        ),
    )


def blocks(count):
    return jax.ShapeDtypeStruct((count, SIDE, SIDE), BF16)


def line_kernel(own, got, line):
    place = Place()

    @pl.when(place.y_hi == 0)
    def _():
        row = jnp.concatenate([got[t] for t in range(4)], axis=1)
        for t in range(4):
            cols = slice(t * SIDE, (t + 1) * SIDE)
            line[t] = jnp.dot(row, own[:, cols], preferred_element_type=F32).astype(BF16)

    @pl.when(place.y_hi == 1)
    def _():
        col = jnp.concatenate([got[t] for t in range(4)], axis=0)
        for t in range(4):
            rows = slice(t * SIDE, (t + 1) * SIDE)
            line[t] = jnp.dot(own[rows, :], col, preferred_element_type=F32).astype(BF16)


def pair_line(own, got):
    return pl.pallas_call(
        line_kernel,
        in_specs=[VMEM] * 2,
        out_specs=VMEM,
        out_shape=blocks(4),
        **small(flops=2 * SIDE * 1024**2),
    )(own, got)


def multiply(left, right, out):
    @pl.loop(0, 4)
    def _(tile):
        cols = span(tile)
        out[:, cols] = jnp.dot(left[...], right[:, cols], preferred_element_type=F32).astype(BF16)


def full_kernel(own, got, got_pair, core_a, core_b, source, theirs, *outs):
    partner, full, mine, others = outs
    place = Place()
    quarters = ((0, got, 0), (2, got_pair, 0), (1, core_a, 0), (3, core_b, 0))

    def line_of(flip):
        return (place.y_lo + flip // 2) % 2 * 2 + (place.core + flip) % 2

    half = source[pl.ds(pl.multiple_of(128 * place.y_hi, 128), 128), :]

    @pl.when(place.y_hi == 1)
    def _():
        for flip, ref, start in quarters:
            for t in range(4):
                partner[t * SIDE : (t + 1) * SIDE, span(line_of(flip))] = ref[start + t]
        multiply(own, partner, full)
        trace = act_add(own[...], theirs[...], half)
        mine[...] = trace[:64]
        others[...] = trace[64:]

    @pl.when(place.y_hi == 0)
    def _():
        for flip, ref, start in quarters:
            for t in range(4):
                partner[span(line_of(flip)), t * SIDE : (t + 1) * SIDE] = ref[start + t]
        multiply(partner, own, full)
        trace = act_add(partner[...], half, theirs[...])
        mine[...] = trace[:64]
        others[...] = trace[64:]

    @pl.when(place.strip == 1)
    def _():
        first, second = mine[...], others[...]
        mine[...] = second
        others[...] = first


def pair_map(*args):
    strip = jax.ShapeDtypeStruct((64, 1024), BF16)
    return pl.pallas_call(
        full_kernel,
        in_specs=[VMEM] * 7,
        out_specs=[VMEM] * 4,
        out_shape=[map_shape(), map_shape(), strip, strip],
        compiler_params=pltpu.CompilerParams(vmem_limit_bytes=16 * 1024 * 1024),
        cost_estimate=pl.CostEstimate(
            flops=2 * 1024**3, bytes_accessed=8 * 1024**2, transcendentals=0
        ),
    )(*args)


def pack_kernel(*refs):
    out, filled = refs[-1], 0
    for ref in refs[:-1]:
        size = min(ref.shape[0], 4)
        out[filled : filled + size] = ref[:size]
        filled += size


def pack(*arrays):
    return pl.pallas_call(
        pack_kernel,
        in_specs=[VMEM] * len(arrays),
        out_specs=VMEM,
        out_shape=blocks(sum(min(array.shape[0], 4) for array in arrays)),
        **small(),
    )(*arrays)


def gather_copies(place, target, lines, sems):
    copies = []
    upper = place.y_hi == 1
    for flip, line in zip((0, 2, 1, 3), lines):
        index = (place.y_lo + flip // 2) % 2 * 2 + (place.core + flip) % 2
        for t in range(4):
            row = jnp.where(upper, t, index)
            col = jnp.where(upper, index, t)
            copies.append(
                pltpu.make_async_copy(line.at[t], block_of(target, row, col), sems.at[len(copies)])
            )
    return copies


def map_shape(*lead):
    return jax.ShapeDtypeStruct((*lead, 1024, 1024), BF16)


def join_kernel(*refs):
    pair, pair_2, mirror, mirror_2, far, far_2, core_b, core_c = refs[:8]
    full, mine, beside, across, from_far = refs[8:13]
    pair_full, others, group_trace, other_trace, plane_trace, moving, sems = refs[13:]
    place = Place()
    mirror_slot = place.x_lo
    pair_lines = (pair, pair_2, core_b.at[4:8], core_c.at[0:4])
    mirror_lines = (mirror, mirror_2, core_b.at[8:12], core_c.at[4:8])
    far_lines = (far, far_2, core_c.at[8:12], core_c.at[12:16])
    pair_copies = gather_copies(place, pair_full, pair_lines, sems.at[0])
    other_copies = gather_copies(place, others.at[mirror_slot], mirror_lines, sems.at[1])
    other_copies += gather_copies(place, others.at[1 - mirror_slot], far_lines, sems.at[2])
    for copy in pair_copies + other_copies:
        copy.start()
    for copy in pair_copies:
        copy.wait()

    @pl.when(place.x_lo == 1)
    def _():
        group_trace[...] = act_add(full[...], beside[...], mine[...])

    @pl.when(place.x_lo == 0)
    def _():
        group_trace[...] = act_add(pair_full[...], mine[...], beside[...])

    for copy in other_copies:
        copy.wait()
    mirror_low = place.x_lo == 1
    low = jnp.where(mirror_low, across[...], from_far[...])
    high = jnp.where(mirror_low, from_far[...], across[...])
    other_trace[...] = act_add(others[0], low, high)

    def through(upper, lower, low, high):
        inner = act(lower[...], low[...]).astype(BF16)
        plane_trace[...] = act_add(upper[...], inner, high[...])

    @pl.when(jnp.logical_and(place.x_hi == 1, place.x_lo == 1))
    def _():
        through(full, pair_full, other_trace, group_trace)

    @pl.when(jnp.logical_and(place.x_hi == 1, place.x_lo == 0))
    def _():
        through(pair_full, full, other_trace, group_trace)

    @pl.when(place.x_hi == 0)
    def _():
        through(others.at[0], others.at[1], group_trace, other_trace)

    moving[...] = jnp.where(place.x_hi == 1, group_trace[...], plane_trace[...])


def join(*args):
    strip = jax.ShapeDtypeStruct((64, 1024), BF16)
    return pl.pallas_call(
        join_kernel,
        in_specs=[ANY] * 8 + [VMEM] * 5,
        out_specs=[VMEM] * 6,
        out_shape=[map_shape(), map_shape(2), strip, strip, strip, strip],
        scratch_shapes=[pltpu.SemaphoreType.DMA((3, 16))],
        compiler_params=pltpu.CompilerParams(vmem_limit_bytes=18 * 1024 * 1024),
        cost_estimate=pl.CostEstimate(
            flops=8 * 64 * 1024**2, bytes_accessed=14 * 1024**2, transcendentals=0
        ),
    )(*args)


def plane_kernel(full, pair_full, others, other, plane, own):
    place = Place()

    @pl.when(place.x_lo == 1)
    def _():
        multiply(full, pair_full, own)

    @pl.when(place.x_lo == 0)
    def _():
        multiply(pair_full, full, own)

    multiply(others.at[0], others.at[1], other)

    @pl.when(place.x_hi == 1)
    def _():
        multiply(own, other, plane)

    @pl.when(place.x_hi == 0)
    def _():
        multiply(other, own, plane)


def to_plane(*args):
    return pl.pallas_call(
        plane_kernel,
        in_specs=[VMEM] * 3,
        out_specs=[VMEM] * 2,
        out_shape=[map_shape()] * 2,
        scratch_shapes=[pltpu.VMEM((1024, 1024), BF16)],
        compiler_params=pltpu.CompilerParams(vmem_limit_bytes=18 * 1024 * 1024),
        cost_estimate=pl.CostEstimate(
            flops=6 * 1024**3, bytes_accessed=12 * 1024**2, transcendentals=0
        ),
    )(*args)


def lift_kernel(part_a, part_b, other_map, other_trace, full, pair_full, mine, beside, own, across):
    place = Place()
    own[0:32, :] = part_a[...]
    own[32:64, :] = part_b[...]

    @pl.when(place.x_hi == 1)
    def _():
        own[...] = act_add(other_map[...], own[...], other_trace[...])

    @pl.when(place.x_lo == 1)
    def _():
        across[...] = own[...]
        own[...] = act_add(pair_full[...], own[...], beside[...])

    @pl.when(place.x_lo == 0)
    def _():
        across[...] = act_add(full[...], own[...], mine[...])


def lift(*args):
    strip = jax.ShapeDtypeStruct((64, 1024), BF16)
    return pl.pallas_call(
        lift_kernel,
        in_specs=[VMEM] * 8,
        out_specs=[VMEM] * 2,
        out_shape=[strip, strip],
        **small(flops=4 * 64 * 1024**2),
    )(*args)


def last_kernel(e00, e01, e10, e11, partner, late, theirs, out, held):
    place = Place()
    for part, (flip_y, flip_x) in ((e00, (0, 0)), (e01, (0, 1)), (e10, (1, 0)), (e11, (1, 1))):
        index = 2 * ((place.y_hi + flip_y) % 2) + (place.strip + flip_x) % 2
        held[span(index, 64), :] = part[...]

    @pl.when(place.y_hi == 0)
    def _():
        out[...] = held[...]

    @pl.when(place.y_hi == 1)
    def _():
        added = jnp.concatenate([late[...], theirs[...]], axis=0)
        out[...] = act_add(partner[...], held[...], added)


def last(*args):
    return pl.pallas_call(
        last_kernel,
        in_specs=[VMEM] * 7,
        out_specs=VMEM,
        out_shape=jax.ShapeDtypeStruct((256, 1024), BF16),
        scratch_shapes=[pltpu.VMEM((256, 1024), BF16)],
        **small(flops=2 * 256 * 1024**2),
    )(*args)


def together(*values):
    return lax.optimization_barrier(values)


def local(transfer, leaf_map, volume_source):
    place = Place()
    own_map = transfer[0]

    got = permute(send_line(own_map), to_y_mirror)
    source = act(leaf_map[0], volume_source[0]).astype(BF16)
    got, source = together(got, source)
    line = pair_line(own_map, got)

    pair = permute(line, to_x_pair)
    mirror = permute(line, to_x_mirror)
    got_pair = permute(got, to_y_pair)
    relay = permute(source, to_y_mirror).reshape(2, 128, 1024)
    theirs = permute(lax.dynamic_index_in_dim(relay, place.y_hi, 0, False), to_y_pair)
    core_a = permute(got, to_core)
    pair, mirror, got_pair, theirs, core_a = together(pair, mirror, got_pair, theirs, core_a)

    line_2 = pair_line(own_map, got_pair)
    pair_2 = permute(line_2, to_x_pair)
    mirror_2 = permute(line_2, to_x_mirror)
    far = pack(permute(pair[:2], to_x_mirror), permute(mirror[2:], to_x_pair))
    far_2 = permute(far, to_y_pair)
    core_b = permute(pack(got_pair, pair, mirror), to_core)
    partner, full, mine, others = pair_map(
        own_map, got, got_pair, core_a, core_b, source, theirs
    )
    beside = permute(others, to_x_pair)
    across = permute(mine, to_x_mirror)
    pair_2, mirror_2, far_2, beside, across = together(pair_2, mirror_2, far_2, beside, across)

    core_c = permute(pack(pair_2, mirror_2, far, far_2), to_core)
    from_far = permute(beside, to_x_mirror)
    pair_full, other_maps, group_trace, other_trace, plane_trace, moving = join(
        pair, pair_2, mirror, mirror_2, far, far_2, core_b, core_c,
        full, mine, beside, across, from_far,
    )

    added = [plane_trace[:32], plane_trace[32:]]
    parts = [permute(part, to_z_next) for part in (moving[:32], moving[32:])]
    other_map, plane_map = to_plane(full, pair_full, other_maps)
    for turn in range(7):
        parts = [act_add(plane_map, part, extra) for part, extra in zip(parts, added)]
        if turn == 1:
            late = lax.dynamic_index_in_dim(relay, 1 - place.y_hi, 0, False)
            late = permute(together(late, *parts)[0], to_y_pair)
        parts = [permute(part, to_z_next) for part in parts]

    own, other = lift(*parts, other_map, other_trace, full, pair_full, mine, beside)
    pieces = (
        own,
        permute(other, to_x_pair),
        permute(own, to_y_far),
        permute(other, to_xy_far),
    )
    traces = last(*pieces, partner, late, theirs)
    return traces[None]


def solution(mesh):
    in_specs = (P("guide", None, None), P("guide", None, None), P("guide", "face", None))
    out_specs = P("guide", "face", None)
    return jax.shard_map(local, mesh=mesh, in_specs=in_specs, out_specs=out_specs, check_vma=False)
```

```python
import functools

import jax
import jax.numpy as jnp
from jax import lax
from jax.experimental import pallas as pl
from jax.experimental.pallas import tpu as pltpu
from jax.sharding import PartitionSpec as P

AXES = ("guide", "face")
BF16, F32 = jnp.bfloat16, jnp.float32
SIDE = 256
ANY = pl.BlockSpec(memory_space=pl.ANY)
VMEM = pl.BlockSpec(memory_space=pltpu.VMEM)


def coords(device):
    guide, face = divmod(device, 4)
    return guide // 2 % 4, guide % 2 * 2 + face // 2, guide // 8, face % 2


def device_at(x, y, z, core):
    x, y, z = x % 4, y % 4, z % 8
    return (z * 8 + x * 2 + y // 2) * 4 + y % 2 * 2 + core


def permute(block, target):
    route = [(i, device_at(*target(*coords(i)))) for i in range(256)]
    return lax.ppermute(block, AXES, route)


def to_core(x, y, z, c):
    return x, y, z, 1 - c


def to_y_mirror(x, y, z, c):
    return x, 3 - y, z, c


def to_y_pair(x, y, z, c):
    return x, y ^ 1, z, c


def to_y_far(x, y, z, c):
    return x, y + 2, z, c


def to_x_pair(x, y, z, c):
    return x ^ 1, y, z, c


def to_x_mirror(x, y, z, c):
    return 3 - x, y, z, c


def to_xy_far(x, y, z, c):
    return x ^ 1, y + 2, z, c


def to_z_next(x, y, z, c):
    return x, y, z + 1, c


def act(linear_map, vectors):
    return lax.dot_general(
        vectors, linear_map, (((1,), (1,)), ((), ())), preferred_element_type=F32
    )


def act_add(linear_map, vectors, added):
    return (act(linear_map, vectors) + added.astype(F32)).astype(BF16)


class Place:
    def __init__(self):
        guide, self.face = lax.axis_index("guide"), lax.axis_index("face")
        self.x, self.y_hi, self.y_lo = guide // 2 % 4, guide % 2, self.face // 2
        self.core = self.face % 2
        self.x_hi, self.x_lo = self.x // 2, self.x % 2
        self.strip = (self.x_lo + self.x_hi) % 2


def span(index, size=SIDE):
    return pl.ds(pl.multiple_of(index * size, size), size)


def block_of(ref, row, col):
    return ref.at[span(row), span(col)]


def send_kernel(own, out):
    place = Place()
    line = span((place.face + 2) % 4)

    @pl.when(place.y_hi == 1)
    def _():
        for t in range(4):
            out[t] = own[line, t * SIDE : (t + 1) * SIDE]

    @pl.when(place.y_hi == 0)
    def _():
        for t in range(4):
            out[t] = own[t * SIDE : (t + 1) * SIDE, line]


def send_line(own):
    return pl.pallas_call(
        send_kernel,
        in_specs=[VMEM],
        out_specs=VMEM,
        out_shape=jax.ShapeDtypeStruct((4, SIDE, SIDE), BF16),
        compiler_params=pltpu.CompilerParams(vmem_limit_bytes=8 * 1024 * 1024),
    )(own)


def small(**sizes):
    return dict(
        compiler_params=pltpu.CompilerParams(vmem_limit_bytes=12 * 1024 * 1024),
        cost_estimate=pl.CostEstimate(
            flops=sizes.get("flops", 0), bytes_accessed=1024**2, transcendentals=0
        ),
    )


def blocks(count):
    return jax.ShapeDtypeStruct((count, SIDE, SIDE), BF16)


def source_kernel(volume, leaf, out):
    out[...] = act(leaf[...], volume[...]).astype(BF16)


def to_source(leaf, volume):
    rows, depth = volume.shape
    return pl.pallas_call(
        source_kernel,
        grid=(leaf.shape[0] // SIDE,),
        in_specs=[
            pl.BlockSpec((rows, depth), lambda t: (0, 0)),
            pl.BlockSpec((SIDE, depth), lambda t: (t, 0)),
        ],
        out_specs=pl.BlockSpec((rows, SIDE), lambda t: (0, t)),
        out_shape=jax.ShapeDtypeStruct((rows, leaf.shape[0]), BF16),
        compiler_params=pltpu.CompilerParams(vmem_limit_bytes=16 * 1024 * 1024),
        cost_estimate=pl.CostEstimate(
            flops=2 * rows * depth * leaf.shape[0],
            bytes_accessed=2 * depth * (rows + leaf.shape[0]),
            transcendentals=0,
        ),
    )(volume, leaf)


def line_kernel(own, got, line):
    place = Place()

    @pl.when(place.y_hi == 0)
    def _():
        row = jnp.concatenate([got[t] for t in range(4)], axis=1)
        for t in range(4):
            cols = slice(t * SIDE, (t + 1) * SIDE)
            line[t] = jnp.dot(row, own[:, cols], preferred_element_type=F32).astype(BF16)

    @pl.when(place.y_hi == 1)
    def _():
        col = jnp.concatenate([got[t] for t in range(4)], axis=0)
        for t in range(4):
            rows = slice(t * SIDE, (t + 1) * SIDE)
            line[t] = jnp.dot(own[rows, :], col, preferred_element_type=F32).astype(BF16)


def pair_line(own, got):
    return pl.pallas_call(
        line_kernel,
        in_specs=[VMEM] * 2,
        out_specs=VMEM,
        out_shape=blocks(4),
        **small(flops=2 * SIDE * 1024**2),
    )(own, got)


def multiply(left, right, out):
    @pl.loop(0, 4)
    def _(tile):
        cols = span(tile)
        out[:, cols] = jnp.dot(left[...], right[:, cols], preferred_element_type=F32).astype(BF16)


def full_kernel(own, got, got_pair, core_got, core_pair, source, theirs, *outs):
    partner, full, mine, others = outs
    place = Place()
    quarters = ((0, got), (2, got_pair), (1, core_got), (3, core_pair))

    def line_of(flip):
        return (place.y_lo + flip // 2) % 2 * 2 + (place.core + flip) % 2

    half = source[pl.ds(pl.multiple_of(128 * place.y_hi, 128), 128), :]

    @pl.when(place.y_hi == 1)
    def _():
        for flip, ref in quarters:
            for t in range(4):
                partner[t * SIDE : (t + 1) * SIDE, span(line_of(flip))] = ref[t]
        multiply(own, partner, full)
        trace = act_add(own[...], theirs[...], half)
        mine[...] = trace[:64]
        others[...] = trace[64:]

    @pl.when(place.y_hi == 0)
    def _():
        for flip, ref in quarters:
            for t in range(4):
                partner[span(line_of(flip)), t * SIDE : (t + 1) * SIDE] = ref[t]
        multiply(partner, own, full)
        trace = act_add(partner[...], half, theirs[...])
        mine[...] = trace[:64]
        others[...] = trace[64:]

    @pl.when(place.strip == 1)
    def _():
        first, second = mine[...], others[...]
        mine[...] = second
        others[...] = first


def pair_map(*args):
    strip = jax.ShapeDtypeStruct((64, 1024), BF16)
    return pl.pallas_call(
        full_kernel,
        in_specs=[VMEM] * 7,
        out_specs=[VMEM] * 4,
        out_shape=[map_shape(), map_shape(), strip, strip],
        compiler_params=pltpu.CompilerParams(vmem_limit_bytes=16 * 1024 * 1024),
        cost_estimate=pl.CostEstimate(
            flops=2 * 1024**3, bytes_accessed=8 * 1024**2, transcendentals=0
        ),
    )(*args)


def pack_kernel(*refs):
    out, filled = refs[-1], 0
    for ref in refs[:-1]:
        size = min(ref.shape[0], 4)
        out[filled : filled + size] = ref[:size]
        filled += size


def pack(*arrays):
    return pl.pallas_call(
        pack_kernel,
        in_specs=[VMEM] * len(arrays),
        out_specs=VMEM,
        out_shape=blocks(sum(min(array.shape[0], 4) for array in arrays)),
        **small(),
    )(*arrays)


def gather_copies(place, target, lines, sems):
    copies = []
    upper = place.y_hi == 1
    for flip, line in zip((0, 2, 1, 3), lines):
        index = (place.y_lo + flip // 2) % 2 * 2 + (place.core + flip) % 2
        for t in range(4):
            row = jnp.where(upper, t, index)
            col = jnp.where(upper, index, t)
            copies.append(
                pltpu.make_async_copy(line.at[t], block_of(target, row, col), sems.at[len(copies)])
            )
    return copies


def map_shape(*lead):
    return jax.ShapeDtypeStruct((*lead, 1024, 1024), BF16)


def join_kernel(*refs):
    pair, pair_2, mirror, mirror_2, far, far_2, core = refs[:7]
    full, mine, beside, across, from_far = refs[7:12]
    pair_full, others, group_trace, other_trace, plane_trace, moving, sems = refs[12:]
    place = Place()
    mirror_slot = place.x_lo
    pair_lines = (pair, pair_2, core.at[0:4], core.at[8:12])
    mirror_lines = (mirror, mirror_2, core.at[4:8], core.at[12:16])
    far_lines = (far, far_2, core.at[16:20], core.at[20:24])
    pair_copies = gather_copies(place, pair_full, pair_lines, sems.at[0])
    other_copies = gather_copies(place, others.at[mirror_slot], mirror_lines, sems.at[1])
    other_copies += gather_copies(place, others.at[1 - mirror_slot], far_lines, sems.at[2])
    for copy in pair_copies + other_copies:
        copy.start()
    for copy in pair_copies:
        copy.wait()

    @pl.when(place.x_lo == 1)
    def _():
        group_trace[...] = act_add(full[...], beside[...], mine[...])

    @pl.when(place.x_lo == 0)
    def _():
        group_trace[...] = act_add(pair_full[...], mine[...], beside[...])

    for copy in other_copies:
        copy.wait()
    mirror_low = place.x_lo == 1
    low = jnp.where(mirror_low, across[...], from_far[...])
    high = jnp.where(mirror_low, from_far[...], across[...])
    other_trace[...] = act_add(others[0], low, high)

    def through(upper, lower, low, high):
        inner = act(lower[...], low[...]).astype(BF16)
        plane_trace[...] = act_add(upper[...], inner, high[...])

    @pl.when(jnp.logical_and(place.x_hi == 1, place.x_lo == 1))
    def _():
        through(full, pair_full, other_trace, group_trace)

    @pl.when(jnp.logical_and(place.x_hi == 1, place.x_lo == 0))
    def _():
        through(pair_full, full, other_trace, group_trace)

    @pl.when(place.x_hi == 0)
    def _():
        through(others.at[0], others.at[1], group_trace, other_trace)

    moving[...] = jnp.where(place.x_hi == 1, group_trace[...], plane_trace[...])


def join(*args):
    strip = jax.ShapeDtypeStruct((64, 1024), BF16)
    return pl.pallas_call(
        join_kernel,
        in_specs=[ANY] * 7 + [VMEM] * 5,
        out_specs=[VMEM] * 6,
        out_shape=[map_shape(), map_shape(2), strip, strip, strip, strip],
        scratch_shapes=[pltpu.SemaphoreType.DMA((3, 16))],
        compiler_params=pltpu.CompilerParams(vmem_limit_bytes=18 * 1024 * 1024),
        cost_estimate=pl.CostEstimate(
            flops=8 * 64 * 1024**2, bytes_accessed=14 * 1024**2, transcendentals=0
        ),
    )(*args)


def plane_kernel(full, pair_full, others, other, plane, own):
    place = Place()

    @pl.when(place.x_lo == 1)
    def _():
        multiply(full, pair_full, own)

    @pl.when(place.x_lo == 0)
    def _():
        multiply(pair_full, full, own)

    multiply(others.at[0], others.at[1], other)

    @pl.when(place.x_hi == 1)
    def _():
        multiply(own, other, plane)

    @pl.when(place.x_hi == 0)
    def _():
        multiply(other, own, plane)


def to_plane(*args):
    return pl.pallas_call(
        plane_kernel,
        in_specs=[VMEM] * 3,
        out_specs=[VMEM] * 2,
        out_shape=[map_shape()] * 2,
        scratch_shapes=[pltpu.VMEM((1024, 1024), BF16)],
        compiler_params=pltpu.CompilerParams(vmem_limit_bytes=18 * 1024 * 1024),
        cost_estimate=pl.CostEstimate(
            flops=6 * 1024**3, bytes_accessed=12 * 1024**2, transcendentals=0
        ),
    )(*args)


def lift_kernel(part_a, part_b, other_map, other_trace, full, pair_full, mine, beside, own, across):
    place = Place()
    own[0:32, :] = part_a[...]
    own[32:64, :] = part_b[...]

    @pl.when(place.x_hi == 1)
    def _():
        own[...] = act_add(other_map[...], own[...], other_trace[...])

    @pl.when(place.x_lo == 1)
    def _():
        across[...] = own[...]
        own[...] = act_add(pair_full[...], own[...], beside[...])

    @pl.when(place.x_lo == 0)
    def _():
        across[...] = act_add(full[...], own[...], mine[...])


def lift(*args):
    strip = jax.ShapeDtypeStruct((64, 1024), BF16)
    return pl.pallas_call(
        lift_kernel,
        in_specs=[VMEM] * 8,
        out_specs=[VMEM] * 2,
        out_shape=[strip, strip],
        **small(flops=4 * 64 * 1024**2),
    )(*args)


def last_kernel(e00, e01, e10, e11, partner, late, theirs, out, held):
    place = Place()
    for part, (flip_y, flip_x) in ((e00, (0, 0)), (e01, (0, 1)), (e10, (1, 0)), (e11, (1, 1))):
        index = 2 * ((place.y_hi + flip_y) % 2) + (place.strip + flip_x) % 2
        held[span(index, 64), :] = part[...]

    @pl.when(place.y_hi == 0)
    def _():
        out[...] = held[...]

    @pl.when(place.y_hi == 1)
    def _():
        added = jnp.concatenate([late[...], theirs[...]], axis=0)
        out[...] = act_add(partner[...], held[...], added)


def last(*args):
    return pl.pallas_call(
        last_kernel,
        in_specs=[VMEM] * 7,
        out_specs=VMEM,
        out_shape=jax.ShapeDtypeStruct((256, 1024), BF16),
        scratch_shapes=[pltpu.VMEM((256, 1024), BF16)],
        **small(flops=2 * 256 * 1024**2),
    )(*args)


def together(*values):
    return lax.optimization_barrier(values)


def local(transfer, leaf_map, volume_source):
    place = Place()
    own_map = transfer[0]

    got = permute(send_line(own_map), to_y_mirror)
    source = to_source(leaf_map[0], volume_source[0])
    halves = source.reshape(2, 128, 1024)
    relay = permute(lax.dynamic_index_in_dim(halves, 1 - place.y_hi, 0, False), to_y_pair)
    got, relay = together(got, relay)
    line = pair_line(own_map, got)

    got_pair = permute(got, to_y_pair)
    pair = permute(line, to_x_pair)
    mirror = permute(line, to_x_mirror)
    theirs = permute(relay, to_y_mirror)
    core_got = permute(got, to_core)
    core_pair = permute(got_pair, to_core)
    line_2 = pair_line(own_map, got_pair)
    pair, mirror, theirs, core_got, core_pair, line_2 = together(
        pair, mirror, theirs, core_got, core_pair, line_2
    )

    pair_2 = permute(line_2, to_x_pair)
    mirror_2 = permute(line_2, to_x_mirror)
    far_a, far_b = permute(pair[:2], to_x_mirror), permute(mirror[2:], to_x_pair)
    partner, full, mine, others = pair_map(
        own_map, got, got_pair, core_got, core_pair, source, theirs
    )
    far_a, far_b, mine, others = together(far_a, far_b, mine, others)
    far = pack(far_a, far_b)
    far_2 = permute(far, to_y_pair)
    beside = permute(others, to_x_pair)
    across = permute(mine, to_x_mirror)
    pair_2, mirror_2, far_2, beside, across = together(pair_2, mirror_2, far_2, beside, across)

    core = permute(pack(pair, mirror, pair_2, mirror_2, far, far_2), to_core)
    from_far = permute(beside, to_x_mirror)
    pair_full, other_maps, group_trace, other_trace, plane_trace, moving = join(
        pair, pair_2, mirror, mirror_2, far, far_2, core,
        full, mine, beside, across, from_far,
    )

    added = [plane_trace[:32], plane_trace[32:]]
    parts = [permute(part, to_z_next) for part in (moving[:32], moving[32:])]
    other_map, plane_map = to_plane(full, pair_full, other_maps)
    for turn in range(7):
        parts = [act_add(plane_map, part, extra) for part, extra in zip(parts, added)]
        if turn == 1:
            late = lax.dynamic_index_in_dim(halves, place.y_hi, 0, False)
            late = permute(together(late, *parts)[0], to_y_far)
        parts = [permute(part, to_z_next) for part in parts]

    own, other = lift(*parts, other_map, other_trace, full, pair_full, mine, beside)
    pieces = (
        own,
        permute(other, to_x_pair),
        permute(own, to_y_far),
        permute(other, to_xy_far),
    )
    traces = last(*pieces, partner, late, theirs)
    return traces[None]


def solution(mesh):
    in_specs = (P("guide", None, None), P("guide", None, None), P("guide", "face", None))
    out_specs = P("guide", "face", None)
    return jax.shard_map(local, mesh=mesh, in_specs=in_specs, out_specs=out_specs, check_vma=False)
```

```python
import functools

import jax
import jax.numpy as jnp
from jax import lax
from jax.experimental import pallas as pl
from jax.experimental.pallas import tpu as pltpu
from jax.sharding import PartitionSpec as P

AXES = ("guide", "face")
BF16, F32 = jnp.bfloat16, jnp.float32
SIDE = 256
ANY = pl.BlockSpec(memory_space=pl.ANY)
VMEM = pl.BlockSpec(memory_space=pltpu.VMEM)


def coords(device):
    guide, face = divmod(device, 4)
    return guide // 2 % 4, guide % 2 * 2 + face // 2, guide // 8, face % 2


def device_at(x, y, z, core):
    x, y, z = x % 4, y % 4, z % 8
    return (z * 8 + x * 2 + y // 2) * 4 + y % 2 * 2 + core


def permute(block, target):
    route = [(i, device_at(*target(*coords(i)))) for i in range(256)]
    return lax.ppermute(block, AXES, route)


def to_core(x, y, z, c):
    return x, y, z, 1 - c


def to_y_mirror(x, y, z, c):
    return x, 3 - y, z, c


def to_y_pair(x, y, z, c):
    return x, y ^ 1, z, c


def to_y_far(x, y, z, c):
    return x, y + 2, z, c


def to_x_pair(x, y, z, c):
    return x ^ 1, y, z, c


def to_x_mirror(x, y, z, c):
    return 3 - x, y, z, c


def to_x_far(x, y, z, c):
    return x + 2, y, z, c


def to_xy_far(x, y, z, c):
    return x ^ 1, y + 2, z, c


def to_z_next(x, y, z, c):
    return x, y, z + 1, c


def act(linear_map, vectors):
    return lax.dot_general(
        vectors, linear_map, (((1,), (1,)), ((), ())), preferred_element_type=F32
    )


def act_add(linear_map, vectors, added):
    return (act(linear_map, vectors) + added.astype(F32)).astype(BF16)


def apply_t(transposed, vectors):
    return jnp.dot(vectors, transposed, preferred_element_type=F32)


def apply_t_add(transposed, vectors, added):
    return (apply_t(transposed, vectors) + added.astype(F32)).astype(BF16)


class Place:
    def __init__(self):
        guide, self.face = lax.axis_index("guide"), lax.axis_index("face")
        self.x, self.y_hi, self.y_lo = guide // 2 % 4, guide % 2, self.face // 2
        self.core = self.face % 2
        self.x_hi, self.x_lo = self.x // 2, self.x % 2
        self.strip = (self.x_lo + self.x_hi) % 2


def span(index, size=SIDE):
    return pl.ds(pl.multiple_of(index * size, size), size)


def block_of(ref, row, col):
    return ref.at[span(row), span(col)]


def send_kernel(own, out):
    place = Place()
    line = span((place.face + 2) % 4)

    @pl.when(place.y_hi == 1)
    def _():
        for t in range(4):
            out[t] = own[line, t * SIDE : (t + 1) * SIDE]

    @pl.when(place.y_hi == 0)
    def _():
        for t in range(4):
            out[t] = own[t * SIDE : (t + 1) * SIDE, line]


def send_line(own):
    return pl.pallas_call(
        send_kernel,
        in_specs=[VMEM],
        out_specs=VMEM,
        out_shape=jax.ShapeDtypeStruct((4, SIDE, SIDE), BF16),
        compiler_params=pltpu.CompilerParams(vmem_limit_bytes=8 * 1024 * 1024),
    )(own)


def small(**sizes):
    return dict(
        compiler_params=pltpu.CompilerParams(vmem_limit_bytes=12 * 1024 * 1024),
        cost_estimate=pl.CostEstimate(
            flops=sizes.get("flops", 0), bytes_accessed=1024**2, transcendentals=0
        ),
    )


def blocks(count):
    return jax.ShapeDtypeStruct((count, SIDE, SIDE), BF16)


def source_kernel(volume, leaf, out):
    out[...] = act(leaf[...], volume[...]).astype(BF16)


def to_source(leaf, volume):
    rows, depth = volume.shape
    return pl.pallas_call(
        source_kernel,
        grid=(leaf.shape[0] // SIDE,),
        in_specs=[
            pl.BlockSpec((rows, depth), lambda t: (0, 0)),
            pl.BlockSpec((SIDE, depth), lambda t: (t, 0)),
        ],
        out_specs=pl.BlockSpec((rows, SIDE), lambda t: (0, t)),
        out_shape=jax.ShapeDtypeStruct((rows, leaf.shape[0]), BF16),
        compiler_params=pltpu.CompilerParams(vmem_limit_bytes=56 * 1024 * 1024),
        cost_estimate=pl.CostEstimate(
            flops=2 * rows * depth * leaf.shape[0],
            bytes_accessed=2 * depth * (rows + leaf.shape[0]),
            transcendentals=0,
        ),
    )(volume, leaf)


def line_kernel(own, got, line):
    place = Place()

    @pl.when(place.y_hi == 0)
    def _():
        row = jnp.concatenate([got[t] for t in range(4)], axis=1)
        for t in range(4):
            cols = slice(t * SIDE, (t + 1) * SIDE)
            line[t] = jnp.dot(row, own[:, cols], preferred_element_type=F32).T.astype(BF16)

    @pl.when(place.y_hi == 1)
    def _():
        col = jnp.concatenate([got[t] for t in range(4)], axis=0)
        for t in range(4):
            rows = slice(t * SIDE, (t + 1) * SIDE)
            line[t] = jnp.dot(own[rows, :], col, preferred_element_type=F32).T.astype(BF16)


def pair_line(own, got):
    return pl.pallas_call(
        line_kernel,
        in_specs=[VMEM] * 2,
        out_specs=VMEM,
        out_shape=blocks(4),
        **small(flops=2 * SIDE * 1024**2),
    )(own, got)


def multiply(left, right):
    return jnp.dot(left[...], right[...], preferred_element_type=F32).astype(BF16)


def multiply_transposed(left, right, out):
    for t in range(4):
        cols = slice(t * SIDE, (t + 1) * SIDE)
        out[cols, :] = jnp.dot(left[...], right[:, cols], preferred_element_type=F32).T.astype(BF16)


def full_kernel(own, got, got_pair, core_got, core_pair, source, theirs, *outs):
    partner, full, mine, others = outs
    place = Place()
    quarters = ((0, got), (2, got_pair), (1, core_got), (3, core_pair))

    def line_of(flip):
        return (place.y_lo + flip // 2) % 2 * 2 + (place.core + flip) % 2

    half = source[pl.ds(pl.multiple_of(128 * place.y_hi, 128), 128), :]

    @pl.when(place.y_hi == 1)
    def _():
        for flip, ref in quarters:
            for t in range(4):
                partner[t * SIDE : (t + 1) * SIDE, span(line_of(flip))] = ref[t]
        multiply_transposed(own, partner, full)
        trace = act_add(own[...], theirs[...], half)
        mine[...] = trace[:64]
        others[...] = trace[64:]

    @pl.when(place.y_hi == 0)
    def _():
        for flip, ref in quarters:
            for t in range(4):
                partner[span(line_of(flip)), t * SIDE : (t + 1) * SIDE] = ref[t]
        multiply_transposed(partner, own, full)
        trace = act_add(partner[...], half, theirs[...])
        mine[...] = trace[:64]
        others[...] = trace[64:]

    @pl.when(place.strip == 1)
    def _():
        first, second = mine[...], others[...]
        mine[...] = second
        others[...] = first


def pair_map(*args):
    strip = jax.ShapeDtypeStruct((64, 1024), BF16)
    return pl.pallas_call(
        full_kernel,
        in_specs=[VMEM] * 7,
        out_specs=[VMEM] * 4,
        out_shape=[map_shape(), map_shape(), strip, strip],
        compiler_params=pltpu.CompilerParams(vmem_limit_bytes=16 * 1024 * 1024),
        cost_estimate=pl.CostEstimate(
            flops=2 * 1024**3, bytes_accessed=8 * 1024**2, transcendentals=0
        ),
    )(*args)


def pack_kernel(*refs):
    out, filled = refs[-1], 0
    for ref in refs[:-1]:
        size = min(ref.shape[0], 4)
        out[filled : filled + size] = ref[:size]
        filled += size


def pack(*arrays):
    return pl.pallas_call(
        pack_kernel,
        in_specs=[VMEM] * len(arrays),
        out_specs=VMEM,
        out_shape=blocks(sum(min(array.shape[0], 4) for array in arrays)),
        **small(),
    )(*arrays)


def gather_copies(place, target, lines, sems):
    copies = []
    upper = place.y_hi == 1
    for flip, line in zip((0, 2, 1, 3), lines):
        index = (place.y_lo + flip // 2) % 2 * 2 + (place.core + flip) % 2
        for t in range(4):
            row = jnp.where(upper, index, t)
            col = jnp.where(upper, t, index)
            copies.append(
                pltpu.make_async_copy(line.at[t], block_of(target, row, col), sems.at[len(copies)])
            )
    return copies


def map_shape(*lead):
    return jax.ShapeDtypeStruct((*lead, 1024, 1024), BF16)


def join_kernel(*refs):
    pair, pair_2, mirror, mirror_2, far, far_2, core = refs[:7]
    full, mine, beside, across, from_far = refs[7:12]
    pair_full, others, group_trace, other_trace, plane_trace, moving, sems = refs[12:]
    place = Place()
    mirror_slot = place.x_lo
    pair_lines = (pair, pair_2, core.at[0:4], core.at[8:12])
    mirror_lines = (mirror, mirror_2, core.at[4:8], core.at[12:16])
    far_lines = (far, far_2, core.at[16:20], core.at[20:24])
    pair_copies = gather_copies(place, pair_full, pair_lines, sems.at[0])
    other_copies = gather_copies(place, others.at[mirror_slot], mirror_lines, sems.at[1])
    other_copies += gather_copies(place, others.at[1 - mirror_slot], far_lines, sems.at[2])
    for copy in pair_copies + other_copies:
        copy.start()
    for copy in pair_copies:
        copy.wait()

    @pl.when(place.x_lo == 1)
    def _():
        group_trace[...] = apply_t_add(full[...], beside[...], mine[...])

    @pl.when(place.x_lo == 0)
    def _():
        group_trace[...] = apply_t_add(pair_full[...], mine[...], beside[...])

    for copy in other_copies:
        copy.wait()
    mirror_low = place.x_lo == 1
    low = jnp.where(mirror_low, across[...], from_far[...])
    high = jnp.where(mirror_low, from_far[...], across[...])
    other_trace[...] = apply_t_add(others[0], low, high)

    def through(upper, lower, low, high):
        inner = apply_t(lower[...], low[...]).astype(BF16)
        plane_trace[...] = apply_t_add(upper[...], inner, high[...])

    @pl.when(jnp.logical_and(place.x_hi == 1, place.x_lo == 1))
    def _():
        through(full, pair_full, other_trace, group_trace)

    @pl.when(jnp.logical_and(place.x_hi == 1, place.x_lo == 0))
    def _():
        through(pair_full, full, other_trace, group_trace)

    @pl.when(place.x_hi == 0)
    def _():
        through(others.at[0], others.at[1], group_trace, other_trace)

    moving[...] = jnp.where(place.x_hi == 1, group_trace[...], plane_trace[...])


def join(*args):
    strip = jax.ShapeDtypeStruct((64, 1024), BF16)
    return pl.pallas_call(
        join_kernel,
        in_specs=[ANY] * 7 + [VMEM] * 5,
        out_specs=[VMEM] * 6,
        out_shape=[map_shape(), map_shape(2), strip, strip, strip, strip],
        scratch_shapes=[pltpu.SemaphoreType.DMA((3, 16))],
        compiler_params=pltpu.CompilerParams(vmem_limit_bytes=18 * 1024 * 1024),
        cost_estimate=pl.CostEstimate(
            flops=8 * 64 * 1024**2, bytes_accessed=14 * 1024**2, transcendentals=0
        ),
    )(*args)


def plane_kernel(full, pair_full, others, other, plane, own):
    place = Place()

    @pl.when(place.x_lo == 1)
    def _():
        own[...] = multiply(pair_full, full)

    @pl.when(place.x_lo == 0)
    def _():
        own[...] = multiply(full, pair_full)

    other[...] = multiply(others.at[1], others.at[0])

    @pl.when(place.x_hi == 1)
    def _():
        plane[...] = multiply(other, own)

    @pl.when(place.x_hi == 0)
    def _():
        plane[...] = multiply(own, other)


def to_plane(*args):
    return pl.pallas_call(
        plane_kernel,
        in_specs=[VMEM] * 3,
        out_specs=[VMEM] * 2,
        out_shape=[map_shape()] * 2,
        scratch_shapes=[pltpu.VMEM((1024, 1024), BF16)],
        compiler_params=pltpu.CompilerParams(vmem_limit_bytes=18 * 1024 * 1024),
        cost_estimate=pl.CostEstimate(
            flops=6 * 1024**3, bytes_accessed=12 * 1024**2, transcendentals=0
        ),
    )(*args)


def lift_kernel(part_a, part_b, other_map, other_trace, full, pair_full, mine, beside, own, across):
    place = Place()
    own[0:32, :] = part_a[...]
    own[32:64, :] = part_b[...]

    @pl.when(place.x_hi == 1)
    def _():
        own[...] = apply_t_add(other_map[...], own[...], other_trace[...])

    @pl.when(place.x_lo == 1)
    def _():
        across[...] = own[...]
        own[...] = apply_t_add(pair_full[...], own[...], beside[...])

    @pl.when(place.x_lo == 0)
    def _():
        across[...] = apply_t_add(full[...], own[...], mine[...])


def lift(*args):
    strip = jax.ShapeDtypeStruct((64, 1024), BF16)
    return pl.pallas_call(
        lift_kernel,
        in_specs=[VMEM] * 8,
        out_specs=[VMEM] * 2,
        out_shape=[strip, strip],
        **small(flops=4 * 64 * 1024**2),
    )(*args)


def last_kernel(e00, e01, e10, e11, partner, late, theirs, out, held):
    place = Place()
    for part, (flip_y, flip_x) in ((e00, (0, 0)), (e01, (0, 1)), (e10, (1, 0)), (e11, (1, 1))):
        index = 2 * ((place.y_hi + flip_y) % 2) + (place.strip + flip_x) % 2
        held[span(index, 64), :] = part[...]

    @pl.when(place.y_hi == 0)
    def _():
        out[...] = held[...]

    @pl.when(place.y_hi == 1)
    def _():
        added = jnp.concatenate([late[...], theirs[...]], axis=0)
        out[...] = act_add(partner[...], held[...], added)


def last(*args):
    return pl.pallas_call(
        last_kernel,
        in_specs=[VMEM] * 7,
        out_specs=VMEM,
        out_shape=jax.ShapeDtypeStruct((256, 1024), BF16),
        scratch_shapes=[pltpu.VMEM((256, 1024), BF16)],
        **small(flops=2 * 256 * 1024**2),
    )(*args)


def together(*values):
    return lax.optimization_barrier(values)


def local(transfer, leaf_map, volume_source):
    place = Place()
    own_map = transfer[0]

    got = permute(send_line(own_map), to_y_mirror)
    source = to_source(leaf_map[0], volume_source[0])
    halves = source.reshape(2, 128, 1024)
    relay = permute(lax.dynamic_index_in_dim(halves, 1 - place.y_hi, 0, False), to_y_pair)
    got, relay = together(got, relay)
    line = pair_line(own_map, got)

    got_pair = permute(got, to_y_pair)
    pair = permute(line, to_x_pair)
    mirror = permute(line, to_x_mirror)
    theirs = permute(relay, to_y_mirror)
    core_got = permute(got, to_core)
    got_pair, theirs = together(got_pair, theirs)
    core_pair = permute(got_pair, to_core)
    line_2 = pair_line(own_map, got_pair)
    pair, mirror, theirs, core_got, core_pair, line_2 = together(
        pair, mirror, theirs, core_got, core_pair, line_2
    )

    pair_2 = permute(line_2, to_x_pair)
    mirror_2 = permute(line_2, to_x_mirror)
    far_a, far_b = permute(pair[:2], to_x_mirror), permute(mirror[2:], to_x_pair)
    partner, full, mine, others = pair_map(
        own_map, got, got_pair, core_got, core_pair, source, theirs
    )
    far_a, far_b, mine, others = together(far_a, far_b, mine, others)
    far = pack(far_a, far_b)
    far_2 = permute(far, to_y_pair)
    pair_2, mirror_2, far_2 = together(pair_2, mirror_2, far_2)
    beside = permute(together(others, far_2)[0], to_x_pair)
    across = permute(together(mine, far_2)[0], to_x_mirror)
    from_far = permute(together(others, far_2)[0], to_x_far)

    core = permute(pack(pair, mirror, pair_2, mirror_2, far, far_2), to_core)
    pair_full, other_maps, group_trace, other_trace, plane_trace, moving = join(
        pair, pair_2, mirror, mirror_2, far, far_2, core,
        full, mine, beside, across, from_far,
    )

    added = [plane_trace[:32], plane_trace[32:]]
    parts = [permute(part, to_z_next) for part in (moving[:32], moving[32:])]
    other_map, plane_map = to_plane(full, pair_full, other_maps)
    for turn in range(7):
        parts = [apply_t_add(plane_map, part, extra) for part, extra in zip(parts, added)]
        if turn == 1:
            late = lax.dynamic_index_in_dim(halves, place.y_hi, 0, False)
            late = permute(together(late, *parts)[0], to_y_far)
        parts = [permute(part, to_z_next) for part in parts]

    own, other = lift(*parts, other_map, other_trace, full, pair_full, mine, beside)
    pieces = (
        own,
        permute(other, to_x_pair),
        permute(own, to_y_far),
        permute(other, to_xy_far),
    )
    traces = last(*pieces, partner, late, theirs)
    return traces[None]


def solution(mesh):
    in_specs = (P("guide", None, None), P("guide", None, None), P("guide", "face", None))
    out_specs = P("guide", "face", None)
    return jax.shard_map(local, mesh=mesh, in_specs=in_specs, out_specs=out_specs, check_vma=False)
```

```python
import functools

import jax
import jax.numpy as jnp
from jax import lax
from jax.experimental import pallas as pl
from jax.experimental.pallas import tpu as pltpu
from jax.sharding import PartitionSpec as P

AXES = ("guide", "face")
BF16, F32 = jnp.bfloat16, jnp.float32
SIDE = 256
ANY = pl.BlockSpec(memory_space=pl.ANY)
VMEM = pl.BlockSpec(memory_space=pltpu.VMEM)


def coords(device):
    guide, face = divmod(device, 4)
    return guide // 2 % 4, guide % 2 * 2 + face // 2, guide // 8, face % 2


def device_at(x, y, z, core):
    x, y, z = x % 4, y % 4, z % 8
    return (z * 8 + x * 2 + y // 2) * 4 + y % 2 * 2 + core


def permute(block, target):
    route = [(i, device_at(*target(*coords(i)))) for i in range(256)]
    return lax.ppermute(block, AXES, route)


def to_core(x, y, z, c):
    return x, y, z, 1 - c


def to_y_mirror(x, y, z, c):
    return x, 3 - y, z, c


def to_y_pair(x, y, z, c):
    return x, y ^ 1, z, c


def to_y_far(x, y, z, c):
    return x, y + 2, z, c


def to_x_pair(x, y, z, c):
    return x ^ 1, y, z, c


def to_x_mirror(x, y, z, c):
    return 3 - x, y, z, c


def to_xy_far(x, y, z, c):
    return x ^ 1, y + 2, z, c


def to_z_next(x, y, z, c):
    return x, y, z + 1, c


def act(linear_map, vectors):
    return lax.dot_general(
        vectors, linear_map, (((1,), (1,)), ((), ())), preferred_element_type=F32
    )


def act_add(linear_map, vectors, added):
    return (act(linear_map, vectors) + added.astype(F32)).astype(BF16)


def apply_t(transposed, vectors):
    return jnp.dot(vectors, transposed, preferred_element_type=F32)


def apply_t_add(transposed, vectors, added):
    return (apply_t(transposed, vectors) + added.astype(F32)).astype(BF16)


class Place:
    def __init__(self):
        guide, self.face = lax.axis_index("guide"), lax.axis_index("face")
        self.x, self.y_hi, self.y_lo = guide // 2 % 4, guide % 2, self.face // 2
        self.core = self.face % 2
        self.x_hi, self.x_lo = self.x // 2, self.x % 2
        self.strip = (self.x_lo + self.x_hi) % 2


def span(index, size=SIDE):
    return pl.ds(pl.multiple_of(index * size, size), size)


def block_of(ref, row, col):
    return ref.at[span(row), span(col)]


def send_kernel(own, out):
    place = Place()
    line = span((place.face + 2) % 4)

    @pl.when(place.y_hi == 1)
    def _():
        for t in range(4):
            out[t] = own[line, t * SIDE : (t + 1) * SIDE]

    @pl.when(place.y_hi == 0)
    def _():
        for t in range(4):
            out[t] = own[t * SIDE : (t + 1) * SIDE, line]


def send_line(own):
    return pl.pallas_call(
        send_kernel,
        in_specs=[VMEM],
        out_specs=VMEM,
        out_shape=jax.ShapeDtypeStruct((4, SIDE, SIDE), BF16),
        compiler_params=pltpu.CompilerParams(vmem_limit_bytes=8 * 1024 * 1024),
    )(own)


def small(**sizes):
    return dict(
        compiler_params=pltpu.CompilerParams(vmem_limit_bytes=12 * 1024 * 1024),
        cost_estimate=pl.CostEstimate(
            flops=sizes.get("flops", 0), bytes_accessed=1024**2, transcendentals=0
        ),
    )


def blocks(count):
    return jax.ShapeDtypeStruct((count, SIDE, SIDE), BF16)


SOURCE_CHUNK = 64


def source_kernel(volume, leaf, keep, send, volume_held, leaf_held, sems):
    place = Place()
    pieces = []
    for ref, held in ((volume, volume_held), (leaf, leaf_held)):
        for start in range(0, ref.shape[0], SOURCE_CHUNK):
            rows = pl.ds(start, SOURCE_CHUNK)
            pieces.append(pltpu.make_async_copy(ref.at[rows], held.at[rows], sems.at[len(pieces)]))
    for piece in pieces:
        piece.start()
    leading = volume.shape[0] // SOURCE_CHUNK
    for piece in pieces[:leading]:
        piece.wait()
    per_tile = SIDE // SOURCE_CHUNK
    for t in range(leaf.shape[0] // SIDE):
        for piece in pieces[leading + t * per_tile : leading + (t + 1) * per_tile]:
            piece.wait()
        cols = slice(t * SIDE, (t + 1) * SIDE)
        tile = act(leaf_held[cols, :], volume_held[...]).astype(BF16)
        for half in range(2):

            @pl.when(place.y_hi == half)
            def _():
                keep[:, cols] = tile[128 * half : 128 * half + 128]
                send[:, cols] = tile[128 * (1 - half) : 128 * (1 - half) + 128]


def to_source(leaf, volume):
    rows, depth = volume.shape
    half = jax.ShapeDtypeStruct((rows // 2, leaf.shape[0]), BF16)
    return pl.pallas_call(
        source_kernel,
        in_specs=[ANY] * 2,
        out_specs=[VMEM] * 2,
        out_shape=[half, half],
        scratch_shapes=[
            pltpu.VMEM(volume.shape, BF16),
            pltpu.VMEM(leaf.shape, BF16),
            pltpu.SemaphoreType.DMA(((rows + leaf.shape[0]) // SOURCE_CHUNK,)),
        ],
        compiler_params=pltpu.CompilerParams(vmem_limit_bytes=56 * 1024 * 1024),
        cost_estimate=pl.CostEstimate(
            flops=2 * rows * depth * leaf.shape[0],
            bytes_accessed=2 * depth * (rows + leaf.shape[0]),
            transcendentals=0,
        ),
    )(volume, leaf)


def line_kernel(own, got, line):
    place = Place()

    @pl.when(place.y_hi == 0)
    def _():
        row = jnp.concatenate([got[t] for t in range(4)], axis=1)
        for t in range(4):
            cols = slice(t * SIDE, (t + 1) * SIDE)
            line[t] = jnp.dot(row, own[:, cols], preferred_element_type=F32).T.astype(BF16)

    @pl.when(place.y_hi == 1)
    def _():
        col = jnp.concatenate([got[t] for t in range(4)], axis=0)
        for t in range(4):
            rows = slice(t * SIDE, (t + 1) * SIDE)
            line[t] = jnp.dot(own[rows, :], col, preferred_element_type=F32).T.astype(BF16)


def pair_line(own, got):
    return pl.pallas_call(
        line_kernel,
        in_specs=[VMEM] * 2,
        out_specs=VMEM,
        out_shape=blocks(4),
        **small(flops=2 * SIDE * 1024**2),
    )(own, got)


def multiply(left, right):
    return jnp.dot(left[...], right[...], preferred_element_type=F32).astype(BF16)


def multiply_transposed(left, right, out):
    for t in range(4):
        cols = slice(t * SIDE, (t + 1) * SIDE)
        out[cols, :] = jnp.dot(left[...], right[:, cols], preferred_element_type=F32).T.astype(BF16)


def full_kernel(own, got, got_pair, core_got, core_pair, half, theirs, *outs):
    partner, full, mine, others = outs
    place = Place()
    quarters = ((0, got), (2, got_pair), (1, core_got), (3, core_pair))

    def line_of(flip):
        return (place.y_lo + flip // 2) % 2 * 2 + (place.core + flip) % 2

    @pl.when(place.y_hi == 1)
    def _():
        for flip, ref in quarters:
            for t in range(4):
                partner[t * SIDE : (t + 1) * SIDE, span(line_of(flip))] = ref[t]
        multiply_transposed(own, partner, full)
        trace = act_add(own[...], theirs[...], half[...])
        mine[...] = trace[:64]
        others[...] = trace[64:]

    @pl.when(place.y_hi == 0)
    def _():
        for flip, ref in quarters:
            for t in range(4):
                partner[span(line_of(flip)), t * SIDE : (t + 1) * SIDE] = ref[t]
        multiply_transposed(partner, own, full)
        trace = act_add(partner[...], half[...], theirs[...])
        mine[...] = trace[:64]
        others[...] = trace[64:]

    @pl.when(place.strip == 1)
    def _():
        first, second = mine[...], others[...]
        mine[...] = second
        others[...] = first


def pair_map(*args):
    strip = jax.ShapeDtypeStruct((64, 1024), BF16)
    return pl.pallas_call(
        full_kernel,
        in_specs=[VMEM] * 7,
        out_specs=[VMEM] * 4,
        out_shape=[map_shape(), map_shape(), strip, strip],
        compiler_params=pltpu.CompilerParams(vmem_limit_bytes=16 * 1024 * 1024),
        cost_estimate=pl.CostEstimate(
            flops=2 * 1024**3, bytes_accessed=8 * 1024**2, transcendentals=0
        ),
    )(*args)


def pack_kernel(*refs):
    out, filled = refs[-1], 0
    for ref in refs[:-1]:
        size = min(ref.shape[0], 4)
        out[filled : filled + size] = ref[:size]
        filled += size


def pack(*arrays):
    return pl.pallas_call(
        pack_kernel,
        in_specs=[VMEM] * len(arrays),
        out_specs=VMEM,
        out_shape=blocks(sum(min(array.shape[0], 4) for array in arrays)),
        **small(),
    )(*arrays)


def gather_copies(place, target, lines, sems):
    copies = []
    upper = place.y_hi == 1
    for flip, line in zip((0, 2, 1, 3), lines):
        index = (place.y_lo + flip // 2) % 2 * 2 + (place.core + flip) % 2
        for t in range(4):
            row = jnp.where(upper, index, t)
            col = jnp.where(upper, t, index)
            copies.append(
                pltpu.make_async_copy(line.at[t], block_of(target, row, col), sems.at[len(copies)])
            )
    return copies


def map_shape(*lead):
    return jax.ShapeDtypeStruct((*lead, 1024, 1024), BF16)


def join_kernel(*refs):
    pair, pair_2, mirror, mirror_2, far, far_2, core = refs[:7]
    full, mine, beside, across, from_far = refs[7:12]
    pair_full, others, group_trace, other_trace, plane_trace, moving, sems = refs[12:]
    place = Place()
    mirror_slot = place.x_lo
    pair_lines = (pair, pair_2, core.at[0:4], core.at[8:12])
    mirror_lines = (mirror, mirror_2, core.at[4:8], core.at[12:16])
    far_lines = (far, far_2, core.at[16:20], core.at[20:24])
    pair_copies = gather_copies(place, pair_full, pair_lines, sems.at[0])
    other_copies = gather_copies(place, others.at[mirror_slot], mirror_lines, sems.at[1])
    other_copies += gather_copies(place, others.at[1 - mirror_slot], far_lines, sems.at[2])
    for copy in pair_copies + other_copies:
        copy.start()
    for copy in pair_copies:
        copy.wait()

    @pl.when(place.x_lo == 1)
    def _():
        group_trace[...] = apply_t_add(full[...], beside[...], mine[...])

    @pl.when(place.x_lo == 0)
    def _():
        group_trace[...] = apply_t_add(pair_full[...], mine[...], beside[...])

    for copy in other_copies:
        copy.wait()
    mirror_low = place.x_lo == 1
    low = jnp.where(mirror_low, across[...], from_far[...])
    high = jnp.where(mirror_low, from_far[...], across[...])
    other_trace[...] = apply_t_add(others[0], low, high)

    def through(upper, lower, low, high):
        inner = apply_t(lower[...], low[...]).astype(BF16)
        plane_trace[...] = apply_t_add(upper[...], inner, high[...])

    @pl.when(jnp.logical_and(place.x_hi == 1, place.x_lo == 1))
    def _():
        through(full, pair_full, other_trace, group_trace)

    @pl.when(jnp.logical_and(place.x_hi == 1, place.x_lo == 0))
    def _():
        through(pair_full, full, other_trace, group_trace)

    @pl.when(place.x_hi == 0)
    def _():
        through(others.at[0], others.at[1], group_trace, other_trace)

    moving[...] = jnp.where(place.x_hi == 1, group_trace[...], plane_trace[...])


def join(*args):
    strip = jax.ShapeDtypeStruct((64, 1024), BF16)
    return pl.pallas_call(
        join_kernel,
        in_specs=[ANY] * 7 + [VMEM] * 5,
        out_specs=[VMEM] * 6,
        out_shape=[map_shape(), map_shape(2), strip, strip, strip, strip],
        scratch_shapes=[pltpu.SemaphoreType.DMA((3, 16))],
        compiler_params=pltpu.CompilerParams(vmem_limit_bytes=18 * 1024 * 1024),
        cost_estimate=pl.CostEstimate(
            flops=8 * 64 * 1024**2, bytes_accessed=14 * 1024**2, transcendentals=0
        ),
    )(*args)


def plane_kernel(full, pair_full, others, other, plane, own):
    place = Place()

    @pl.when(place.x_lo == 1)
    def _():
        own[...] = multiply(pair_full, full)

    @pl.when(place.x_lo == 0)
    def _():
        own[...] = multiply(full, pair_full)

    other[...] = multiply(others.at[1], others.at[0])

    @pl.when(place.x_hi == 1)
    def _():
        plane[...] = multiply(other, own)

    @pl.when(place.x_hi == 0)
    def _():
        plane[...] = multiply(own, other)


def to_plane(*args):
    return pl.pallas_call(
        plane_kernel,
        in_specs=[VMEM] * 3,
        out_specs=[VMEM] * 2,
        out_shape=[map_shape()] * 2,
        scratch_shapes=[pltpu.VMEM((1024, 1024), BF16)],
        compiler_params=pltpu.CompilerParams(vmem_limit_bytes=18 * 1024 * 1024),
        cost_estimate=pl.CostEstimate(
            flops=6 * 1024**3, bytes_accessed=12 * 1024**2, transcendentals=0
        ),
    )(*args)


def lift_kernel(part_a, part_b, other_map, other_trace, full, pair_full, mine, beside, own, across):
    place = Place()
    own[0:32, :] = part_a[...]
    own[32:64, :] = part_b[...]

    @pl.when(place.x_hi == 1)
    def _():
        own[...] = apply_t_add(other_map[...], own[...], other_trace[...])

    @pl.when(place.x_lo == 1)
    def _():
        across[...] = own[...]
        own[...] = apply_t_add(pair_full[...], own[...], beside[...])

    @pl.when(place.x_lo == 0)
    def _():
        across[...] = apply_t_add(full[...], own[...], mine[...])


def lift(*args):
    strip = jax.ShapeDtypeStruct((64, 1024), BF16)
    return pl.pallas_call(
        lift_kernel,
        in_specs=[VMEM] * 8,
        out_specs=[VMEM] * 2,
        out_shape=[strip, strip],
        **small(flops=4 * 64 * 1024**2),
    )(*args)


def last_kernel(e00, e01, e10, e11, partner, late, theirs, out, held):
    place = Place()
    for part, (flip_y, flip_x) in ((e00, (0, 0)), (e01, (0, 1)), (e10, (1, 0)), (e11, (1, 1))):
        index = 2 * ((place.y_hi + flip_y) % 2) + (place.strip + flip_x) % 2
        held[span(index, 64), :] = part[...]

    @pl.when(place.y_hi == 0)
    def _():
        out[...] = held[...]

    @pl.when(place.y_hi == 1)
    def _():
        added = jnp.concatenate([late[...], theirs[...]], axis=0)
        out[...] = act_add(partner[...], held[...], added)


def last(*args):
    return pl.pallas_call(
        last_kernel,
        in_specs=[VMEM] * 7,
        out_specs=VMEM,
        out_shape=jax.ShapeDtypeStruct((256, 1024), BF16),
        scratch_shapes=[pltpu.VMEM((256, 1024), BF16)],
        **small(flops=2 * 256 * 1024**2),
    )(*args)


def together(*values):
    return lax.optimization_barrier(values)


def local(transfer, leaf_map, volume_source):
    place = Place()
    own_map = transfer[0]

    got = permute(send_line(own_map), to_y_mirror)
    source, source_out = to_source(leaf_map[0], volume_source[0])
    relay = permute(source_out, to_y_pair)
    got, relay = together(got, relay)
    line = pair_line(own_map, got)

    got_pair = permute(got, to_y_pair)
    pair = permute(line, to_x_pair)
    mirror = permute(line, to_x_mirror)
    theirs = permute(relay, to_y_mirror)
    core_got = permute(got, to_core)
    got_pair, theirs = together(got_pair, theirs)
    core_pair = permute(got_pair, to_core)
    line_2 = pair_line(own_map, got_pair)
    pair, mirror, theirs, core_got, core_pair, line_2 = together(
        pair, mirror, theirs, core_got, core_pair, line_2
    )

    pair_2 = permute(line_2, to_x_pair)
    mirror_2 = permute(line_2, to_x_mirror)
    far_a, far_b = permute(pair[:2], to_x_mirror), permute(mirror[2:], to_x_pair)
    partner, full, mine, others = pair_map(
        own_map, got, got_pair, core_got, core_pair, source, theirs
    )
    late = permute(source, to_y_far)
    far_a, far_b, mine, others, late = together(far_a, far_b, mine, others, late)
    far = pack(far_a, far_b)
    far_2 = permute(far, to_y_pair)
    beside = permute(others, to_x_pair)
    across = permute(mine, to_x_mirror)
    pair_2, mirror_2, far_2, beside, across = together(pair_2, mirror_2, far_2, beside, across)
    from_far = permute(beside, to_x_mirror)

    core = permute(pack(pair, mirror, pair_2, mirror_2, far, far_2), to_core)
    pair_full, other_maps, group_trace, other_trace, plane_trace, moving = join(
        pair, pair_2, mirror, mirror_2, far, far_2, core,
        full, mine, beside, across, from_far,
    )

    added = [plane_trace[:32], plane_trace[32:]]
    parts = [permute(part, to_z_next) for part in (moving[:32], moving[32:])]
    other_map, plane_map = to_plane(full, pair_full, other_maps)
    for _ in range(7):
        parts = [apply_t_add(plane_map, part, extra) for part, extra in zip(parts, added)]
        parts = [permute(part, to_z_next) for part in parts]

    own, other = lift(*parts, other_map, other_trace, full, pair_full, mine, beside)
    pieces = (
        own,
        permute(other, to_x_pair),
        permute(own, to_y_far),
        permute(other, to_xy_far),
    )
    traces = last(*pieces, partner, late, theirs)
    return traces[None]


def solution(mesh):
    in_specs = (P("guide", None, None), P("guide", None, None), P("guide", "face", None))
    out_specs = P("guide", "face", None)
    return jax.shard_map(local, mesh=mesh, in_specs=in_specs, out_specs=out_specs, check_vma=False)
```

```python
import functools

import jax
import jax.numpy as jnp
from jax import lax
from jax.experimental import pallas as pl
from jax.experimental.pallas import tpu as pltpu
from jax.sharding import PartitionSpec as P

AXES = ("guide", "face")
BF16, F32 = jnp.bfloat16, jnp.float32
SIDE = 256
ANY = pl.BlockSpec(memory_space=pl.ANY)
VMEM = pl.BlockSpec(memory_space=pltpu.VMEM)


def coords(device):
    guide, face = divmod(device, 4)
    return guide // 2 % 4, guide % 2 * 2 + face // 2, guide // 8, face % 2


def device_at(x, y, z, core):
    x, y, z = x % 4, y % 4, z % 8
    return (z * 8 + x * 2 + y // 2) * 4 + y % 2 * 2 + core


def permute(block, target):
    route = [(i, device_at(*target(*coords(i)))) for i in range(256)]
    return lax.ppermute(block, AXES, route)


def to_core(x, y, z, c):
    return x, y, z, 1 - c


def to_y_mirror(x, y, z, c):
    return x, 3 - y, z, c


def to_y_pair(x, y, z, c):
    return x, y ^ 1, z, c


def to_y_far(x, y, z, c):
    return x, y + 2, z, c


def to_x_pair(x, y, z, c):
    return x ^ 1, y, z, c


def to_x_mirror(x, y, z, c):
    return 3 - x, y, z, c


def to_xy_far(x, y, z, c):
    return x ^ 1, y + 2, z, c


def to_z_next(x, y, z, c):
    return x, y, z + 1, c


def act(linear_map, vectors):
    return lax.dot_general(
        vectors, linear_map, (((1,), (1,)), ((), ())), preferred_element_type=F32
    )


def act_add(linear_map, vectors, added):
    return (act(linear_map, vectors) + added.astype(F32)).astype(BF16)


def apply_t(transposed, vectors):
    return jnp.dot(vectors, transposed, preferred_element_type=F32)


def apply_t_add(transposed, vectors, added):
    return (apply_t(transposed, vectors) + added.astype(F32)).astype(BF16)


class Place:
    def __init__(self):
        guide, self.face = lax.axis_index("guide"), lax.axis_index("face")
        self.x, self.y_hi, self.y_lo = guide // 2 % 4, guide % 2, self.face // 2
        self.core = self.face % 2
        self.x_hi, self.x_lo = self.x // 2, self.x % 2
        self.strip = (self.x_lo + self.x_hi) % 2


def span(index, size=SIDE):
    return pl.ds(pl.multiple_of(index * size, size), size)


def block_of(ref, row, col):
    return ref.at[span(row), span(col)]


def send_kernel(own, out):
    place = Place()
    line = span((place.face + 2) % 4)

    @pl.when(place.y_hi == 1)
    def _():
        for t in range(4):
            out[t] = own[line, t * SIDE : (t + 1) * SIDE]

    @pl.when(place.y_hi == 0)
    def _():
        for t in range(4):
            out[t] = own[t * SIDE : (t + 1) * SIDE, line]


def send_line(own):
    return pl.pallas_call(
        send_kernel,
        in_specs=[VMEM],
        out_specs=VMEM,
        out_shape=jax.ShapeDtypeStruct((4, SIDE, SIDE), BF16),
        compiler_params=pltpu.CompilerParams(vmem_limit_bytes=8 * 1024 * 1024),
    )(own)


def small(**sizes):
    return dict(
        compiler_params=pltpu.CompilerParams(vmem_limit_bytes=12 * 1024 * 1024),
        cost_estimate=pl.CostEstimate(
            flops=sizes.get("flops", 0), bytes_accessed=1024**2, transcendentals=0
        ),
    )


def blocks(count):
    return jax.ShapeDtypeStruct((count, SIDE, SIDE), BF16)


SOURCE_CHUNK = 64


def source_kernel(volume, leaf, keep, send, volume_held, leaf_held, sems):
    place = Place()
    pieces = []
    for ref, held in ((volume, volume_held), (leaf, leaf_held)):
        for start in range(0, ref.shape[0], SOURCE_CHUNK):
            rows = pl.ds(start, SOURCE_CHUNK)
            pieces.append(pltpu.make_async_copy(ref.at[rows], held.at[rows], sems.at[len(pieces)]))
    for piece in pieces:
        piece.start()
    leading = volume.shape[0] // SOURCE_CHUNK
    for piece in pieces[:leading]:
        piece.wait()
    per_tile = SIDE // SOURCE_CHUNK
    for t in range(leaf.shape[0] // SIDE):
        for piece in pieces[leading + t * per_tile : leading + (t + 1) * per_tile]:
            piece.wait()
        cols = slice(t * SIDE, (t + 1) * SIDE)
        tile = act(leaf_held[cols, :], volume_held[...]).astype(BF16)
        for half in range(2):

            @pl.when(place.y_hi == half)
            def _():
                keep[:, cols] = tile[128 * half : 128 * half + 128]
                send[:, cols] = tile[128 * (1 - half) : 128 * (1 - half) + 128]


def to_source(leaf, volume):
    rows, depth = volume.shape
    half = jax.ShapeDtypeStruct((rows // 2, leaf.shape[0]), BF16)
    return pl.pallas_call(
        source_kernel,
        in_specs=[ANY] * 2,
        out_specs=[VMEM] * 2,
        out_shape=[half, half],
        scratch_shapes=[
            pltpu.VMEM(volume.shape, BF16),
            pltpu.VMEM(leaf.shape, BF16),
            pltpu.SemaphoreType.DMA(((rows + leaf.shape[0]) // SOURCE_CHUNK,)),
        ],
        compiler_params=pltpu.CompilerParams(vmem_limit_bytes=56 * 1024 * 1024),
        cost_estimate=pl.CostEstimate(
            flops=2 * rows * depth * leaf.shape[0],
            bytes_accessed=2 * depth * (rows + leaf.shape[0]),
            transcendentals=0,
        ),
    )(volume, leaf)


def line_kernel(own, got, line):
    place = Place()

    @pl.when(place.y_hi == 0)
    def _():
        row = jnp.concatenate([got[t] for t in range(4)], axis=1)
        for t in range(4):
            cols = slice(t * SIDE, (t + 1) * SIDE)
            line[t] = jnp.dot(row, own[:, cols], preferred_element_type=F32).T.astype(BF16)

    @pl.when(place.y_hi == 1)
    def _():
        col = jnp.concatenate([got[t] for t in range(4)], axis=0)
        for t in range(4):
            rows = slice(t * SIDE, (t + 1) * SIDE)
            line[t] = jnp.dot(own[rows, :], col, preferred_element_type=F32).T.astype(BF16)


def pair_line(own, got):
    return pl.pallas_call(
        line_kernel,
        in_specs=[VMEM] * 2,
        out_specs=VMEM,
        out_shape=blocks(4),
        **small(flops=2 * SIDE * 1024**2),
    )(own, got)


def multiply(left, right):
    return jnp.dot(left[...], right[...], preferred_element_type=F32).astype(BF16)


def multiply_transposed(left, right, out):
    for t in range(4):
        cols = slice(t * SIDE, (t + 1) * SIDE)
        out[cols, :] = jnp.dot(left[...], right[:, cols], preferred_element_type=F32).T.astype(BF16)


def full_kernel(own, got, got_pair, core_got, core_pair, half, theirs, *outs):
    partner, full, mine, others = outs
    place = Place()
    quarters = ((0, got), (2, got_pair), (1, core_got), (3, core_pair))

    def line_of(flip):
        return (place.y_lo + flip // 2) % 2 * 2 + (place.core + flip) % 2

    @pl.when(place.y_hi == 1)
    def _():
        for flip, ref in quarters:
            for t in range(4):
                partner[t * SIDE : (t + 1) * SIDE, span(line_of(flip))] = ref[t]
        multiply_transposed(own, partner, full)
        trace = act_add(own[...], theirs[...], half[...])
        mine[...] = trace[:64]
        others[...] = trace[64:]

    @pl.when(place.y_hi == 0)
    def _():
        for flip, ref in quarters:
            for t in range(4):
                partner[span(line_of(flip)), t * SIDE : (t + 1) * SIDE] = ref[t]
        multiply_transposed(partner, own, full)
        trace = act_add(partner[...], half[...], theirs[...])
        mine[...] = trace[:64]
        others[...] = trace[64:]

    @pl.when(place.strip == 1)
    def _():
        first, second = mine[...], others[...]
        mine[...] = second
        others[...] = first


def pair_map(*args):
    strip = jax.ShapeDtypeStruct((64, 1024), BF16)
    return pl.pallas_call(
        full_kernel,
        in_specs=[VMEM] * 7,
        out_specs=[VMEM] * 4,
        out_shape=[map_shape(), map_shape(), strip, strip],
        compiler_params=pltpu.CompilerParams(vmem_limit_bytes=16 * 1024 * 1024),
        cost_estimate=pl.CostEstimate(
            flops=2 * 1024**3, bytes_accessed=8 * 1024**2, transcendentals=0
        ),
    )(*args)


def pack_kernel(*refs):
    out, filled = refs[-1], 0
    for ref in refs[:-1]:
        size = min(ref.shape[0], 4)
        out[filled : filled + size] = ref[:size]
        filled += size


def pack(*arrays):
    return pl.pallas_call(
        pack_kernel,
        in_specs=[VMEM] * len(arrays),
        out_specs=VMEM,
        out_shape=blocks(sum(min(array.shape[0], 4) for array in arrays)),
        **small(),
    )(*arrays)


def gather_copies(place, target, lines, sems):
    copies = []
    upper = place.y_hi == 1
    for flip, line in zip((0, 2, 1, 3), lines):
        index = (place.y_lo + flip // 2) % 2 * 2 + (place.core + flip) % 2
        for t in range(4):
            row = jnp.where(upper, index, t)
            col = jnp.where(upper, t, index)
            copies.append(
                pltpu.make_async_copy(line.at[t], block_of(target, row, col), sems.at[len(copies)])
            )
    return copies


def map_shape(*lead):
    return jax.ShapeDtypeStruct((*lead, 1024, 1024), BF16)


def join_kernel(*refs):
    pair, pair_2, mirror, mirror_2, far, far_2, core = refs[:7]
    full, mine, beside, across, from_far = refs[7:12]
    pair_full, others, group_trace, other_trace, plane_trace, moving, sems = refs[12:]
    place = Place()
    mirror_slot = place.x_lo
    pair_lines = (pair, pair_2, core.at[0:4], core.at[8:12])
    mirror_lines = (mirror, mirror_2, core.at[4:8], core.at[12:16])
    far_lines = (far, far_2, core.at[16:20], core.at[20:24])
    pair_copies = gather_copies(place, pair_full, pair_lines, sems.at[0])
    other_copies = gather_copies(place, others.at[mirror_slot], mirror_lines, sems.at[1])
    other_copies += gather_copies(place, others.at[1 - mirror_slot], far_lines, sems.at[2])
    for copy in pair_copies + other_copies:
        copy.start()
    for copy in pair_copies:
        copy.wait()

    @pl.when(place.x_lo == 1)
    def _():
        group_trace[...] = apply_t_add(full[...], beside[...], mine[...])

    @pl.when(place.x_lo == 0)
    def _():
        group_trace[...] = apply_t_add(pair_full[...], mine[...], beside[...])

    for copy in other_copies:
        copy.wait()
    mirror_low = place.x_lo == 1
    low = jnp.where(mirror_low, across[...], from_far[...])
    high = jnp.where(mirror_low, from_far[...], across[...])
    other_trace[...] = apply_t_add(others[0], low, high)

    def through(upper, lower, low, high):
        inner = apply_t(lower[...], low[...]).astype(BF16)
        plane_trace[...] = apply_t_add(upper[...], inner, high[...])

    @pl.when(jnp.logical_and(place.x_hi == 1, place.x_lo == 1))
    def _():
        through(full, pair_full, other_trace, group_trace)

    @pl.when(jnp.logical_and(place.x_hi == 1, place.x_lo == 0))
    def _():
        through(pair_full, full, other_trace, group_trace)

    @pl.when(place.x_hi == 0)
    def _():
        through(others.at[0], others.at[1], group_trace, other_trace)

    moving[...] = jnp.where(place.x_hi == 1, group_trace[...], plane_trace[...])


def join(*args):
    strip = jax.ShapeDtypeStruct((64, 1024), BF16)
    return pl.pallas_call(
        join_kernel,
        in_specs=[ANY] * 7 + [VMEM] * 5,
        out_specs=[VMEM] * 6,
        out_shape=[map_shape(), map_shape(2), strip, strip, strip, strip],
        scratch_shapes=[pltpu.SemaphoreType.DMA((3, 16))],
        compiler_params=pltpu.CompilerParams(vmem_limit_bytes=18 * 1024 * 1024),
        cost_estimate=pl.CostEstimate(
            flops=8 * 64 * 1024**2, bytes_accessed=14 * 1024**2, transcendentals=0
        ),
    )(*args)


def plane_kernel(full, pair_full, others, other, plane, own):
    place = Place()

    @pl.when(place.x_lo == 1)
    def _():
        own[...] = multiply(pair_full, full)

    @pl.when(place.x_lo == 0)
    def _():
        own[...] = multiply(full, pair_full)

    other[...] = multiply(others.at[1], others.at[0])

    @pl.when(place.x_hi == 1)
    def _():
        plane[...] = multiply(other, own)

    @pl.when(place.x_hi == 0)
    def _():
        plane[...] = multiply(own, other)


def to_plane(*args):
    return pl.pallas_call(
        plane_kernel,
        in_specs=[VMEM] * 3,
        out_specs=[VMEM] * 2,
        out_shape=[map_shape()] * 2,
        scratch_shapes=[pltpu.VMEM((1024, 1024), BF16)],
        compiler_params=pltpu.CompilerParams(vmem_limit_bytes=18 * 1024 * 1024),
        cost_estimate=pl.CostEstimate(
            flops=6 * 1024**3, bytes_accessed=12 * 1024**2, transcendentals=0
        ),
    )(*args)


def lift_kernel(part_a, part_b, other_map, other_trace, full, pair_full, mine, beside, own, across):
    place = Place()
    own[0:32, :] = part_a[...]
    own[32:64, :] = part_b[...]

    @pl.when(place.x_hi == 1)
    def _():
        own[...] = apply_t_add(other_map[...], own[...], other_trace[...])

    @pl.when(place.x_lo == 1)
    def _():
        across[...] = own[...]
        own[...] = apply_t_add(pair_full[...], own[...], beside[...])

    @pl.when(place.x_lo == 0)
    def _():
        across[...] = apply_t_add(full[...], own[...], mine[...])


def lift(*args):
    strip = jax.ShapeDtypeStruct((64, 1024), BF16)
    return pl.pallas_call(
        lift_kernel,
        in_specs=[VMEM] * 8,
        out_specs=[VMEM] * 2,
        out_shape=[strip, strip],
        **small(flops=4 * 64 * 1024**2),
    )(*args)


def last_kernel(e00, e01, e10, e11, partner, late, theirs, out, held):
    place = Place()
    for part, (flip_y, flip_x) in ((e00, (0, 0)), (e01, (0, 1)), (e10, (1, 0)), (e11, (1, 1))):
        index = 2 * ((place.y_hi + flip_y) % 2) + (place.strip + flip_x) % 2
        held[span(index, 64), :] = part[...]

    @pl.when(place.y_hi == 0)
    def _():
        out[...] = held[...]

    @pl.when(place.y_hi == 1)
    def _():
        added = jnp.concatenate([late[...], theirs[...]], axis=0)
        out[...] = act_add(partner[...], held[...], added)


def last(*args):
    return pl.pallas_call(
        last_kernel,
        in_specs=[VMEM] * 7,
        out_specs=VMEM,
        out_shape=jax.ShapeDtypeStruct((256, 1024), BF16),
        scratch_shapes=[pltpu.VMEM((256, 1024), BF16)],
        **small(flops=2 * 256 * 1024**2),
    )(*args)


def together(*values):
    return lax.optimization_barrier(values)


def local(transfer, leaf_map, volume_source):
    place = Place()
    own_map = transfer[0]

    got = permute(send_line(own_map), to_y_mirror)
    source, source_out = to_source(leaf_map[0], volume_source[0])
    got, source_out = together(got, source_out)
    line = pair_line(own_map, got)

    got_pair = permute(got, to_y_pair)
    pair = permute(line, to_x_pair)
    mirror = permute(line, to_x_mirror)
    theirs = permute(permute(source_out, to_y_pair), to_y_mirror)
    core_got = permute(got, to_core)
    core_pair = permute(got_pair, to_core)
    line_2 = pair_line(own_map, got_pair)
    pair, mirror, theirs, core_got, core_pair, line_2 = together(
        pair, mirror, theirs, core_got, core_pair, line_2
    )

    pair_2 = permute(line_2, to_x_pair)
    mirror_2 = permute(line_2, to_x_mirror)
    far_a, far_b = permute(pair[:2], to_x_mirror), permute(mirror[2:], to_x_pair)
    partner, full, mine, others = pair_map(
        own_map, got, got_pair, core_got, core_pair, source, theirs
    )
    far_a, far_b, mine, others = together(far_a, far_b, mine, others)
    far = pack(far_a, far_b)
    far_2 = permute(far, to_y_pair)
    beside = permute(others, to_x_pair)
    across = permute(mine, to_x_mirror)
    pair_2, mirror_2, far_2, beside, across = together(pair_2, mirror_2, far_2, beside, across)
    from_far = permute(beside, to_x_mirror)

    core = permute(pack(pair, mirror, pair_2, mirror_2, far, far_2), to_core)
    pair_full, other_maps, group_trace, other_trace, plane_trace, moving = join(
        pair, pair_2, mirror, mirror_2, far, far_2, core,
        full, mine, beside, across, from_far,
    )

    added = [plane_trace[:32], plane_trace[32:]]
    parts = [permute(part, to_z_next) for part in (moving[:32], moving[32:])]
    other_map, plane_map = to_plane(full, pair_full, other_maps)
    for turn in range(7):
        parts = [apply_t_add(plane_map, part, extra) for part, extra in zip(parts, added)]
        if turn == 1:
            late = permute(together(source, *parts)[0], to_y_far)
        parts = [permute(part, to_z_next) for part in parts]

    own, other = lift(*parts, other_map, other_trace, full, pair_full, mine, beside)
    pieces = (
        own,
        permute(other, to_x_pair),
        permute(own, to_y_far),
        permute(other, to_xy_far),
    )
    traces = last(*pieces, partner, late, theirs)
    return traces[None]


def solution(mesh):
    in_specs = (P("guide", None, None), P("guide", None, None), P("guide", "face", None))
    out_specs = P("guide", "face", None)
    return jax.shard_map(local, mesh=mesh, in_specs=in_specs, out_specs=out_specs, check_vma=False)
```

```python
import functools

import jax
import jax.numpy as jnp
from jax import lax
from jax.experimental import pallas as pl
from jax.experimental.pallas import tpu as pltpu
from jax.sharding import PartitionSpec as P

AXES = ("guide", "face")
BF16, F32 = jnp.bfloat16, jnp.float32
SIDE = 256
ANY = pl.BlockSpec(memory_space=pl.ANY)
VMEM = pl.BlockSpec(memory_space=pltpu.VMEM)


def coords(device):
    guide, face = divmod(device, 4)
    return guide // 2 % 4, guide % 2 * 2 + face // 2, guide // 8, face % 2


def device_at(x, y, z, core):
    x, y, z = x % 4, y % 4, z % 8
    return (z * 8 + x * 2 + y // 2) * 4 + y % 2 * 2 + core


def permute(block, target):
    route = [(i, device_at(*target(*coords(i)))) for i in range(256)]
    return lax.ppermute(block, AXES, route)


def to_core(x, y, z, c):
    return x, y, z, 1 - c


def to_y_mirror(x, y, z, c):
    return x, 3 - y, z, c


def to_y_pair(x, y, z, c):
    return x, y ^ 1, z, c


def to_y_far(x, y, z, c):
    return x, y + 2, z, c


def to_x_pair(x, y, z, c):
    return x ^ 1, y, z, c


def to_x_mirror(x, y, z, c):
    return 3 - x, y, z, c


def to_xy_far(x, y, z, c):
    return x ^ 1, y + 2, z, c


def to_z_next(x, y, z, c):
    return x, y, z + 1, c


def act(linear_map, vectors):
    return lax.dot_general(
        vectors, linear_map, (((1,), (1,)), ((), ())), preferred_element_type=F32
    )


def act_add(linear_map, vectors, added):
    return (act(linear_map, vectors) + added.astype(F32)).astype(BF16)


def apply_t(transposed, vectors):
    return jnp.dot(vectors, transposed, preferred_element_type=F32)


def apply_t_add(transposed, vectors, added):
    return (apply_t(transposed, vectors) + added.astype(F32)).astype(BF16)


class Place:
    def __init__(self):
        guide, self.face = lax.axis_index("guide"), lax.axis_index("face")
        self.x, self.y_hi, self.y_lo = guide // 2 % 4, guide % 2, self.face // 2
        self.core = self.face % 2
        self.x_hi, self.x_lo = self.x // 2, self.x % 2
        self.strip = (self.x_lo + self.x_hi) % 2


def span(index, size=SIDE):
    return pl.ds(pl.multiple_of(index * size, size), size)


def block_of(ref, row, col):
    return ref.at[span(row), span(col)]


def send_kernel(own, out):
    place = Place()
    line = span((place.face + 2) % 4)

    @pl.when(place.y_hi == 1)
    def _():
        for t in range(4):
            out[t] = own[line, t * SIDE : (t + 1) * SIDE]

    @pl.when(place.y_hi == 0)
    def _():
        for t in range(4):
            out[t] = own[t * SIDE : (t + 1) * SIDE, line]


def send_line(own):
    return pl.pallas_call(
        send_kernel,
        in_specs=[VMEM],
        out_specs=VMEM,
        out_shape=jax.ShapeDtypeStruct((4, SIDE, SIDE), BF16),
        compiler_params=pltpu.CompilerParams(vmem_limit_bytes=8 * 1024 * 1024),
    )(own)


def small(**sizes):
    return dict(
        compiler_params=pltpu.CompilerParams(vmem_limit_bytes=12 * 1024 * 1024),
        cost_estimate=pl.CostEstimate(
            flops=sizes.get("flops", 0), bytes_accessed=1024**2, transcendentals=0
        ),
    )


def blocks(count):
    return jax.ShapeDtypeStruct((count, SIDE, SIDE), BF16)


SOURCE_CHUNK = 64


def source_kernel(volume, leaf, keep, send, volume_held, leaf_held, sems):
    place = Place()
    pieces = []
    for ref, held in ((volume, volume_held), (leaf, leaf_held)):
        for start in range(0, ref.shape[0], SOURCE_CHUNK):
            rows = pl.ds(start, SOURCE_CHUNK)
            pieces.append(pltpu.make_async_copy(ref.at[rows], held.at[rows], sems.at[len(pieces)]))
    for piece in pieces:
        piece.start()
    leading = volume.shape[0] // SOURCE_CHUNK
    for piece in pieces[:leading]:
        piece.wait()
    per_tile = SIDE // SOURCE_CHUNK
    for t in range(leaf.shape[0] // SIDE):
        for piece in pieces[leading + t * per_tile : leading + (t + 1) * per_tile]:
            piece.wait()
        cols = slice(t * SIDE, (t + 1) * SIDE)
        tile = act(leaf_held[cols, :], volume_held[...]).astype(BF16)
        for half in range(2):

            @pl.when(place.y_hi == half)
            def _():
                keep[:, cols] = tile[128 * half : 128 * half + 128]
                send[:, cols] = tile[128 * (1 - half) : 128 * (1 - half) + 128]


def to_source(leaf, volume):
    rows, depth = volume.shape
    half = jax.ShapeDtypeStruct((rows // 2, leaf.shape[0]), BF16)
    return pl.pallas_call(
        source_kernel,
        in_specs=[ANY] * 2,
        out_specs=[VMEM] * 2,
        out_shape=[half, half],
        scratch_shapes=[
            pltpu.VMEM(volume.shape, BF16),
            pltpu.VMEM(leaf.shape, BF16),
            pltpu.SemaphoreType.DMA(((rows + leaf.shape[0]) // SOURCE_CHUNK,)),
        ],
        compiler_params=pltpu.CompilerParams(vmem_limit_bytes=56 * 1024 * 1024),
        cost_estimate=pl.CostEstimate(
            flops=2 * rows * depth * leaf.shape[0],
            bytes_accessed=2 * depth * (rows + leaf.shape[0]),
            transcendentals=0,
        ),
    )(volume, leaf)


def line_kernel(own, got, line):
    place = Place()

    @pl.when(place.y_hi == 0)
    def _():
        row = jnp.concatenate([got[t] for t in range(4)], axis=1)
        for t in range(4):
            cols = slice(t * SIDE, (t + 1) * SIDE)
            line[t] = jnp.dot(row, own[:, cols], preferred_element_type=F32).T.astype(BF16)

    @pl.when(place.y_hi == 1)
    def _():
        col = jnp.concatenate([got[t] for t in range(4)], axis=0)
        for t in range(4):
            rows = slice(t * SIDE, (t + 1) * SIDE)
            line[t] = jnp.dot(own[rows, :], col, preferred_element_type=F32).T.astype(BF16)


def pair_line(own, got):
    return pl.pallas_call(
        line_kernel,
        in_specs=[VMEM] * 2,
        out_specs=VMEM,
        out_shape=blocks(4),
        **small(flops=2 * SIDE * 1024**2),
    )(own, got)


def multiply(left, right):
    return jnp.dot(left[...], right[...], preferred_element_type=F32).astype(BF16)


def multiply_transposed(left, right, out):
    for t in range(4):
        cols = slice(t * SIDE, (t + 1) * SIDE)
        out[cols, :] = jnp.dot(left[...], right[:, cols], preferred_element_type=F32).T.astype(BF16)


def full_kernel(own, got, got_pair, core_got, core_pair, half, theirs, *outs):
    partner, full, mine, others = outs
    place = Place()
    quarters = ((0, got), (2, got_pair), (1, core_got), (3, core_pair))

    def line_of(flip):
        return (place.y_lo + flip // 2) % 2 * 2 + (place.core + flip) % 2

    @pl.when(place.y_hi == 1)
    def _():
        for flip, ref in quarters:
            for t in range(4):
                partner[t * SIDE : (t + 1) * SIDE, span(line_of(flip))] = ref[t]
        multiply_transposed(own, partner, full)
        trace = act_add(own[...], theirs[...], half[...])
        mine[...] = trace[:64]
        others[...] = trace[64:]

    @pl.when(place.y_hi == 0)
    def _():
        for flip, ref in quarters:
            for t in range(4):
                partner[span(line_of(flip)), t * SIDE : (t + 1) * SIDE] = ref[t]
        multiply_transposed(partner, own, full)
        trace = act_add(partner[...], half[...], theirs[...])
        mine[...] = trace[:64]
        others[...] = trace[64:]

    @pl.when(place.strip == 1)
    def _():
        first, second = mine[...], others[...]
        mine[...] = second
        others[...] = first


def pair_map(*args):
    strip = jax.ShapeDtypeStruct((64, 1024), BF16)
    return pl.pallas_call(
        full_kernel,
        in_specs=[VMEM] * 7,
        out_specs=[VMEM] * 4,
        out_shape=[map_shape(), map_shape(), strip, strip],
        compiler_params=pltpu.CompilerParams(vmem_limit_bytes=16 * 1024 * 1024),
        cost_estimate=pl.CostEstimate(
            flops=2 * 1024**3, bytes_accessed=8 * 1024**2, transcendentals=0
        ),
    )(*args)


def pack_kernel(*refs):
    out, filled = refs[-1], 0
    for ref in refs[:-1]:
        size = min(ref.shape[0], 4)
        out[filled : filled + size] = ref[:size]
        filled += size


def pack(*arrays):
    return pl.pallas_call(
        pack_kernel,
        in_specs=[VMEM] * len(arrays),
        out_specs=VMEM,
        out_shape=blocks(sum(min(array.shape[0], 4) for array in arrays)),
        **small(),
    )(*arrays)


def gather_copies(place, target, lines, sems):
    copies = []
    upper = place.y_hi == 1
    for flip, line in zip((0, 2, 1, 3), lines):
        index = (place.y_lo + flip // 2) % 2 * 2 + (place.core + flip) % 2
        for t in range(4):
            row = jnp.where(upper, index, t)
            col = jnp.where(upper, t, index)
            copies.append(
                pltpu.make_async_copy(line.at[t], block_of(target, row, col), sems.at[len(copies)])
            )
    return copies


def map_shape(*lead):
    return jax.ShapeDtypeStruct((*lead, 1024, 1024), BF16)


def join_kernel(*refs):
    pair, pair_2, mirror, mirror_2, far, far_2, core = refs[:7]
    full, mine, beside, across, from_far = refs[7:12]
    pair_full, others, group_trace, other_trace, plane_trace, moving, sems = refs[12:]
    place = Place()
    mirror_slot = place.x_lo
    pair_lines = (pair, pair_2, core.at[0:4], core.at[8:12])
    mirror_lines = (mirror, mirror_2, core.at[4:8], core.at[12:16])
    far_lines = (far, far_2, core.at[16:20], core.at[20:24])
    pair_copies = gather_copies(place, pair_full, pair_lines, sems.at[0])
    other_copies = gather_copies(place, others.at[mirror_slot], mirror_lines, sems.at[1])
    other_copies += gather_copies(place, others.at[1 - mirror_slot], far_lines, sems.at[2])
    for copy in pair_copies + other_copies:
        copy.start()
    for copy in pair_copies:
        copy.wait()

    @pl.when(place.x_lo == 1)
    def _():
        group_trace[...] = apply_t_add(full[...], beside[...], mine[...])

    @pl.when(place.x_lo == 0)
    def _():
        group_trace[...] = apply_t_add(pair_full[...], mine[...], beside[...])

    for copy in other_copies:
        copy.wait()
    mirror_low = place.x_lo == 1
    low = jnp.where(mirror_low, across[...], from_far[...])
    high = jnp.where(mirror_low, from_far[...], across[...])
    other_trace[...] = apply_t_add(others[0], low, high)

    def through(upper, lower, low, high):
        inner = apply_t(lower[...], low[...]).astype(BF16)
        plane_trace[...] = apply_t_add(upper[...], inner, high[...])

    @pl.when(jnp.logical_and(place.x_hi == 1, place.x_lo == 1))
    def _():
        through(full, pair_full, other_trace, group_trace)

    @pl.when(jnp.logical_and(place.x_hi == 1, place.x_lo == 0))
    def _():
        through(pair_full, full, other_trace, group_trace)

    @pl.when(place.x_hi == 0)
    def _():
        through(others.at[0], others.at[1], group_trace, other_trace)

    moving[...] = jnp.where(place.x_hi == 1, group_trace[...], plane_trace[...])


def join(*args):
    strip = jax.ShapeDtypeStruct((64, 1024), BF16)
    return pl.pallas_call(
        join_kernel,
        in_specs=[ANY] * 7 + [VMEM] * 5,
        out_specs=[VMEM] * 6,
        out_shape=[map_shape(), map_shape(2), strip, strip, strip, strip],
        scratch_shapes=[pltpu.SemaphoreType.DMA((3, 16))],
        compiler_params=pltpu.CompilerParams(vmem_limit_bytes=18 * 1024 * 1024),
        cost_estimate=pl.CostEstimate(
            flops=8 * 64 * 1024**2, bytes_accessed=14 * 1024**2, transcendentals=0
        ),
    )(*args)


def plane_kernel(full, pair_full, others, other, plane, own):
    place = Place()

    @pl.when(place.x_lo == 1)
    def _():
        own[...] = multiply(pair_full, full)

    @pl.when(place.x_lo == 0)
    def _():
        own[...] = multiply(full, pair_full)

    other[...] = multiply(others.at[1], others.at[0])

    @pl.when(place.x_hi == 1)
    def _():
        plane[...] = multiply(other, own)

    @pl.when(place.x_hi == 0)
    def _():
        plane[...] = multiply(own, other)


def to_plane(*args):
    return pl.pallas_call(
        plane_kernel,
        in_specs=[VMEM] * 3,
        out_specs=[VMEM] * 2,
        out_shape=[map_shape()] * 2,
        scratch_shapes=[pltpu.VMEM((1024, 1024), BF16)],
        compiler_params=pltpu.CompilerParams(vmem_limit_bytes=18 * 1024 * 1024),
        cost_estimate=pl.CostEstimate(
            flops=6 * 1024**3, bytes_accessed=12 * 1024**2, transcendentals=0
        ),
    )(*args)


def lift_kernel(part_a, part_b, other_map, other_trace, full, pair_full, mine, beside, own, across):
    place = Place()
    own[0:32, :] = part_a[...]
    own[32:64, :] = part_b[...]

    @pl.when(place.x_hi == 1)
    def _():
        own[...] = apply_t_add(other_map[...], own[...], other_trace[...])

    @pl.when(place.x_lo == 1)
    def _():
        across[...] = own[...]
        own[...] = apply_t_add(pair_full[...], own[...], beside[...])

    @pl.when(place.x_lo == 0)
    def _():
        across[...] = apply_t_add(full[...], own[...], mine[...])


def lift(*args):
    strip = jax.ShapeDtypeStruct((64, 1024), BF16)
    return pl.pallas_call(
        lift_kernel,
        in_specs=[VMEM] * 8,
        out_specs=[VMEM] * 2,
        out_shape=[strip, strip],
        **small(flops=4 * 64 * 1024**2),
    )(*args)


def last_kernel(e00, e01, e10, e11, partner, late, theirs, out, held):
    place = Place()
    for part, (flip_y, flip_x) in ((e00, (0, 0)), (e01, (0, 1)), (e10, (1, 0)), (e11, (1, 1))):
        index = 2 * ((place.y_hi + flip_y) % 2) + (place.strip + flip_x) % 2
        held[span(index, 64), :] = part[...]

    @pl.when(place.y_hi == 0)
    def _():
        out[...] = held[...]

    @pl.when(place.y_hi == 1)
    def _():
        added = jnp.concatenate([late[...], theirs[...]], axis=0)
        out[...] = act_add(partner[...], held[...], added)


def last(*args):
    return pl.pallas_call(
        last_kernel,
        in_specs=[VMEM] * 7,
        out_specs=VMEM,
        out_shape=jax.ShapeDtypeStruct((256, 1024), BF16),
        scratch_shapes=[pltpu.VMEM((256, 1024), BF16)],
        **small(flops=2 * 256 * 1024**2),
    )(*args)


def together(*values):
    return lax.optimization_barrier(values)


def local(transfer, leaf_map, volume_source):
    place = Place()
    own_map = transfer[0]

    got = permute(send_line(own_map), to_y_mirror)
    source, source_out = to_source(leaf_map[0], volume_source[0])
    got, source_out = together(got, source_out)
    line = pair_line(own_map, got)

    got_pair = permute(got, to_y_pair)
    pair = permute(line, to_x_pair)
    mirror = permute(line, to_x_mirror)
    relay = permute(source_out, to_y_pair)
    core_got = permute(got, to_core)
    line_2 = pair_line(own_map, got_pair)
    got_pair, line_2, relay = together(got_pair, line_2, relay)
    core_pair = permute(got_pair, to_core)
    theirs = permute(relay, to_y_mirror)
    pair, mirror, core_got, core_pair, line_2 = together(
        pair, mirror, core_got, core_pair, line_2
    )

    pair_2 = permute(line_2, to_x_pair)
    mirror_2 = permute(line_2, to_x_mirror)
    far_a, far_b = permute(pair[:2], to_x_mirror), permute(mirror[2:], to_x_pair)
    partner, full, mine, others = pair_map(
        own_map, got, got_pair, core_got, core_pair, source, theirs
    )
    far_a, far_b, mine, others = together(far_a, far_b, mine, others)
    far = pack(far_a, far_b)
    far_2 = permute(far, to_y_pair)
    beside = permute(others, to_x_pair)
    across = permute(mine, to_x_mirror)
    pair_2, mirror_2, far_2, beside, across = together(pair_2, mirror_2, far_2, beside, across)
    from_far = permute(beside, to_x_mirror)

    core = permute(pack(pair, mirror, pair_2, mirror_2, far, far_2), to_core)
    pair_full, other_maps, group_trace, other_trace, plane_trace, moving = join(
        pair, pair_2, mirror, mirror_2, far, far_2, core,
        full, mine, beside, across, from_far,
    )

    added = [plane_trace[:32], plane_trace[32:]]
    parts = [permute(part, to_z_next) for part in (moving[:32], moving[32:])]
    other_map, plane_map = to_plane(full, pair_full, other_maps)
    for turn in range(7):
        parts = [apply_t_add(plane_map, part, extra) for part, extra in zip(parts, added)]
        if turn == 1:
            late = permute(together(source, *parts)[0], to_y_far)
        parts = [permute(part, to_z_next) for part in parts]

    own, other = lift(*parts, other_map, other_trace, full, pair_full, mine, beside)
    pieces = (
        own,
        permute(other, to_x_pair),
        permute(own, to_y_far),
        permute(other, to_xy_far),
    )
    traces = last(*pieces, partner, late, theirs)
    return traces[None]


def solution(mesh):
    in_specs = (P("guide", None, None), P("guide", None, None), P("guide", "face", None))
    out_specs = P("guide", "face", None)
    return jax.shard_map(local, mesh=mesh, in_specs=in_specs, out_specs=out_specs, check_vma=False)
```

```python
import functools

import jax
import jax.numpy as jnp
from jax import lax
from jax.experimental import pallas as pl
from jax.experimental.pallas import tpu as pltpu
from jax.sharding import PartitionSpec as P

AXES = ("guide", "face")
BF16, F32 = jnp.bfloat16, jnp.float32
SIDE = 256
ANY = pl.BlockSpec(memory_space=pl.ANY)
VMEM = pl.BlockSpec(memory_space=pltpu.VMEM)


def coords(device):
    guide, face = divmod(device, 4)
    return guide // 2 % 4, guide % 2 * 2 + face // 2, guide // 8, face % 2


def device_at(x, y, z, core):
    x, y, z = x % 4, y % 4, z % 8
    return (z * 8 + x * 2 + y // 2) * 4 + y % 2 * 2 + core


def permute(block, target):
    route = [(i, device_at(*target(*coords(i)))) for i in range(256)]
    return lax.ppermute(block, AXES, route)


def to_core(x, y, z, c):
    return x, y, z, 1 - c


def to_y_mirror(x, y, z, c):
    return x, 3 - y, z, c


def to_y_pair(x, y, z, c):
    return x, y ^ 1, z, c


def to_y_far(x, y, z, c):
    return x, y + 2, z, c


def to_x_pair(x, y, z, c):
    return x ^ 1, y, z, c


def to_x_mirror(x, y, z, c):
    return 3 - x, y, z, c


def to_xy_far(x, y, z, c):
    return x ^ 1, y + 2, z, c


def to_z_next(x, y, z, c):
    return x, y, z + 1, c


def act(linear_map, vectors):
    return lax.dot_general(
        vectors, linear_map, (((1,), (1,)), ((), ())), preferred_element_type=F32
    )


def act_add(linear_map, vectors, added):
    return (act(linear_map, vectors) + added.astype(F32)).astype(BF16)


def apply_t(transposed, vectors):
    return jnp.dot(vectors, transposed, preferred_element_type=F32)


def apply_t_add(transposed, vectors, added):
    return (apply_t(transposed, vectors) + added.astype(F32)).astype(BF16)


class Place:
    def __init__(self):
        guide, self.face = lax.axis_index("guide"), lax.axis_index("face")
        self.x, self.y_hi, self.y_lo = guide // 2 % 4, guide % 2, self.face // 2
        self.core = self.face % 2
        self.x_hi, self.x_lo = self.x // 2, self.x % 2
        self.strip = (self.x_lo + self.x_hi) % 2


def span(index, size=SIDE):
    return pl.ds(pl.multiple_of(index * size, size), size)


def block_of(ref, row, col):
    return ref.at[span(row), span(col)]


def send_kernel(own, out):
    place = Place()
    line = span((place.face + 2) % 4)

    @pl.when(place.y_hi == 1)
    def _():
        for t in range(4):
            out[t] = own[line, t * SIDE : (t + 1) * SIDE]

    @pl.when(place.y_hi == 0)
    def _():
        for t in range(4):
            out[t] = own[t * SIDE : (t + 1) * SIDE, line]


def send_line(own):
    return pl.pallas_call(
        send_kernel,
        in_specs=[VMEM],
        out_specs=VMEM,
        out_shape=jax.ShapeDtypeStruct((4, SIDE, SIDE), BF16),
        compiler_params=pltpu.CompilerParams(vmem_limit_bytes=8 * 1024 * 1024),
    )(own)


def small(**sizes):
    return dict(
        compiler_params=pltpu.CompilerParams(vmem_limit_bytes=12 * 1024 * 1024),
        cost_estimate=pl.CostEstimate(
            flops=sizes.get("flops", 0), bytes_accessed=1024**2, transcendentals=0
        ),
    )


def blocks(count):
    return jax.ShapeDtypeStruct((count, SIDE, SIDE), BF16)


def source_kernel(volume, leaf, keep, send):
    place = Place()
    tile = act(leaf[...], volume[...]).astype(BF16)
    half_rows = keep.shape[0]
    for half in range(2):

        @pl.when(place.y_hi == half)
        def _():
            keep[...] = tile[half_rows * half : half_rows * (half + 1)]
            send[...] = tile[half_rows * (1 - half) : half_rows * (2 - half)]


def to_source(leaf, volume):
    rows, depth = volume.shape
    half = pl.BlockSpec((rows // 2, SIDE), lambda t: (0, t))
    return pl.pallas_call(
        source_kernel,
        grid=(leaf.shape[0] // SIDE,),
        in_specs=[
            pl.BlockSpec((rows, depth), lambda t: (0, 0)),
            pl.BlockSpec((SIDE, depth), lambda t: (t, 0)),
        ],
        out_specs=[half, half],
        out_shape=[jax.ShapeDtypeStruct((rows // 2, leaf.shape[0]), BF16)] * 2,
        compiler_params=pltpu.CompilerParams(vmem_limit_bytes=16 * 1024 * 1024),
        cost_estimate=pl.CostEstimate(
            flops=2 * rows * depth * leaf.shape[0],
            bytes_accessed=2 * depth * (rows + leaf.shape[0]),
            transcendentals=0,
        ),
    )(volume, leaf)


def line_kernel(own, got, line):
    place = Place()

    @pl.when(place.y_hi == 0)
    def _():
        row = jnp.concatenate([got[t] for t in range(4)], axis=1)
        for t in range(4):
            cols = slice(t * SIDE, (t + 1) * SIDE)
            line[t] = jnp.dot(row, own[:, cols], preferred_element_type=F32).T.astype(BF16)

    @pl.when(place.y_hi == 1)
    def _():
        col = jnp.concatenate([got[t] for t in range(4)], axis=0)
        for t in range(4):
            rows = slice(t * SIDE, (t + 1) * SIDE)
            line[t] = jnp.dot(own[rows, :], col, preferred_element_type=F32).T.astype(BF16)


def pair_line(own, got):
    return pl.pallas_call(
        line_kernel,
        in_specs=[VMEM] * 2,
        out_specs=VMEM,
        out_shape=blocks(4),
        **small(flops=2 * SIDE * 1024**2),
    )(own, got)


def multiply(left, right):
    return jnp.dot(left[...], right[...], preferred_element_type=F32).astype(BF16)


def multiply_transposed(left, right, out):
    for t in range(4):
        cols = slice(t * SIDE, (t + 1) * SIDE)
        out[cols, :] = jnp.dot(left[...], right[:, cols], preferred_element_type=F32).T.astype(BF16)


def full_kernel(own, got, got_pair, core_got, core_pair, half, theirs, *outs):
    partner, full, mine, others = outs
    place = Place()
    quarters = ((0, got), (2, got_pair), (1, core_got), (3, core_pair))

    def line_of(flip):
        return (place.y_lo + flip // 2) % 2 * 2 + (place.core + flip) % 2

    @pl.when(place.y_hi == 1)
    def _():
        for flip, ref in quarters:
            for t in range(4):
                partner[t * SIDE : (t + 1) * SIDE, span(line_of(flip))] = ref[t]
        multiply_transposed(own, partner, full)
        trace = act_add(own[...], theirs[...], half[...])
        mine[...] = trace[:64]
        others[...] = trace[64:]

    @pl.when(place.y_hi == 0)
    def _():
        for flip, ref in quarters:
            for t in range(4):
                partner[span(line_of(flip)), t * SIDE : (t + 1) * SIDE] = ref[t]
        multiply_transposed(partner, own, full)
        trace = act_add(partner[...], half[...], theirs[...])
        mine[...] = trace[:64]
        others[...] = trace[64:]

    @pl.when(place.strip == 1)
    def _():
        first, second = mine[...], others[...]
        mine[...] = second
        others[...] = first


def pair_map(*args):
    strip = jax.ShapeDtypeStruct((64, 1024), BF16)
    return pl.pallas_call(
        full_kernel,
        in_specs=[VMEM] * 7,
        out_specs=[VMEM] * 4,
        out_shape=[map_shape(), map_shape(), strip, strip],
        compiler_params=pltpu.CompilerParams(vmem_limit_bytes=16 * 1024 * 1024),
        cost_estimate=pl.CostEstimate(
            flops=2 * 1024**3, bytes_accessed=8 * 1024**2, transcendentals=0
        ),
    )(*args)


def pack_kernel(*refs):
    out, filled = refs[-1], 0
    for ref in refs[:-1]:
        size = min(ref.shape[0], 4)
        out[filled : filled + size] = ref[:size]
        filled += size


def pack(*arrays):
    return pl.pallas_call(
        pack_kernel,
        in_specs=[VMEM] * len(arrays),
        out_specs=VMEM,
        out_shape=blocks(sum(min(array.shape[0], 4) for array in arrays)),
        **small(),
    )(*arrays)


def gather_copies(place, target, lines, sems):
    copies = []
    upper = place.y_hi == 1
    for flip, line in zip((0, 2, 1, 3), lines):
        index = (place.y_lo + flip // 2) % 2 * 2 + (place.core + flip) % 2
        for t in range(4):
            row = jnp.where(upper, index, t)
            col = jnp.where(upper, t, index)
            copies.append(
                pltpu.make_async_copy(line.at[t], block_of(target, row, col), sems.at[len(copies)])
            )
    return copies


def map_shape(*lead):
    return jax.ShapeDtypeStruct((*lead, 1024, 1024), BF16)


def group_kernel(line, line_2, core, full, mine, beside, pair_full, group, trace, sems):
    place = Place()
    lines = (line, line_2, core.at[0:4], core.at[4:8])
    copies = gather_copies(place, pair_full, lines, sems)
    for copy in copies:
        copy.start()
    for copy in copies:
        copy.wait()

    @pl.when(place.x_lo == 1)
    def _():
        trace[...] = apply_t_add(full[...], beside[...], mine[...])
        group[...] = multiply(pair_full, full)

    @pl.when(place.x_lo == 0)
    def _():
        trace[...] = apply_t_add(pair_full[...], mine[...], beside[...])
        group[...] = multiply(full, pair_full)


def to_group(*args):
    return pl.pallas_call(
        group_kernel,
        in_specs=[ANY] * 3 + [VMEM] * 3,
        out_specs=[VMEM] * 3,
        out_shape=[map_shape(), map_shape(), jax.ShapeDtypeStruct((64, 1024), BF16)],
        scratch_shapes=[pltpu.SemaphoreType.DMA((16,))],
        compiler_params=pltpu.CompilerParams(vmem_limit_bytes=16 * 1024 * 1024),
        cost_estimate=pl.CostEstimate(
            flops=2 * 1024**3, bytes_accessed=8 * 1024**2, transcendentals=0
        ),
    )(*args)


def join_kernel(*refs):
    mirror, mirror_2, far, far_2, core = refs[:5]
    group, group_trace, across, from_far = refs[5:9]
    others, other_trace, plane_trace, moving, sems = refs[9:]
    place = Place()
    mirror_slot = place.x_lo
    mirror_lines = (mirror, mirror_2, core.at[0:4], core.at[4:8])
    far_lines = (far, far_2, core.at[8:12], core.at[12:16])
    copies = gather_copies(place, others.at[mirror_slot], mirror_lines, sems.at[0])
    copies += gather_copies(place, others.at[1 - mirror_slot], far_lines, sems.at[1])
    for copy in copies:
        copy.start()
    for copy in copies:
        copy.wait()
    mirror_low = place.x_lo == 1
    low = jnp.where(mirror_low, across[...], from_far[...])
    high = jnp.where(mirror_low, from_far[...], across[...])
    other_trace[...] = apply_t_add(others[0], low, high)

    @pl.when(place.x_hi == 1)
    def _():
        plane_trace[...] = apply_t_add(group[...], other_trace[...], group_trace[...])
        moving[...] = group_trace[...]

    @pl.when(place.x_hi == 0)
    def _():
        inner = apply_t(others[1], group_trace[...]).astype(BF16)
        total = apply_t_add(others[0], inner, other_trace[...])
        plane_trace[...] = total
        moving[...] = total


def join(*args):
    strip = jax.ShapeDtypeStruct((64, 1024), BF16)
    return pl.pallas_call(
        join_kernel,
        in_specs=[ANY] * 5 + [VMEM] * 4,
        out_specs=[VMEM] * 4,
        out_shape=[map_shape(2), strip, strip, strip],
        scratch_shapes=[pltpu.SemaphoreType.DMA((2, 16))],
        compiler_params=pltpu.CompilerParams(vmem_limit_bytes=16 * 1024 * 1024),
        cost_estimate=pl.CostEstimate(
            flops=6 * 64 * 1024**2, bytes_accessed=10 * 1024**2, transcendentals=0
        ),
    )(*args)


def plane_kernel(group, others, other, plane):
    place = Place()
    other[...] = multiply(others.at[1], others.at[0])

    @pl.when(place.x_hi == 1)
    def _():
        plane[...] = multiply(other, group)

    @pl.when(place.x_hi == 0)
    def _():
        plane[...] = multiply(group, other)


def to_plane(*args):
    return pl.pallas_call(
        plane_kernel,
        in_specs=[VMEM] * 2,
        out_specs=[VMEM] * 2,
        out_shape=[map_shape()] * 2,
        compiler_params=pltpu.CompilerParams(vmem_limit_bytes=16 * 1024 * 1024),
        cost_estimate=pl.CostEstimate(
            flops=4 * 1024**3, bytes_accessed=10 * 1024**2, transcendentals=0
        ),
    )(*args)


def lift_kernel(part_a, part_b, other_map, other_trace, full, pair_full, mine, beside, own, across):
    place = Place()
    own[0:32, :] = part_a[...]
    own[32:64, :] = part_b[...]

    @pl.when(place.x_hi == 1)
    def _():
        own[...] = apply_t_add(other_map[...], own[...], other_trace[...])

    @pl.when(place.x_lo == 1)
    def _():
        across[...] = own[...]
        own[...] = apply_t_add(pair_full[...], own[...], beside[...])

    @pl.when(place.x_lo == 0)
    def _():
        across[...] = apply_t_add(full[...], own[...], mine[...])


def lift(*args):
    strip = jax.ShapeDtypeStruct((64, 1024), BF16)
    return pl.pallas_call(
        lift_kernel,
        in_specs=[VMEM] * 8,
        out_specs=[VMEM] * 2,
        out_shape=[strip, strip],
        **small(flops=4 * 64 * 1024**2),
    )(*args)


def last_kernel(e00, e01, e10, e11, partner, late, theirs, out, held):
    place = Place()
    for part, (flip_y, flip_x) in ((e00, (0, 0)), (e01, (0, 1)), (e10, (1, 0)), (e11, (1, 1))):
        index = 2 * ((place.y_hi + flip_y) % 2) + (place.strip + flip_x) % 2
        held[span(index, 64), :] = part[...]

    @pl.when(place.y_hi == 0)
    def _():
        out[...] = held[...]

    @pl.when(place.y_hi == 1)
    def _():
        added = jnp.concatenate([late[...], theirs[...]], axis=0)
        out[...] = act_add(partner[...], held[...], added)


def last(*args):
    return pl.pallas_call(
        last_kernel,
        in_specs=[VMEM] * 7,
        out_specs=VMEM,
        out_shape=jax.ShapeDtypeStruct((256, 1024), BF16),
        scratch_shapes=[pltpu.VMEM((256, 1024), BF16)],
        **small(flops=2 * 256 * 1024**2),
    )(*args)


def together(*values):
    return lax.optimization_barrier(values)


def local(transfer, leaf_map, volume_source):
    place = Place()
    own_map = transfer[0]

    got = permute(send_line(own_map), to_y_mirror)
    source, source_out = to_source(leaf_map[0], volume_source[0])
    relay = permute(source_out, to_y_pair)
    got, relay = together(got, relay)
    line = pair_line(own_map, got)

    got_pair = permute(got, to_y_pair)
    pair = permute(line, to_x_pair)
    mirror = permute(line, to_x_mirror)
    theirs = permute(relay, to_y_mirror)
    core_got = permute(got, to_core)
    got_pair, theirs = together(got_pair, theirs)
    core_pair = permute(got_pair, to_core)
    line_2 = pair_line(own_map, got_pair)
    pair, mirror, theirs, core_got, core_pair, line_2 = together(
        pair, mirror, theirs, core_got, core_pair, line_2
    )

    pair_2 = permute(line_2, to_x_pair)
    mirror_2 = permute(line_2, to_x_mirror)
    far_a, far_b = permute(pair[:2], to_x_mirror), permute(mirror[2:], to_x_pair)
    partner, full, mine, others = pair_map(
        own_map, got, got_pair, core_got, core_pair, source, theirs
    )
    late = permute(source, to_y_far)
    far_a, far_b, mine, others, late = together(far_a, far_b, mine, others, late)
    far = pack(far_a, far_b)
    far_2 = permute(far, to_y_pair)
    beside = permute(others, to_x_pair)
    across = permute(mine, to_x_mirror)
    pair_2, mirror_2, far_2, beside, across = together(pair_2, mirror_2, far_2, beside, across)
    from_far = permute(beside, to_x_mirror)

    core_pairs = permute(pack(pair, pair_2), to_core)
    core_pairs, packed = together(core_pairs, pack(mirror, mirror_2, far, far_2))
    core_others = permute(packed, to_core)
    from_far = permute(beside, to_x_mirror)
    pair_full, group_map, group_trace = to_group(
        pair, pair_2, core_pairs, full, mine, beside
    )
    core_others, group_trace = together(core_others, group_trace)
    other_maps, other_trace, plane_trace, moving = join(
        mirror, mirror_2, far, far_2, core_others, group_map, group_trace, across, from_far
    )

    added = [plane_trace[:32], plane_trace[32:]]
    parts = [permute(part, to_z_next) for part in (moving[:32], moving[32:])]
    other_map, plane_map = to_plane(group_map, other_maps)
    for _ in range(7):
        parts = [apply_t_add(plane_map, part, extra) for part, extra in zip(parts, added)]
        parts = [permute(part, to_z_next) for part in parts]

    own, other = lift(*parts, other_map, other_trace, full, pair_full, mine, beside)
    pieces = (
        own,
        permute(other, to_x_pair),
        permute(own, to_y_far),
        permute(other, to_xy_far),
    )
    traces = last(*pieces, partner, late, theirs)
    return traces[None]


def solution(mesh):
    in_specs = (P("guide", None, None), P("guide", None, None), P("guide", "face", None))
    out_specs = P("guide", "face", None)
    return jax.shard_map(local, mesh=mesh, in_specs=in_specs, out_specs=out_specs, check_vma=False)
```

```python
import functools

import jax
import jax.numpy as jnp
from jax import lax
from jax.experimental import pallas as pl
from jax.experimental.pallas import tpu as pltpu
from jax.sharding import PartitionSpec as P

AXES = ("guide", "face")
BF16, F32 = jnp.bfloat16, jnp.float32
SIDE = 256
ANY = pl.BlockSpec(memory_space=pl.ANY)
VMEM = pl.BlockSpec(memory_space=pltpu.VMEM)


def coords(device):
    guide, face = divmod(device, 4)
    return guide // 2 % 4, guide % 2 * 2 + face // 2, guide // 8, face % 2


def device_at(x, y, z, core):
    x, y, z = x % 4, y % 4, z % 8
    return (z * 8 + x * 2 + y // 2) * 4 + y % 2 * 2 + core


def permute(block, target):
    route = [(i, device_at(*target(*coords(i)))) for i in range(256)]
    return lax.ppermute(block, AXES, route)


def to_core(x, y, z, c):
    return x, y, z, 1 - c


def to_y_mirror(x, y, z, c):
    return x, 3 - y, z, c


def to_y_pair(x, y, z, c):
    return x, y ^ 1, z, c


def to_y_far(x, y, z, c):
    return x, y + 2, z, c


def to_x_pair(x, y, z, c):
    return x ^ 1, y, z, c


def to_x_mirror(x, y, z, c):
    return 3 - x, y, z, c


def to_xy_far(x, y, z, c):
    return x ^ 1, y + 2, z, c


def to_z_next(x, y, z, c):
    return x, y, z + 1, c


def act(linear_map, vectors):
    return lax.dot_general(
        vectors, linear_map, (((1,), (1,)), ((), ())), preferred_element_type=F32
    )


def act_add(linear_map, vectors, added):
    return (act(linear_map, vectors) + added.astype(F32)).astype(BF16)


def apply_t(transposed, vectors):
    return jnp.dot(vectors, transposed, preferred_element_type=F32)


def apply_t_add(transposed, vectors, added):
    return (apply_t(transposed, vectors) + added.astype(F32)).astype(BF16)


class Place:
    def __init__(self):
        guide, self.face = lax.axis_index("guide"), lax.axis_index("face")
        self.x, self.y_hi, self.y_lo = guide // 2 % 4, guide % 2, self.face // 2
        self.core = self.face % 2
        self.x_hi, self.x_lo = self.x // 2, self.x % 2
        self.strip = (self.x_lo + self.x_hi) % 2


def span(index, size=SIDE):
    return pl.ds(pl.multiple_of(index * size, size), size)


def block_of(ref, row, col):
    return ref.at[span(row), span(col)]


def send_kernel(own, out):
    place = Place()
    line = span((place.face + 2) % 4)

    @pl.when(place.y_hi == 1)
    def _():
        for t in range(4):
            out[t] = own[line, t * SIDE : (t + 1) * SIDE]

    @pl.when(place.y_hi == 0)
    def _():
        for t in range(4):
            out[t] = own[t * SIDE : (t + 1) * SIDE, line]


def send_line(own):
    return pl.pallas_call(
        send_kernel,
        in_specs=[VMEM],
        out_specs=VMEM,
        out_shape=jax.ShapeDtypeStruct((4, SIDE, SIDE), BF16),
        compiler_params=pltpu.CompilerParams(vmem_limit_bytes=8 * 1024 * 1024),
    )(own)


def small(**sizes):
    return dict(
        compiler_params=pltpu.CompilerParams(vmem_limit_bytes=12 * 1024 * 1024),
        cost_estimate=pl.CostEstimate(
            flops=sizes.get("flops", 0), bytes_accessed=1024**2, transcendentals=0
        ),
    )


def blocks(count):
    return jax.ShapeDtypeStruct((count, SIDE, SIDE), BF16)


def source_kernel(volume, leaf, keep, send):
    place = Place()
    for t in range(leaf.shape[0] // SIDE):
        cols = slice(t * SIDE, (t + 1) * SIDE)
        tile = act(leaf[cols, :], volume[...]).astype(BF16)
        half_rows = keep.shape[0]
        for half in range(2):

            @pl.when(place.y_hi == half)
            def _():
                keep[:, cols] = tile[half_rows * half : half_rows * (half + 1)]
                send[:, cols] = tile[half_rows * (1 - half) : half_rows * (2 - half)]


def to_source(leaf, volume):
    rows, depth = volume.shape
    half = jax.ShapeDtypeStruct((rows // 2, leaf.shape[0]), BF16)
    return pl.pallas_call(
        source_kernel,
        in_specs=[VMEM] * 2,
        out_specs=[VMEM] * 2,
        out_shape=[half, half],
        compiler_params=pltpu.CompilerParams(vmem_limit_bytes=24 * 1024 * 1024),
        cost_estimate=pl.CostEstimate(
            flops=2 * rows * depth * leaf.shape[0],
            bytes_accessed=2 * depth * (rows + leaf.shape[0]),
            transcendentals=0,
        ),
    )(volume, leaf)


def line_kernel(own, got, line):
    place = Place()

    @pl.when(place.y_hi == 0)
    def _():
        row = jnp.concatenate([got[t] for t in range(4)], axis=1)
        for t in range(4):
            cols = slice(t * SIDE, (t + 1) * SIDE)
            line[t] = jnp.dot(row, own[:, cols], preferred_element_type=F32).T.astype(BF16)

    @pl.when(place.y_hi == 1)
    def _():
        col = jnp.concatenate([got[t] for t in range(4)], axis=0)
        for t in range(4):
            rows = slice(t * SIDE, (t + 1) * SIDE)
            line[t] = jnp.dot(own[rows, :], col, preferred_element_type=F32).T.astype(BF16)


def pair_line(own, got):
    return pl.pallas_call(
        line_kernel,
        in_specs=[VMEM] * 2,
        out_specs=VMEM,
        out_shape=blocks(4),
        **small(flops=2 * SIDE * 1024**2),
    )(own, got)


def multiply(left, right):
    return jnp.dot(left[...], right[...], preferred_element_type=F32).astype(BF16)


def multiply_transposed(left, right, out):
    for t in range(4):
        cols = slice(t * SIDE, (t + 1) * SIDE)
        out[cols, :] = jnp.dot(left[...], right[:, cols], preferred_element_type=F32).T.astype(BF16)


def full_kernel(own, got, got_pair, core_got, core_pair, half, theirs, *outs):
    partner, full, mine, others = outs
    place = Place()
    quarters = ((0, got), (2, got_pair), (1, core_got), (3, core_pair))

    def line_of(flip):
        return (place.y_lo + flip // 2) % 2 * 2 + (place.core + flip) % 2

    @pl.when(place.y_hi == 1)
    def _():
        for flip, ref in quarters:
            for t in range(4):
                partner[t * SIDE : (t + 1) * SIDE, span(line_of(flip))] = ref[t]
        multiply_transposed(own, partner, full)
        trace = act_add(own[...], theirs[...], half[...])
        mine[...] = trace[:64]
        others[...] = trace[64:]

    @pl.when(place.y_hi == 0)
    def _():
        for flip, ref in quarters:
            for t in range(4):
                partner[span(line_of(flip)), t * SIDE : (t + 1) * SIDE] = ref[t]
        multiply_transposed(partner, own, full)
        trace = act_add(partner[...], half[...], theirs[...])
        mine[...] = trace[:64]
        others[...] = trace[64:]

    @pl.when(place.strip == 1)
    def _():
        first, second = mine[...], others[...]
        mine[...] = second
        others[...] = first


def pair_map(*args):
    strip = jax.ShapeDtypeStruct((64, 1024), BF16)
    return pl.pallas_call(
        full_kernel,
        in_specs=[VMEM] * 7,
        out_specs=[VMEM] * 4,
        out_shape=[map_shape(), map_shape(), strip, strip],
        compiler_params=pltpu.CompilerParams(vmem_limit_bytes=16 * 1024 * 1024),
        cost_estimate=pl.CostEstimate(
            flops=2 * 1024**3, bytes_accessed=8 * 1024**2, transcendentals=0
        ),
    )(*args)


def pack_kernel(*refs):
    out, filled = refs[-1], 0
    for ref in refs[:-1]:
        size = min(ref.shape[0], 4)
        out[filled : filled + size] = ref[:size]
        filled += size


def pack(*arrays):
    return pl.pallas_call(
        pack_kernel,
        in_specs=[VMEM] * len(arrays),
        out_specs=VMEM,
        out_shape=blocks(sum(min(array.shape[0], 4) for array in arrays)),
        **small(),
    )(*arrays)


def gather_copies(place, target, lines, sems):
    copies = []
    upper = place.y_hi == 1
    for flip, line in zip((0, 2, 1, 3), lines):
        index = (place.y_lo + flip // 2) % 2 * 2 + (place.core + flip) % 2
        for t in range(4):
            row = jnp.where(upper, index, t)
            col = jnp.where(upper, t, index)
            copies.append(
                pltpu.make_async_copy(line.at[t], block_of(target, row, col), sems.at[len(copies)])
            )
    return copies


def map_shape(*lead):
    return jax.ShapeDtypeStruct((*lead, 1024, 1024), BF16)


def group_kernel(line, line_2, core, full, mine, beside, pair_full, group, trace, sems):
    place = Place()
    lines = (line, line_2, core.at[0:4], core.at[4:8])
    copies = gather_copies(place, pair_full, lines, sems)
    for copy in copies:
        copy.start()
    for copy in copies:
        copy.wait()

    @pl.when(place.x_lo == 1)
    def _():
        trace[...] = apply_t_add(full[...], beside[...], mine[...])
        group[...] = multiply(pair_full, full)

    @pl.when(place.x_lo == 0)
    def _():
        trace[...] = apply_t_add(pair_full[...], mine[...], beside[...])
        group[...] = multiply(full, pair_full)


def to_group(*args):
    return pl.pallas_call(
        group_kernel,
        in_specs=[ANY] * 3 + [VMEM] * 3,
        out_specs=[VMEM] * 3,
        out_shape=[map_shape(), map_shape(), jax.ShapeDtypeStruct((64, 1024), BF16)],
        scratch_shapes=[pltpu.SemaphoreType.DMA((16,))],
        compiler_params=pltpu.CompilerParams(vmem_limit_bytes=16 * 1024 * 1024),
        cost_estimate=pl.CostEstimate(
            flops=2 * 1024**3, bytes_accessed=8 * 1024**2, transcendentals=0
        ),
    )(*args)


def join_kernel(*refs):
    mirror, mirror_2, far, far_2, core = refs[:5]
    group, group_trace, across, from_far = refs[5:9]
    others, other_trace, plane_trace, moving, sems = refs[9:]
    place = Place()
    mirror_slot = place.x_lo
    mirror_lines = (mirror, mirror_2, core.at[0:4], core.at[4:8])
    far_lines = (far, far_2, core.at[8:12], core.at[12:16])
    copies = gather_copies(place, others.at[mirror_slot], mirror_lines, sems.at[0])
    copies += gather_copies(place, others.at[1 - mirror_slot], far_lines, sems.at[1])
    for copy in copies:
        copy.start()
    for copy in copies:
        copy.wait()
    mirror_low = place.x_lo == 1
    low = jnp.where(mirror_low, across[...], from_far[...])
    high = jnp.where(mirror_low, from_far[...], across[...])
    other_trace[...] = apply_t_add(others[0], low, high)

    @pl.when(place.x_hi == 1)
    def _():
        plane_trace[...] = apply_t_add(group[...], other_trace[...], group_trace[...])
        moving[...] = group_trace[...]

    @pl.when(place.x_hi == 0)
    def _():
        inner = apply_t(others[1], group_trace[...]).astype(BF16)
        total = apply_t_add(others[0], inner, other_trace[...])
        plane_trace[...] = total
        moving[...] = total


def join(*args):
    strip = jax.ShapeDtypeStruct((64, 1024), BF16)
    return pl.pallas_call(
        join_kernel,
        in_specs=[ANY] * 5 + [VMEM] * 4,
        out_specs=[VMEM] * 4,
        out_shape=[map_shape(2), strip, strip, strip],
        scratch_shapes=[pltpu.SemaphoreType.DMA((2, 16))],
        compiler_params=pltpu.CompilerParams(vmem_limit_bytes=16 * 1024 * 1024),
        cost_estimate=pl.CostEstimate(
            flops=6 * 64 * 1024**2, bytes_accessed=10 * 1024**2, transcendentals=0
        ),
    )(*args)


def plane_kernel(group, others, other, plane):
    place = Place()
    other[...] = multiply(others.at[1], others.at[0])

    @pl.when(place.x_hi == 1)
    def _():
        plane[...] = multiply(other, group)

    @pl.when(place.x_hi == 0)
    def _():
        plane[...] = multiply(group, other)


def to_plane(*args):
    return pl.pallas_call(
        plane_kernel,
        in_specs=[VMEM] * 2,
        out_specs=[VMEM] * 2,
        out_shape=[map_shape()] * 2,
        compiler_params=pltpu.CompilerParams(vmem_limit_bytes=16 * 1024 * 1024),
        cost_estimate=pl.CostEstimate(
            flops=4 * 1024**3, bytes_accessed=10 * 1024**2, transcendentals=0
        ),
    )(*args)


def lift_kernel(part_a, part_b, other_map, other_trace, full, pair_full, mine, beside, own, across):
    place = Place()
    own[0:32, :] = part_a[...]
    own[32:64, :] = part_b[...]

    @pl.when(place.x_hi == 1)
    def _():
        own[...] = apply_t_add(other_map[...], own[...], other_trace[...])

    @pl.when(place.x_lo == 1)
    def _():
        across[...] = own[...]
        own[...] = apply_t_add(pair_full[...], own[...], beside[...])

    @pl.when(place.x_lo == 0)
    def _():
        across[...] = apply_t_add(full[...], own[...], mine[...])


def lift(*args):
    strip = jax.ShapeDtypeStruct((64, 1024), BF16)
    return pl.pallas_call(
        lift_kernel,
        in_specs=[VMEM] * 8,
        out_specs=[VMEM] * 2,
        out_shape=[strip, strip],
        **small(flops=4 * 64 * 1024**2),
    )(*args)


def last_kernel(e00, e01, e10, e11, partner, late, theirs, out, held):
    place = Place()
    for part, (flip_y, flip_x) in ((e00, (0, 0)), (e01, (0, 1)), (e10, (1, 0)), (e11, (1, 1))):
        index = 2 * ((place.y_hi + flip_y) % 2) + (place.strip + flip_x) % 2
        held[span(index, 64), :] = part[...]

    @pl.when(place.y_hi == 0)
    def _():
        out[...] = held[...]

    @pl.when(place.y_hi == 1)
    def _():
        added = jnp.concatenate([late[...], theirs[...]], axis=0)
        out[...] = act_add(partner[...], held[...], added)


def last(*args):
    return pl.pallas_call(
        last_kernel,
        in_specs=[VMEM] * 7,
        out_specs=VMEM,
        out_shape=jax.ShapeDtypeStruct((256, 1024), BF16),
        scratch_shapes=[pltpu.VMEM((256, 1024), BF16)],
        **small(flops=2 * 256 * 1024**2),
    )(*args)


def together(*values):
    return lax.optimization_barrier(values)


def local(transfer, leaf_map, volume_source):
    place = Place()
    own_map = transfer[0]

    got = permute(send_line(own_map), to_y_mirror)
    source, source_out = to_source(leaf_map[0], volume_source[0])
    relay = permute(source_out, to_y_pair)
    got, relay = together(got, relay)
    line = pair_line(own_map, got)

    got_pair = permute(got, to_y_pair)
    relay, line = together(relay, line)
    pair = permute(line, to_x_pair)
    mirror = permute(line, to_x_mirror)
    theirs = permute(relay, to_y_mirror)
    core_got = permute(got, to_core)
    got_pair, theirs = together(got_pair, theirs)
    line_2 = pair_line(own_map, got_pair)
    got_pair, line_2 = together(got_pair, line_2)
    core_pair = permute(got_pair, to_core)
    pair, mirror, theirs, core_got, core_pair, line_2 = together(
        pair, mirror, theirs, core_got, core_pair, line_2
    )

    pair_2 = permute(line_2, to_x_pair)
    mirror_2 = permute(line_2, to_x_mirror)
    far_a, far_b = permute(pair[:2], to_x_mirror), permute(mirror[2:], to_x_pair)
    partner, full, mine, others = pair_map(
        own_map, got, got_pair, core_got, core_pair, source, theirs
    )
    late = permute(source, to_y_far)
    far_a, far_b, mine, others, late = together(far_a, far_b, mine, others, late)
    far = pack(far_a, far_b)
    far_2 = permute(far, to_y_pair)
    beside = permute(others, to_x_pair)
    across = permute(mine, to_x_mirror)
    pair_2, mirror_2, far_2, beside, across = together(pair_2, mirror_2, far_2, beside, across)
    from_far = permute(beside, to_x_mirror)

    core_pairs = permute(pack(pair, pair_2), to_core)
    core_pairs, packed = together(core_pairs, pack(mirror, mirror_2, far, far_2))
    core_others = permute(packed, to_core)
    from_far = permute(beside, to_x_mirror)
    pair_full, group_map, group_trace = to_group(
        pair, pair_2, core_pairs, full, mine, beside
    )
    core_others, group_trace = together(core_others, group_trace)
    other_maps, other_trace, plane_trace, moving = join(
        mirror, mirror_2, far, far_2, core_others, group_map, group_trace, across, from_far
    )

    added = [plane_trace[:32], plane_trace[32:]]
    parts = [permute(part, to_z_next) for part in (moving[:32], moving[32:])]
    other_map, plane_map = to_plane(group_map, other_maps)
    for _ in range(7):
        parts = [apply_t_add(plane_map, part, extra) for part, extra in zip(parts, added)]
        parts = [permute(part, to_z_next) for part in parts]

    own, other = lift(*parts, other_map, other_trace, full, pair_full, mine, beside)
    pieces = (
        own,
        permute(other, to_x_pair),
        permute(own, to_y_far),
        permute(other, to_xy_far),
    )
    traces = last(*pieces, partner, late, theirs)
    return traces[None]


def solution(mesh):
    in_specs = (P("guide", None, None), P("guide", None, None), P("guide", "face", None))
    out_specs = P("guide", "face", None)
    return jax.shard_map(local, mesh=mesh, in_specs=in_specs, out_specs=out_specs, check_vma=False)
```

```python
import functools

import jax
import jax.numpy as jnp
from jax import lax
from jax.experimental import pallas as pl
from jax.experimental.pallas import tpu as pltpu
from jax.sharding import PartitionSpec as P

AXES = ("guide", "face")
BF16, F32 = jnp.bfloat16, jnp.float32
SIDE = 256
ANY = pl.BlockSpec(memory_space=pl.ANY)
VMEM = pl.BlockSpec(memory_space=pltpu.VMEM)


def coords(device):
    guide, face = divmod(device, 4)
    return guide // 2 % 4, guide % 2 * 2 + face // 2, guide // 8, face % 2


def device_at(x, y, z, core):
    x, y, z = x % 4, y % 4, z % 8
    return (z * 8 + x * 2 + y // 2) * 4 + y % 2 * 2 + core


def permute(block, target):
    route = [(i, device_at(*target(*coords(i)))) for i in range(256)]
    return lax.ppermute(block, AXES, route)


def to_core(x, y, z, c):
    return x, y, z, 1 - c


def to_y_mirror(x, y, z, c):
    return x, 3 - y, z, c


def to_y_pair(x, y, z, c):
    return x, y ^ 1, z, c


def to_y_far(x, y, z, c):
    return x, y + 2, z, c


def to_x_pair(x, y, z, c):
    return x ^ 1, y, z, c


def to_x_mirror(x, y, z, c):
    return 3 - x, y, z, c


def to_xy_far(x, y, z, c):
    return x ^ 1, y + 2, z, c


def to_z_next(x, y, z, c):
    return x, y, z + 1, c


def act(linear_map, vectors):
    return lax.dot_general(
        vectors, linear_map, (((1,), (1,)), ((), ())), preferred_element_type=F32
    )


def act_add(linear_map, vectors, added):
    return (act(linear_map, vectors) + added.astype(F32)).astype(BF16)


def apply_t(transposed, vectors):
    return jnp.dot(vectors, transposed, preferred_element_type=F32)


def apply_t_add(transposed, vectors, added):
    return (apply_t(transposed, vectors) + added.astype(F32)).astype(BF16)


class Place:
    def __init__(self):
        guide, self.face = lax.axis_index("guide"), lax.axis_index("face")
        self.x, self.y_hi, self.y_lo = guide // 2 % 4, guide % 2, self.face // 2
        self.core = self.face % 2
        self.x_hi, self.x_lo = self.x // 2, self.x % 2
        self.strip = (self.x_lo + self.x_hi) % 2


def span(index, size=SIDE):
    return pl.ds(pl.multiple_of(index * size, size), size)


def block_of(ref, row, col):
    return ref.at[span(row), span(col)]


def send_kernel(own, out):
    place = Place()
    line = span((place.face + 2) % 4)

    @pl.when(place.y_hi == 1)
    def _():
        for t in range(4):
            out[t] = own[line, t * SIDE : (t + 1) * SIDE]

    @pl.when(place.y_hi == 0)
    def _():
        for t in range(4):
            out[t] = own[t * SIDE : (t + 1) * SIDE, line]


def send_line(own):
    return pl.pallas_call(
        send_kernel,
        in_specs=[VMEM],
        out_specs=VMEM,
        out_shape=jax.ShapeDtypeStruct((4, SIDE, SIDE), BF16),
        compiler_params=pltpu.CompilerParams(vmem_limit_bytes=8 * 1024 * 1024),
    )(own)


def small(**sizes):
    return dict(
        compiler_params=pltpu.CompilerParams(vmem_limit_bytes=12 * 1024 * 1024),
        cost_estimate=pl.CostEstimate(
            flops=sizes.get("flops", 0), bytes_accessed=1024**2, transcendentals=0
        ),
    )


def blocks(count):
    return jax.ShapeDtypeStruct((count, SIDE, SIDE), BF16)


def source_kernel(volume, leaf, keep, send):
    place = Place()
    tile = act(leaf[...], volume[...]).astype(BF16)
    half_rows = keep.shape[0]
    for half in range(2):

        @pl.when(place.y_hi == half)
        def _():
            keep[...] = tile[half_rows * half : half_rows * (half + 1)]
            send[...] = tile[half_rows * (1 - half) : half_rows * (2 - half)]


def to_source(leaf, volume):
    rows, depth = volume.shape
    half = pl.BlockSpec((rows // 2, SIDE), lambda t: (0, t))
    return pl.pallas_call(
        source_kernel,
        grid=(leaf.shape[0] // SIDE,),
        in_specs=[
            pl.BlockSpec((rows, depth), lambda t: (0, 0)),
            pl.BlockSpec((SIDE, depth), lambda t: (t, 0)),
        ],
        out_specs=[half, half],
        out_shape=[jax.ShapeDtypeStruct((rows // 2, leaf.shape[0]), BF16)] * 2,
        compiler_params=pltpu.CompilerParams(vmem_limit_bytes=16 * 1024 * 1024),
        cost_estimate=pl.CostEstimate(
            flops=2 * rows * depth * leaf.shape[0],
            bytes_accessed=2 * depth * (rows + leaf.shape[0]),
            transcendentals=0,
        ),
    )(volume, leaf)


def line_kernel(own, got, line):
    place = Place()

    @pl.when(place.y_hi == 0)
    def _():
        row = jnp.concatenate([got[t] for t in range(4)], axis=1)
        for t in range(4):
            cols = slice(t * SIDE, (t + 1) * SIDE)
            line[t] = jnp.dot(row, own[:, cols], preferred_element_type=F32).T.astype(BF16)

    @pl.when(place.y_hi == 1)
    def _():
        col = jnp.concatenate([got[t] for t in range(4)], axis=0)
        for t in range(4):
            rows = slice(t * SIDE, (t + 1) * SIDE)
            line[t] = jnp.dot(own[rows, :], col, preferred_element_type=F32).T.astype(BF16)


def pair_line(own, got):
    return pl.pallas_call(
        line_kernel,
        in_specs=[VMEM] * 2,
        out_specs=VMEM,
        out_shape=blocks(4),
        **small(flops=2 * SIDE * 1024**2),
    )(own, got)


def multiply(left, right):
    return jnp.dot(left[...], right[...], preferred_element_type=F32).astype(BF16)


def multiply_transposed(left, right, out):
    for t in range(4):
        cols = slice(t * SIDE, (t + 1) * SIDE)
        out[cols, :] = jnp.dot(left[...], right[:, cols], preferred_element_type=F32).T.astype(BF16)


def full_kernel(own, got, got_pair, core_got, core_pair, half, theirs, *outs):
    partner, full, mine, others = outs
    place = Place()
    quarters = ((0, got), (2, got_pair), (1, core_got), (3, core_pair))

    def line_of(flip):
        return (place.y_lo + flip // 2) % 2 * 2 + (place.core + flip) % 2

    @pl.when(place.y_hi == 1)
    def _():
        for flip, ref in quarters:
            for t in range(4):
                partner[t * SIDE : (t + 1) * SIDE, span(line_of(flip))] = ref[t]
        multiply_transposed(own, partner, full)
        trace = act_add(own[...], theirs[...], half[...])
        mine[...] = trace[:64]
        others[...] = trace[64:]

    @pl.when(place.y_hi == 0)
    def _():
        for flip, ref in quarters:
            for t in range(4):
                partner[span(line_of(flip)), t * SIDE : (t + 1) * SIDE] = ref[t]
        multiply_transposed(partner, own, full)
        trace = act_add(partner[...], half[...], theirs[...])
        mine[...] = trace[:64]
        others[...] = trace[64:]

    @pl.when(place.strip == 1)
    def _():
        first, second = mine[...], others[...]
        mine[...] = second
        others[...] = first


def pair_map(*args):
    strip = jax.ShapeDtypeStruct((64, 1024), BF16)
    return pl.pallas_call(
        full_kernel,
        in_specs=[VMEM] * 7,
        out_specs=[VMEM] * 4,
        out_shape=[map_shape(), map_shape(), strip, strip],
        compiler_params=pltpu.CompilerParams(vmem_limit_bytes=16 * 1024 * 1024),
        cost_estimate=pl.CostEstimate(
            flops=2 * 1024**3, bytes_accessed=8 * 1024**2, transcendentals=0
        ),
    )(*args)


def pack_kernel(*refs):
    out, filled = refs[-1], 0
    for ref in refs[:-1]:
        size = min(ref.shape[0], 4)
        out[filled : filled + size] = ref[:size]
        filled += size


def pack(*arrays):
    return pl.pallas_call(
        pack_kernel,
        in_specs=[VMEM] * len(arrays),
        out_specs=VMEM,
        out_shape=blocks(sum(min(array.shape[0], 4) for array in arrays)),
        **small(),
    )(*arrays)


def gather_copies(place, target, lines, sems):
    copies = []
    upper = place.y_hi == 1
    for flip, line in zip((0, 2, 1, 3), lines):
        index = (place.y_lo + flip // 2) % 2 * 2 + (place.core + flip) % 2
        for t in range(4):
            row = jnp.where(upper, index, t)
            col = jnp.where(upper, t, index)
            copies.append(
                pltpu.make_async_copy(line.at[t], block_of(target, row, col), sems.at[len(copies)])
            )
    return copies


def map_shape(*lead):
    return jax.ShapeDtypeStruct((*lead, 1024, 1024), BF16)


def group_kernel(line, line_2, core, full, mine, beside, pair_full, group, trace, sems):
    place = Place()
    lines = (line, line_2, core.at[0:4], core.at[4:8])
    copies = gather_copies(place, pair_full, lines, sems)
    for copy in copies:
        copy.start()
    for copy in copies:
        copy.wait()

    @pl.when(place.x_lo == 1)
    def _():
        trace[...] = apply_t_add(full[...], beside[...], mine[...])
        group[...] = multiply(pair_full, full)

    @pl.when(place.x_lo == 0)
    def _():
        trace[...] = apply_t_add(pair_full[...], mine[...], beside[...])
        group[...] = multiply(full, pair_full)


def to_group(*args):
    return pl.pallas_call(
        group_kernel,
        in_specs=[ANY] * 3 + [VMEM] * 3,
        out_specs=[VMEM] * 3,
        out_shape=[map_shape(), map_shape(), jax.ShapeDtypeStruct((64, 1024), BF16)],
        scratch_shapes=[pltpu.SemaphoreType.DMA((16,))],
        compiler_params=pltpu.CompilerParams(vmem_limit_bytes=16 * 1024 * 1024),
        cost_estimate=pl.CostEstimate(
            flops=2 * 1024**3, bytes_accessed=8 * 1024**2, transcendentals=0
        ),
    )(*args)


def join_kernel(*refs):
    mirror, mirror_2, far, far_2, core = refs[:5]
    group, group_trace, across, from_far = refs[5:9]
    others, other_trace, plane_trace, moving, sems = refs[9:]
    place = Place()
    mirror_slot = place.x_lo
    mirror_lines = (mirror, mirror_2, core.at[0:4], core.at[4:8])
    far_lines = (far, far_2, core.at[8:12], core.at[12:16])
    copies = gather_copies(place, others.at[mirror_slot], mirror_lines, sems.at[0])
    copies += gather_copies(place, others.at[1 - mirror_slot], far_lines, sems.at[1])
    for copy in copies:
        copy.start()
    for copy in copies:
        copy.wait()
    mirror_low = place.x_lo == 1
    low = jnp.where(mirror_low, across[...], from_far[...])
    high = jnp.where(mirror_low, from_far[...], across[...])
    other_trace[...] = apply_t_add(others[0], low, high)

    @pl.when(place.x_hi == 1)
    def _():
        plane_trace[...] = apply_t_add(group[...], other_trace[...], group_trace[...])
        moving[...] = group_trace[...]

    @pl.when(place.x_hi == 0)
    def _():
        inner = apply_t(others[1], group_trace[...]).astype(BF16)
        total = apply_t_add(others[0], inner, other_trace[...])
        plane_trace[...] = total
        moving[...] = total


def join(*args):
    strip = jax.ShapeDtypeStruct((64, 1024), BF16)
    return pl.pallas_call(
        join_kernel,
        in_specs=[ANY] * 5 + [VMEM] * 4,
        out_specs=[VMEM] * 4,
        out_shape=[map_shape(2), strip, strip, strip],
        scratch_shapes=[pltpu.SemaphoreType.DMA((2, 16))],
        compiler_params=pltpu.CompilerParams(vmem_limit_bytes=16 * 1024 * 1024),
        cost_estimate=pl.CostEstimate(
            flops=6 * 64 * 1024**2, bytes_accessed=10 * 1024**2, transcendentals=0
        ),
    )(*args)


def plane_kernel(group, others, other, plane):
    place = Place()
    other[...] = multiply(others.at[1], others.at[0])

    @pl.when(place.x_hi == 1)
    def _():
        plane[...] = multiply(other, group)

    @pl.when(place.x_hi == 0)
    def _():
        plane[...] = multiply(group, other)


def to_plane(*args):
    return pl.pallas_call(
        plane_kernel,
        in_specs=[VMEM] * 2,
        out_specs=[VMEM] * 2,
        out_shape=[map_shape()] * 2,
        compiler_params=pltpu.CompilerParams(vmem_limit_bytes=16 * 1024 * 1024),
        cost_estimate=pl.CostEstimate(
            flops=4 * 1024**3, bytes_accessed=10 * 1024**2, transcendentals=0
        ),
    )(*args)


def lift_kernel(part_a, part_b, other_map, other_trace, full, pair_full, mine, beside, own, across):
    place = Place()
    own[0:32, :] = part_a[...]
    own[32:64, :] = part_b[...]

    @pl.when(place.x_hi == 1)
    def _():
        own[...] = apply_t_add(other_map[...], own[...], other_trace[...])

    @pl.when(place.x_lo == 1)
    def _():
        across[...] = own[...]
        own[...] = apply_t_add(pair_full[...], own[...], beside[...])

    @pl.when(place.x_lo == 0)
    def _():
        across[...] = apply_t_add(full[...], own[...], mine[...])


def lift(*args):
    strip = jax.ShapeDtypeStruct((64, 1024), BF16)
    return pl.pallas_call(
        lift_kernel,
        in_specs=[VMEM] * 8,
        out_specs=[VMEM] * 2,
        out_shape=[strip, strip],
        **small(flops=4 * 64 * 1024**2),
    )(*args)


def last_kernel(e00, e01, e10, e11, partner, late, theirs, out, held):
    place = Place()
    for part, (flip_y, flip_x) in ((e00, (0, 0)), (e01, (0, 1)), (e10, (1, 0)), (e11, (1, 1))):
        index = 2 * ((place.y_hi + flip_y) % 2) + (place.strip + flip_x) % 2
        held[span(index, 64), :] = part[...]

    @pl.when(place.y_hi == 0)
    def _():
        out[...] = held[...]

    @pl.when(place.y_hi == 1)
    def _():
        added = jnp.concatenate([late[...], theirs[...]], axis=0)
        out[...] = act_add(partner[...], held[...], added)


def last(*args):
    return pl.pallas_call(
        last_kernel,
        in_specs=[VMEM] * 7,
        out_specs=VMEM,
        out_shape=jax.ShapeDtypeStruct((256, 1024), BF16),
        scratch_shapes=[pltpu.VMEM((256, 1024), BF16)],
        **small(flops=2 * 256 * 1024**2),
    )(*args)


def together(*values):
    return lax.optimization_barrier(values)


def local(transfer, leaf_map, volume_source):
    place = Place()
    own_map = transfer[0]

    got = permute(send_line(own_map), to_y_mirror)
    source, source_out = to_source(leaf_map[0], volume_source[0])
    relay = permute(source_out, to_y_pair)
    got, relay = together(got, relay)
    line = pair_line(own_map, got)

    got_pair = permute(got, to_y_pair)
    pair = permute(line, to_x_pair)
    mirror = permute(line, to_x_mirror)
    theirs = permute(relay, to_y_mirror)
    core_got = permute(got, to_core)
    got_pair, theirs = together(got_pair, theirs)
    core_pair = permute(got_pair, to_core)
    line_2 = pair_line(own_map, got_pair)
    pair, mirror, theirs, core_got, core_pair, line_2 = together(
        pair, mirror, theirs, core_got, core_pair, line_2
    )

    pair_2 = permute(line_2, to_x_pair)
    mirror_2 = permute(line_2, to_x_mirror)
    far_a, far_b = permute(pair[:2], to_x_mirror), permute(mirror[2:], to_x_pair)
    partner, full, mine, others = pair_map(
        own_map, got, got_pair, core_got, core_pair, source, theirs
    )
    late = permute(source, to_y_far)
    far_a, far_b, mine, others, late = together(far_a, far_b, mine, others, late)
    far = pack(far_a, far_b)
    far_2 = permute(far, to_y_pair)
    beside = permute(others, to_x_pair)
    pair_2, mirror_2, far_2, beside, strip_out = together(pair_2, mirror_2, far_2, beside, mine)
    across = permute(strip_out, to_x_mirror)
    from_far = permute(beside, to_x_mirror)

    core_pairs = permute(pack(pair, pair_2), to_core)
    core_pairs, packed = together(core_pairs, pack(mirror, mirror_2, far, far_2))
    core_others = permute(packed, to_core)
    from_far = permute(beside, to_x_mirror)
    pair_full, group_map, group_trace = to_group(
        pair, pair_2, core_pairs, full, mine, beside
    )
    core_others, group_trace = together(core_others, group_trace)
    other_maps, other_trace, plane_trace, moving = join(
        mirror, mirror_2, far, far_2, core_others, group_map, group_trace, across, from_far
    )

    added = [plane_trace[:32], plane_trace[32:]]
    parts = [permute(part, to_z_next) for part in (moving[:32], moving[32:])]
    other_map, plane_map = to_plane(group_map, other_maps)
    for _ in range(7):
        parts = [apply_t_add(plane_map, part, extra) for part, extra in zip(parts, added)]
        parts = [permute(part, to_z_next) for part in parts]

    own, other = lift(*parts, other_map, other_trace, full, pair_full, mine, beside)
    pieces = (
        own,
        permute(other, to_x_pair),
        permute(own, to_y_far),
        permute(other, to_xy_far),
    )
    traces = last(*pieces, partner, late, theirs)
    return traces[None]


def solution(mesh):
    in_specs = (P("guide", None, None), P("guide", None, None), P("guide", "face", None))
    out_specs = P("guide", "face", None)
    return jax.shard_map(local, mesh=mesh, in_specs=in_specs, out_specs=out_specs, check_vma=False)
```
